512 devices in a mesh: nodes: 64 (over z, x, y_lo), feat: 8 (over y_hi, core).
Axes of the slice: x: 4, y: 8 (y_hi: 4, y_lo: 2; y = y_hi * 2 + y_lo), z: 8, core: 2. Of those that a mesh axis runs over, the one named last changes fastest.
Arguments:
- features: bfloat16 [65536, 768], P('nodes', 'feat'), may hold values from -6 to 6
- target_ids: int32 [16384], P('nodes'), may hold values from 0 to 1023
- near_ids: int32 [16384, 25], P('nodes'), may hold values from 0 to 1023
- seed_ids: int32 [16384], P('nodes'), may hold values from 0 to 255
- seed_near: int32 [16384, 15], P('nodes'), may hold values from 0 to 255
- w1_self: bfloat16 [768, 1024], P('feat'), may hold values from -0.21875 to 0.21875
- w1_neigh: bfloat16 [768, 1024], P('feat'), may hold values from -0.21875 to 0.21875
- w2_self: bfloat16 [1024, 153], P('feat'), may hold values from -0.1875 to 0.1875
- w2_neigh: bfloat16 [1024, 153], P('feat'), may hold values from -0.1875 to 0.1875
- logit_grad: bfloat16 [16384, 153], P('nodes'), may hold values from -6 to 6
Outputs:
- logits: float32 [16384, 153], P('nodes')
- grad_w1_self: float32 [768, 1024], P('feat')
- grad_w1_neigh: float32 [768, 1024], P('feat')
- grad_w2_self: float32 [1024, 153], P('feat')
- grad_w2_neigh: float32 [1024, 153], P('feat')
The draws below stay inside these ranges and needn't reach their ends.
All inputs are finite; a program needn't handle non-finite values.
Results may differ from the reference program's by a relative error of at most 0.025.
Values may be sent and summed in bfloat16 or wider, within the bound.
A program may use at most 64 MiB of HBM per device.

```python
import jax
import jax.numpy as jnp
from jax import lax

F = 768
HID = 1024
C = 153
K1 = 25
K2 = 15
ND = 1024
TGT_DEV = 256
SEED_DEV = 256
FSL = 96
SLOT = 4
NODES = 65536
TARGETS = 16384
SEEDS = 16384
N_NODES = 64
N_FEAT = 8


def plant(values, stream_key, low, high):
    longest = values.shape.index(max(values.shape))
    spots = []
    for shift in (0, 1):
        where = [jax.random.randint(jax.random.fold_in(stream_key, axis), (), 0, length) for axis, length in enumerate(values.shape)]
        where[longest] = (where[longest] + shift) % values.shape[longest]
        spots.append(tuple(where))
    return values.at[spots[0]].set(low).at[spots[1]].set(high)


def level_of(key, extent, shards, smallest, top_value):
    level = 1.0
    for position, shards_of in shards:
        steps = jax.random.uniform(jax.random.fold_in(jax.random.fold_in(key, 6), position), (shards_of,), jnp.float32, smallest / len(shards), top_value / len(shards))
        level = level * jnp.repeat(jnp.exp(steps), extent[position] // shards_of).reshape((-1,) + (1,) * (len(extent) - 1 - position))
    return level


def scatter_about(stream_key, shape, spread, most, cuts=(), kind=jnp.bfloat16):
    array = jax.random.normal(stream_key, shape, jnp.float32) * spread
    if len(cuts) > 0:
        array = level_of(stream_key, shape, cuts, -0.22, 0.18) * array
    return jnp.clip(array, min=-most, max=most).astype(kind)


def setup_inputs(seed: int = 0) -> dict:
    streams_of = jax.random.split(jax.random.key(seed), 11)
    features = scatter_about(streams_of[0], (NODES, F), 1.0, 6.0, ((0, 64), (1, 8)))
    target_ids = plant(jax.random.randint(streams_of[1], (TARGETS,), 0, ND), jax.random.fold_in(streams_of[1], 1), 0, ND - 1).astype(jnp.int32)
    near_ids = plant(jax.random.randint(streams_of[2], (TARGETS, K1), 0, ND), jax.random.fold_in(streams_of[2], 1), 0, ND - 1).astype(jnp.int32)
    seed_ids = plant(jax.random.randint(streams_of[3], (SEEDS,), 0, TGT_DEV), jax.random.fold_in(streams_of[3], 1), 0, TGT_DEV - 1).astype(jnp.int32)
    seed_near = plant(jax.random.randint(streams_of[4], (SEEDS, K2), 0, TGT_DEV), jax.random.fold_in(streams_of[4], 1), 0, TGT_DEV - 1).astype(jnp.int32)
    w1_self = scatter_about(streams_of[5], (F, HID), F ** -0.5, 0.21875, ((0, 8),))
    w1_neigh = scatter_about(streams_of[6], (F, HID), F ** -0.5, 0.21875, ((0, 8),))
    w2_self = scatter_about(streams_of[7], (HID, C), HID ** -0.5, 0.1875, ((0, 8),))
    w2_neigh = scatter_about(streams_of[8], (HID, C), HID ** -0.5, 0.1875, ((0, 8),))
    logit_grad = scatter_about(streams_of[9], (SEEDS, C), 1.0, 6.0, ((0, 64),))
    return dict(features=features, target_ids=target_ids, near_ids=near_ids, seed_ids=seed_ids, seed_near=seed_near, w1_self=w1_self, w1_neigh=w1_neigh, w2_self=w2_self, w2_neigh=w2_neigh, logit_grad=logit_grad)


def reference(features, target_ids, near_ids, seed_ids, seed_near, w1_self, w1_neigh, w2_self, w2_neigh, logit_grad):
    total_rows = N_NODES * TGT_DEV
    offsets = (jnp.arange(total_rows, dtype=jnp.int32) // TGT_DEV) * ND
    x_self = features[target_ids + offsets]
    running = jnp.zeros((total_rows, F), jnp.float32)
    for column in range(K1):
        running = running + features[near_ids[:, column] + offsets].astype(jnp.float32)
    agg_one = (running / K1).astype(jnp.bfloat16)
    pre_act = jnp.zeros((total_rows, HID), jnp.float32)
    for slice_index in range(N_FEAT):
        first_col = slice_index * FSL
        last_col = first_col + FSL
        partial_sum = jnp.dot(x_self[:, first_col:last_col], w1_self[first_col:last_col], preferred_element_type=jnp.float32)
        partial_sum = partial_sum + jnp.dot(agg_one[:, first_col:last_col], w1_neigh[first_col:last_col], preferred_element_type=jnp.float32)
        rounded = lax.optimization_barrier(partial_sum.astype(jnp.bfloat16))
        pre_act = pre_act + rounded.astype(jnp.float32)
    sigma = 1.0 / (1.0 + jnp.exp(-pre_act))
    hidden = (pre_act * sigma).astype(jnp.bfloat16)
    received = hidden.reshape(N_NODES, N_NODES, SLOT, HID).transpose(1, 0, 2, 3).reshape(N_NODES, TGT_DEV, HID)
    owner_ids = jnp.arange(SEED_DEV * N_NODES, dtype=jnp.int32) // SEED_DEV
    h_self = received[owner_ids, seed_ids]
    running_two = jnp.zeros((SEED_DEV * N_NODES, HID), jnp.float32)
    for column in range(K2):
        running_two = running_two + received[owner_ids, seed_near[:, column]].astype(jnp.float32)
    agg_two = (running_two / K2).astype(jnp.bfloat16)
    logits = jnp.dot(h_self, w2_self, preferred_element_type=jnp.float32) + jnp.dot(agg_two, w2_neigh, preferred_element_type=jnp.float32)
    grad_w2_self = jnp.dot(h_self.T, logit_grad, preferred_element_type=jnp.float32)
    grad_w2_neigh = jnp.dot(agg_two.T, logit_grad, preferred_element_type=jnp.float32)
    g_self = jnp.dot(logit_grad, w2_self.T, preferred_element_type=jnp.float32).astype(jnp.bfloat16)
    g_neigh = jnp.dot(logit_grad, w2_neigh.T, preferred_element_type=jnp.float32).astype(jnp.bfloat16)
    own_part = jnp.zeros((N_NODES, TGT_DEV, HID), jnp.float32).at[owner_ids, seed_ids].add(g_self.astype(jnp.float32))
    near_part = jnp.zeros((N_NODES, TGT_DEV, HID), jnp.float32)
    for column in range(K2):
        near_part = near_part.at[owner_ids, seed_near[:, column]].add(g_neigh.astype(jnp.float32))
    d_received = (own_part + near_part / K2).astype(jnp.bfloat16)
    d_hidden = d_received.reshape(N_NODES, N_NODES, SLOT, HID).transpose(1, 0, 2, 3).reshape(total_rows, HID)
    slope = sigma * (1.0 + pre_act * (1.0 - sigma))
    d_pre = (d_hidden.astype(jnp.float32) * slope).astype(jnp.bfloat16)
    grad_w1_self = jnp.dot(x_self.T, d_pre, preferred_element_type=jnp.float32)
    grad_w1_neigh = jnp.dot(agg_one.T, d_pre, preferred_element_type=jnp.float32)
    return (logits, grad_w1_self, grad_w1_neigh, grad_w2_self, grad_w2_neigh)
```

```python
import jax
import jax.numpy as jnp
from jax import lax
from jax.experimental import pallas as pl
from jax.experimental.pallas import tpu as pltpu
from jax.sharding import PartitionSpec as P

BF = jnp.bfloat16
F32 = jnp.float32
MESH = pl.DeviceIdType.MESH

TGT = 256
ND = 1024
FSL = 96
HID = 1024
HS = 128
C = 153
K1 = 25
K2 = 15
CP = 192
LP = 5
Q = 8
PIECE = 48
SETS = ((0, 2), (2, 2), (4, 1))


def dot(a, b):
    return jnp.dot(a, b, preferred_element_type=F32)


def dot_dims(a, b, ca, cb):
    return lax.dot_general(a, b, (((ca,), (cb,)), ((), ())), preferred_element_type=F32)


def main_kernel(
    features_hbm, near_hbm, tid_hbm, sid_hbm, snear_hbm,
    w1s_hbm, w1n_hbm, w2s_hbm, w2n_hbm, lg_hbm,
    gath, lout,
    feat_v, near_v, tid_v, sid_v, snear_v, w1_v, w2s_v, w2n_v, lg_v,
    keys, tally, sel, x_v, xt, seedtally, lgp, w2c, perm,
    pair_src, pair_rcv, p_own, rs_src, relay_rcv, rs_rcv,
    bz_src, bz_rcv, bw_src, bw_rcv, dt, d_hid,
    fw_src, fw_rcv, fz_src, fz_rcv,
    ag, gst, rw_rcv, zsrc, z_rcv, zc_rcv, zfull, lst, l_rcv, ltot,
    in_sem, out_sem, pair_s, pair_r, rs_s, rs_r, bz_s, bz_r, bw_s, bw_r,
    fw_s, fw_r, fz_s, fz_r, ag_s, ag_r, agf_s, agf_r,
    rw_s, rw_r, z_s, z_r, az_s, az_r, aw_s, aw_r, l_s, l_r, la_s, la_r,
):
    node = lax.axis_index("nodes")
    f = lax.axis_index("feat")
    z = node // Q
    w = node % Q
    h = f // 2
    c = f % 2

    def z_peer(d):
        zz = lax.rem(z + d, Q)
        return zz, (zz * Q + w, f)

    def w_peer(d):
        ww = lax.rem(w + d, Q)
        return ww, (z * Q + ww, f)

    def f_peer(d):
        ff = lax.rem(f + d, Q)
        return ff, (node, ff)

    partner = (node, h * 2 + (1 - c))

    up = (node, lax.rem(h + 1, 4) * 2 + c)
    down = (node, lax.rem(h + 3, 4) * 2 + c)

    def each(body):
        def step(d, carry):
            body(d)
            return carry

        lax.fori_loop(1, Q, step, 0)

    barrier = pltpu.get_barrier_semaphore()

    def greet(d):
        for where in (z_peer(d)[1], w_peer(d)[1], f_peer(d)[1]):
            pl.semaphore_signal(barrier, inc=1, device_id=where, device_id_type=MESH)

    each(greet)

    loads = [
        pltpu.make_async_copy(src, dst, in_sem.at[n])
        for n, (src, dst) in enumerate(
            (
                (snear_hbm, snear_v),
                (sid_hbm, sid_v),
                (lg_hbm, lg_v),
                (w2s_hbm, w2s_v),
                (w2n_hbm, w2n_v),
                (near_hbm, near_v),
                (tid_hbm, tid_v),
                (features_hbm, feat_v),
                (w1s_hbm, w1_v.at[pl.ds(0, FSL)]),
                (w1n_hbm, w1_v.at[pl.ds(FSL, FSL)]),
            )
        )
    ]
    for load in loads:
        load.start()

    pending = []

    def remote(src, dst, s_sem, r_sem, where):
        return pltpu.make_async_remote_copy(
            src_ref=src, dst_ref=dst, send_sem=s_sem, recv_sem=r_sem,
            device_id=where, device_id_type=MESH,
        )

    def send(*args):
        copy = remote(*args)
        copy.start()
        pending.append(copy.wait_send)

    def send_each(copy_of, test_of=None):
        def start(d):
            if test_of is None:
                copy_of(d).start()
            else:
                pl.when(test_of(d))(lambda: copy_of(d).start())

        def finish(d):
            if test_of is None:
                copy_of(d).wait_send()
            else:
                pl.when(test_of(d))(lambda: copy_of(d).wait_send())

        each(start)
        pending.append(lambda: each(finish))

    def sent():
        for finish in pending:
            finish()
        pending.clear()

    def landed(ref, r_sem):
        pltpu.make_async_copy(ref, ref, r_sem).wait()

    one = jnp.ones((16, 128), BF)
    zero = jnp.zeros((16, 128), BF)
    row = lax.broadcasted_iota(jnp.int32, (16, 128), 0)

    def key_of(ids):
        return lax.shift_left(128 + (ids & 127), lax.shift_right_logical(ids, 7)).astype(F32)

    def spread(first, ids):
        for k in range(ids.shape[0]):
            keys[first + k] = jnp.broadcast_to(ids[k:k + 1], (16, TGT)).astype(BF)

    def count(fan, row_key, totals_of, ones_of):
        def body(step, carry):
            mine = [row_key(step * 64 + j * 16 + row).astype(BF) for j in range(4)]
            for half in range(2):
                cols = slice(half * 128, half * 128 + 128)
                totals = [zero] * 4
                for k in range(fan):
                    theirs = keys[k, :, cols]
                    totals = [t + jnp.where(theirs == m, one, zero) for t, m in zip(totals, mine)]
                theirs = keys[fan, :, cols]
                for j in range(4):
                    rows = pl.ds(pl.multiple_of(step * 64 + j * 16, 16), 16)
                    totals_of[rows, cols] = totals[j]
                    ones_of[rows, cols] = jnp.where(theirs == mine[j], one, zero)
            return carry

        return body

    def swap(n):
        return ((n >> 2) & 7) * 32 + (n >> 5) * 4 + (n & 3)

    a = lax.broadcasted_iota(jnp.int32, (TGT, TGT), 0)
    b = lax.broadcasted_iota(jnp.int32, (TGT, TGT), 1)
    perm[...] = jnp.where(swap(a) == b, 1.0, 0.0).astype(BF)

    for n in range(5):
        loads[n].wait()
    for padded, first, given in ((lgp, 0, lg_v), (w2c, 0, w2s_v), (w2c, CP, w2n_v)):
        padded[first:first + CP] = jnp.zeros((CP, padded.shape[1]), BF)
        padded[first:first + C] = given[...]
    spread(0, snear_v[...].astype(F32))
    spread(K2, sid_v[...].astype(F32))
    lax.fori_loop(
        0, TGT // 64, count(K2, lambda n: swap(n).astype(F32), seedtally.at[1], seedtally.at[0]), 0
    )
    lg = lgp[...].astype(F32).T.astype(BF)
    back = jnp.concatenate([dot(seedtally[0], lg), dot(seedtally[1], lg) / K2], axis=1)
    bw_src[...] = back.astype(BF).reshape(Q, 32, 2 * CP)

    def to_w(src, dst, s_sem, r_sem):
        def copy_of(d):
            ww, where = w_peer(d)
            return remote(src.at[ww], dst.at[w], s_sem.at[d - 1], r_sem.at[d - 1], where)

        send_each(copy_of)
        dst[w] = src[w]

    def to_z(src, dst, s_sem, r_sem):
        def copy_of(d):
            zz, where = z_peer(d)
            return remote(src.at[zz], dst.at[z], s_sem.at[d - 1], r_sem.at[d - 1], where)

        send_each(copy_of)
        dst[z] = src[z]

    def from_w(dst, r_sem):
        each(lambda d: landed(dst.at[lax.rem(w + Q - d, Q)], r_sem.at[d - 1]))

    def from_z(dst, r_sem):
        each(lambda d: landed(dst.at[lax.rem(z + Q - d, Q)], r_sem.at[d - 1]))

    pl.semaphore_wait(barrier, 3 * (Q - 1))
    to_w(bw_src, bw_rcv, bw_s, bw_r)

    loads[5].wait()
    loads[6].wait()
    spread(0, key_of(near_v[...]))
    spread(K1, key_of(tid_v[...]))
    lax.fori_loop(0, ND // 64, count(K1, key_of, tally, sel), 0)

    loads[7].wait()
    x_self = (dot(feat_v[...], sel[...])).astype(BF)
    agg = (dot(feat_v[...], tally[...]) / K1).astype(BF)
    xt[0:FSL] = x_self
    xt[FSL:2 * FSL] = agg
    x_v[...] = jnp.concatenate([x_self.astype(F32), agg.astype(F32)], axis=0).T.astype(BF)

    loads[8].wait()
    loads[9].wait()

    def partial(dh, cc):
        col = pl.ds(pl.multiple_of((lax.rem(h + dh, 4) * 2 + cc) * HS, HS), HS)
        return dot(x_v[...], w1_v[:, col])

    for dh in (2, 1, 3, 0):
        pair_src[dh] = partial(dh, 1 - c).astype(BF)
        send(pair_src.at[dh], pair_rcv.at[dh], pair_s.at[dh], pair_r.at[dh], partner)
    for dh in (2, 1, 3, 0):
        p_own[dh] = partial(dh, c)
    from_w(bw_rcv, bw_r)
    turned = dot(perm[...], bw_rcv[...].reshape(TGT, 2 * CP)).astype(BF)
    bz_src[...] = turned.reshape(Q, 32, 2 * CP)
    to_z(bz_src, bz_rcv, bz_s, bz_r)

    lo, hi = pl.ds(0, 128), pl.ds(128, 128)
    landed(pair_rcv.at[2], pair_r.at[2])
    rs_src[0] = (p_own[2] + pair_rcv[2].astype(F32)).astype(BF)
    send(rs_src.at[0, lo], relay_rcv.at[0], rs_s.at[0], rs_r.at[0], up)
    send(rs_src.at[0, hi], relay_rcv.at[1], rs_s.at[1], rs_r.at[1], down)
    landed(pair_rcv.at[1], pair_r.at[1])
    rs_src[1, 128:256] = (p_own[1, 128:256] + pair_rcv[1, 128:256].astype(F32)).astype(BF)
    send(rs_src.at[1, hi], rs_rcv.at[0, hi], rs_s.at[2], rs_r.at[2], up)
    landed(pair_rcv.at[3], pair_r.at[3])
    rs_src[2, 0:128] = (p_own[3, 0:128] + pair_rcv[3, 0:128].astype(F32)).astype(BF)
    send(rs_src.at[2, lo], rs_rcv.at[1, lo], rs_s.at[3], rs_r.at[3], down)
    landed(relay_rcv.at[0], rs_r.at[0])
    rs_src[1, 0:128] = (
        p_own[1, 0:128] + pair_rcv[1, 0:128].astype(F32) + relay_rcv[0].astype(F32)
    ).astype(BF)
    send(rs_src.at[1, lo], rs_rcv.at[0, lo], rs_s.at[4], rs_r.at[4], up)
    landed(relay_rcv.at[1], rs_r.at[1])
    rs_src[2, 128:256] = (
        p_own[3, 128:256] + pair_rcv[3, 128:256].astype(F32) + relay_rcv[1].astype(F32)
    ).astype(BF)
    send(rs_src.at[2, hi], rs_rcv.at[1, hi], rs_s.at[5], rs_r.at[5], down)

    from_z(bz_rcv, bz_r)
    back = bz_rcv[...].reshape(TGT, 2 * CP)
    d_hid[...] = dot(back, w2c[...])
    dt[...] = back.astype(F32).T.astype(BF)

    landed(pair_rcv.at[0], pair_r.at[0])
    pre = p_own[0] + pair_rcv[0].astype(F32)
    landed(rs_rcv.at[0, hi], rs_r.at[2])
    landed(rs_rcv.at[1, lo], rs_r.at[3])
    landed(rs_rcv.at[0, lo], rs_r.at[4])
    landed(rs_rcv.at[1, hi], rs_r.at[5])
    pre = pre + rs_rcv[0].astype(F32) + rs_rcv[1].astype(F32)
    sigma = 1.0 / (1.0 + jnp.exp(-pre))
    ag[0, 0] = (d_hid[...] * (sigma * (1.0 + pre * (1.0 - sigma)))).astype(BF)
    send(ag.at[0, 0, lo], ag.at[3, 0, lo], ag_s.at[0], ag_r.at[0], up)
    send(ag.at[0, 0, hi], ag.at[1, 0, hi], ag_s.at[1], ag_r.at[1], down)
    send(ag.at[0, 0], ag.at[0, 1], agf_s.at[0], agf_r.at[0], partner)
    send(ag.at[0, 0, hi], ag.at[3, 0, hi], ag_s.at[2], ag_r.at[2], up)
    send(ag.at[0, 0, lo], ag.at[1, 0, lo], ag_s.at[3], ag_r.at[3], down)
    hidden = (pre * sigma).astype(BF)
    fz_src[...] = hidden.reshape(Q, 32, HS)
    to_z(fz_src, fz_rcv, fz_s, fz_r)
    gst[:, 0] = dot(dt[...], hidden).astype(BF).reshape(Q, PIECE, HS)

    slots = {0: 1, 1: 2, 3: 3, 2: 4}

    def lower(dh, dc):
        grad = dot(xt[...], ag[dh, dc]).astype(BF).reshape(4, PIECE, HS)
        cc = c if dc == 0 else 1 - c
        gst[pl.ds(cc * 4, 4), slots[dh]] = grad

    def scatter(n):
        span = pl.ds(*SETS[n])

        def copy_of(d):
            ww, where = w_peer(d)
            return remote(
                gst.at[ww, span], rw_rcv.at[d - 1, span], rw_s.at[n, d - 1], rw_r.at[n, d - 1], where
            )

        send_each(copy_of)

    def reduce_w(n):
        first, many = SETS[n]
        each(lambda d: landed(rw_rcv.at[d - 1, pl.ds(first, many)], rw_r.at[n, d - 1]))
        for slot in range(first, first + many):
            total = gst[w, slot].astype(F32)
            for d in range(1, Q):
                total = total + rw_rcv[d - 1, slot].astype(F32)
            zsrc[slot * 3:slot * 3 + 3] = total.astype(BF).reshape(3, 16, HS)

    def owned(n, zz):
        lo, hi = SETS[n][0] * 3, (SETS[n][0] + SETS[n][1]) * 3
        k = lo + lax.rem(zz + 16 - lo % Q, Q)
        return k < hi, jnp.minimum(k, hi - 1)

    def scatter_z(n):
        reduce_w(n)

        def copy_of(d):
            zz, where = z_peer(d)
            k = owned(n, zz)[1]
            return remote(zsrc.at[k], z_rcv.at[n, d - 1], z_s.at[n, d - 1], z_r.at[n, d - 1], where)

        send_each(copy_of, lambda d: owned(n, z_peer(d)[0])[0])

    def gather_z(n):
        test, k = owned(n, z)

        @pl.when(test)
        def _():
            each(lambda d: landed(z_rcv.at[n, d - 1], z_r.at[n, d - 1]))
            total = zsrc[k].astype(F32)
            for d in range(1, Q):
                total = total + z_rcv[n, d - 1].astype(F32)
            zfull[k] = total.astype(BF)

        def copy_of(d):
            return remote(zfull.at[k], zfull.at[k], az_s.at[n, d - 1], az_r.at[n, d - 1], z_peer(d)[1])

        send_each(copy_of, lambda d: test)

    def gather_w(n):
        pieces = pl.ds(SETS[n][0] * 3, SETS[n][1] * 3)

        def wait(d):
            test, k = owned(n, lax.rem(z + Q - d, Q))
            pl.when(test)(lambda: landed(zfull.at[k], az_r.at[n, d - 1]))

        if n < 2:
            each(wait)

        def copy_of(d):
            return remote(
                zfull.at[pieces], gath.at[w, pieces], aw_s.at[n, d - 1], aw_r.at[n, d - 1], w_peer(d)[1]
            )

        send_each(copy_of)
        pltpu.make_async_copy(zfull.at[pieces], gath.at[w, pieces], out_sem.at[n]).start()

    last = pl.ds(12, 3)

    def exchange_z():
        reduce_w(2)

        def copy_of(d):
            return remote(zsrc.at[last], zc_rcv.at[z], z_s.at[2, d - 1], z_r.at[2, d - 1], z_peer(d)[1])

        send_each(copy_of)
        zc_rcv[z] = zsrc[12:15]

    def sum_z():
        from_z(zc_rcv, z_r.at[2])
        total = zc_rcv[0].astype(F32)
        for zz in range(1, Q):
            total = total + zc_rcv[zz].astype(F32)
        zfull[12:15] = total.astype(BF)

    lower(0, 0)
    landed(ag.at[0, 1], agf_r.at[0])
    lower(0, 1)
    scatter(0)

    landed(ag.at[3, 0, lo], ag_r.at[0])
    send(ag.at[3, 0, lo], ag.at[2, 0, lo], ag_s.at[4], ag_r.at[4], up)
    landed(ag.at[1, 0, hi], ag_r.at[1])
    send(ag.at[1, 0, hi], ag.at[2, 0, hi], ag_s.at[5], ag_r.at[5], down)
    landed(ag.at[3, 0, hi], ag_r.at[2])
    send(ag.at[3, 0], ag.at[3, 1], agf_s.at[3], agf_r.at[3], partner)
    landed(ag.at[1, 0, lo], ag_r.at[3])
    send(ag.at[1, 0], ag.at[1, 1], agf_s.at[1], agf_r.at[1], partner)
    lower(3, 0)
    lower(1, 0)

    from_z(fz_rcv, fz_r)
    fw_src[...] = dot(perm[...], fz_rcv[...].reshape(TGT, HS)).astype(BF).reshape(Q, 32, HS)
    to_w(fw_src, fw_rcv, fw_s, fw_r)

    scatter_z(0)
    landed(ag.at[3, 1], agf_r.at[3])
    lower(3, 1)
    landed(ag.at[1, 1], agf_r.at[1])
    lower(1, 1)
    scatter(1)
    landed(ag.at[2, 0, lo], ag_r.at[4])
    landed(ag.at[2, 0, hi], ag_r.at[5])
    send(ag.at[2, 0], ag.at[2, 1], agf_s.at[2], agf_r.at[2], partner)
    lower(2, 0)
    gather_z(0)
    landed(ag.at[2, 1], agf_r.at[2])
    lower(2, 1)
    scatter(2)
    scatter_z(1)

    from_w(fw_rcv, fw_r)
    received = fw_rcv[...].reshape(TGT, HS).astype(F32).T.astype(BF)
    h_self = dot(received, seedtally[0]).astype(BF)
    agg_two = (dot(received, seedtally[1]) / K2).astype(BF)
    part = dot(w2c[0:CP], h_self) + dot(w2c[CP:2 * CP], agg_two)
    lst[...] = part[0:LP * 32].astype(BF).reshape(LP, 32, TGT)

    def logit_part(d):
        ff, where = f_peer(d)
        return remote(lst.at[lax.rem(ff, LP)], l_rcv.at[d - 1], l_s.at[d - 1], l_r.at[d - 1], where)

    send_each(logit_part, lambda d: f_peer(d)[0] < LP)

    gather_w(0)
    exchange_z()
    gather_z(1)

    fl = lax.rem(f, LP)

    @pl.when(f < LP)
    def _():
        each(lambda d: landed(l_rcv.at[d - 1], l_r.at[d - 1]))
        total = lst[fl].astype(F32)
        for d in range(1, Q):
            total = total + l_rcv[d - 1].astype(F32)
        ltot[...] = total.astype(BF)
        pltpu.make_async_copy(ltot, lout.at[fl], out_sem.at[3]).start()

    def logit_sum(d):
        return remote(ltot, lout.at[fl], la_s.at[d - 1], la_r.at[d - 1], f_peer(d)[1])

    send_each(logit_sum, lambda d: f < LP)

    gather_w(1)
    sum_z()
    gather_w(2)
    sent()

    def logits_in(d):
        ff = lax.rem(f + Q - d, Q)
        pl.when(ff < LP)(lambda: landed(lout.at[lax.rem(ff, LP)], la_r.at[d - 1]))

    each(logits_in)

    @pl.when(f < LP)
    def _():
        landed(lout.at[fl], out_sem.at[3])

    for n, (first, many) in enumerate(SETS):
        pieces = pl.ds(first * 3, many * 3)
        each(lambda d: landed(gath.at[lax.rem(w + Q - d, Q), pieces], aw_r.at[n, d - 1]))
        landed(gath.at[w, pieces], out_sem.at[n])


def finish_kernel(gath, lout, logits, g1s, g1n, g2s, g2n):
    h = lax.axis_index("feat") // 2
    logits[...] = lout[...].reshape(LP * 32, TGT)[0:C].astype(F32)
    for ww in range(Q):
        cc, k = ww // 4, ww % 4
        mine = gath[ww].reshape(5 * PIECE, HS).astype(F32)
        out = g2s if ww < 4 else g2n
        count = min(PIECE, C - k * PIECE)
        out[k * PIECE:k * PIECE + count] = mine[0:count]
        out = g1s if k < 2 else g1n
        for slot, dh in ((1, 0), (2, 1), (3, 3), (4, 2)):
            col = pl.ds(pl.multiple_of((2 * lax.rem(h + dh, 4) + cc) * HS, HS), HS)
            out[(k % 2) * PIECE:(k % 2 + 1) * PIECE, col] = mine[slot * PIECE:(slot + 1) * PIECE]


def local(
    features, target_ids, near_ids, seed_ids, seed_near, w1_self, w1_neigh, w2_self, w2_neigh, logit_grad
):
    vm = pltpu.VMEM
    dma = pltpu.SemaphoreType.DMA
    vspec = pl.BlockSpec(memory_space=pltpu.VMEM)
    hspec = pl.BlockSpec(memory_space=pltpu.HBM)
    blocks = vm((Q, 32, HS), BF)
    wide = vm((Q, 32, 2 * CP), BF)
    scratch = [
        vm((FSL, ND), BF), vm((K1, TGT), jnp.int32), vm((1, TGT), jnp.int32), vm((1, TGT), jnp.int32),
        vm((K2, TGT), jnp.int32), vm((2 * FSL, HID), BF), vm((C, HS), BF), vm((C, HS), BF), vm((C, TGT), BF),
        vm((K1 + 1, 16, TGT), BF), vm((ND, TGT), BF), vm((ND, TGT), BF), vm((TGT, 2 * FSL), BF),
        vm((2 * FSL, TGT), BF), vm((2, TGT, TGT), BF), vm((CP, TGT), BF), vm((2 * CP, HS), BF), vm((TGT, TGT), BF),
        vm((4, TGT, HS), BF), vm((4, TGT, HS), BF), vm((4, TGT, HS), F32), vm((3, TGT, HS), BF),
        vm((2, 128, HS), BF), vm((2, TGT, HS), BF),
        wide, wide, wide, wide, vm((2 * CP, TGT), BF), vm((TGT, HS), F32),
        blocks, blocks, blocks, blocks,
        vm((4, 2, TGT, HS), BF), vm((Q, 5, PIECE, HS), BF), vm((Q - 1, 5, PIECE, HS), BF),
        vm((15, 16, HS), BF), vm((2, Q - 1, 16, HS), BF), vm((Q, 3, 16, HS), BF), vm((15, 16, HS), BF),
        vm((LP, 32, TGT), BF), vm((Q - 1, 32, TGT), BF), vm((32, TGT), BF),
        dma((10,)), dma((4,)), dma((4,)), dma((4,)), dma((6,)), dma((6,)),
        dma((7,)), dma((7,)), dma((7,)), dma((7,)), dma((7,)), dma((7,)), dma((7,)), dma((7,)),
        dma((6,)), dma((6,)), dma((4,)), dma((4,)),
        dma((3, 7)), dma((3, 7)), dma((3, 7)), dma((3, 7)), dma((3, 7)), dma((3, 7)), dma((3, 7)), dma((3, 7)),
        dma((7,)), dma((7,)), dma((7,)), dma((7,)),
    ]
    gath, lout = pl.pallas_call(
        main_kernel,
        out_shape=(
            jax.ShapeDtypeStruct((Q, 15, 16, HS), BF),
            jax.ShapeDtypeStruct((LP, 32, TGT), BF),
        ),
        in_specs=[hspec] * 10,
        out_specs=(hspec, hspec),
        scratch_shapes=scratch,
        compiler_params=pltpu.CompilerParams(
            collective_id=0, has_side_effects=True, vmem_limit_bytes=62 * 1024 * 1024
        ),
        name="sage_step",
    )(
        features.T, near_ids.T, target_ids.reshape(1, TGT), seed_ids.reshape(1, TGT), seed_near.T,
        w1_self, w1_neigh, w2_self.T, w2_neigh.T, logit_grad.T,
    )
    logits, g1s, g1n, g2s, g2n = pl.pallas_call(
        finish_kernel,
        out_shape=(
            jax.ShapeDtypeStruct((C, TGT), F32),
            jax.ShapeDtypeStruct((FSL, HID), F32),
            jax.ShapeDtypeStruct((FSL, HID), F32),
            jax.ShapeDtypeStruct((C, HS), F32),
            jax.ShapeDtypeStruct((C, HS), F32),
        ),
        in_specs=[vspec, vspec],
        out_specs=(vspec,) * 5,
        compiler_params=pltpu.CompilerParams(vmem_limit_bytes=62 * 1024 * 1024),
        name="finish",
    )(gath, lout)
    return logits.T, g1s, g1n, g2s.T, g2n.T


def solution(mesh):
    return jax.shard_map(
        local,
        mesh=mesh,
        in_specs=(
            P("nodes", "feat"),
            P("nodes"),
            P("nodes", None),
            P("nodes"),
            P("nodes", None),
            P("feat", None),
            P("feat", None),
            P("feat", None),
            P("feat", None),
            P("nodes", None),
        ),
        out_specs=(
            P("nodes", None),
            P("feat", None),
            P("feat", None),
            P("feat", None),
            P("feat", None),
        ),
        check_vma=False,
    )
```

```python
import jax
import jax.numpy as jnp
from jax import lax
from jax.experimental import pallas as pl
from jax.experimental.pallas import tpu as pltpu
from jax.sharding import PartitionSpec as P

BF = jnp.bfloat16
F32 = jnp.float32
MESH = pl.DeviceIdType.MESH

TGT = 256
ND = 1024
FSL = 96
HID = 1024
HS = 128
C = 153
K1 = 25
K2 = 15
CP = 192
LP = 5
Q = 8
PIECE = 48
SETS = ((0, 2), (2, 2), (4, 1))


def dot(a, b):
    return jnp.dot(a, b, preferred_element_type=F32)


def dot_dims(a, b, ca, cb):
    return lax.dot_general(a, b, (((ca,), (cb,)), ((), ())), preferred_element_type=F32)


def main_kernel(
    features_hbm, near_hbm, tid_hbm, sid_hbm, snear_hbm,
    w1s_hbm, w1n_hbm, w2s_hbm, w2n_hbm, lg_hbm,
    gath, lout,
    feat_v, near_v, tid_v, sid_v, snear_v, w1_v, w2s_v, w2n_v, lg_v,
    keys, tally, sel, x_v, xt, seedtally, lgp, w2c, perm,
    pair_src, pair_rcv, p_own, rs_src, relay_rcv, rs_rcv,
    bz_src, bz_rcv, bw_src, bw_rcv, dt, d_hid,
    fw_src, fw_rcv, fz_src, fz_rcv,
    ag, gst, rw_rcv, zsrc, z_rcv, zc_rcv, zfull, lst, l_rcv, ltot,
    in_sem, out_sem, pair_s, pair_r, rs_s, rs_r, bz_s, bz_r, bw_s, bw_r,
    fw_s, fw_r, fz_s, fz_r, ag_s, ag_r, agf_s, agf_r,
    rw_s, rw_r, z_s, z_r, az_s, az_r, aw_s, aw_r, l_s, l_r, la_s, la_r,
):
    node = lax.axis_index("nodes")
    f = lax.axis_index("feat")
    z = node // Q
    w = node % Q
    h = f // 2
    c = f % 2

    def z_peer(d):
        zz = lax.rem(z + d, Q)
        return zz, (zz * Q + w, f)

    def w_peer(d):
        ww = lax.rem(w + d, Q)
        return ww, (z * Q + ww, f)

    def f_peer(d):
        ff = lax.rem(f + d, Q)
        return ff, (node, ff)

    partner = (node, h * 2 + (1 - c))

    up = (node, lax.rem(h + 1, 4) * 2 + c)
    down = (node, lax.rem(h + 3, 4) * 2 + c)

    def each(body):
        def step(d, carry):
            body(d)
            return carry

        lax.fori_loop(1, Q, step, 0)

    barrier = pltpu.get_barrier_semaphore()

    def greet(d):
        for where in (z_peer(d)[1], w_peer(d)[1], f_peer(d)[1]):
            pl.semaphore_signal(barrier, inc=1, device_id=where, device_id_type=MESH)

    each(greet)

    loads = [
        pltpu.make_async_copy(src, dst, in_sem.at[n])
        for n, (src, dst) in enumerate(
            (
                (snear_hbm, snear_v),
                (sid_hbm, sid_v),
                (lg_hbm, lg_v),
                (w2s_hbm, w2s_v),
                (w2n_hbm, w2n_v),
                (near_hbm, near_v),
                (tid_hbm, tid_v),
                (features_hbm, feat_v),
                (w1s_hbm, w1_v.at[pl.ds(0, FSL)]),
                (w1n_hbm, w1_v.at[pl.ds(FSL, FSL)]),
            )
        )
    ]
    for load in loads:
        load.start()

    pending = []

    def remote(src, dst, s_sem, r_sem, where):
        return pltpu.make_async_remote_copy(
            src_ref=src, dst_ref=dst, send_sem=s_sem, recv_sem=r_sem,
            device_id=where, device_id_type=MESH,
        )

    def send(*args):
        copy = remote(*args)
        copy.start()
        pending.append(copy.wait_send)

    def send_each(copy_of, test_of=None):
        def start(d):
            if test_of is None:
                copy_of(d).start()
            else:
                pl.when(test_of(d))(lambda: copy_of(d).start())

        def finish(d):
            if test_of is None:
                copy_of(d).wait_send()
            else:
                pl.when(test_of(d))(lambda: copy_of(d).wait_send())

        each(start)
        pending.append(lambda: each(finish))

    def sent():
        for finish in pending:
            finish()
        pending.clear()

    def landed(ref, r_sem):
        pltpu.make_async_copy(ref, ref, r_sem).wait()

    row = lax.broadcasted_iota(jnp.int32, (8, 128), 0)

    def count(ids, own, low, words, totals_of, ones_of):
        fan = ids.shape[0]
        high = lax.shift_right_logical(ids, low.bit_length() - 1)
        digit = lax.shift_left(jnp.ones_like(ids), (high & 3) * 8)
        tables = [ids & (low - 1)]
        tables += [jnp.where((high >> 2) == g, digit, 0) for g in range(words)]
        for n, table in enumerate(tables):
            for k in range(fan):
                keys[n, k] = jnp.broadcast_to(table[k:k + 1], (8, TGT))
        keys[0, K1] = jnp.broadcast_to(own, (8, TGT))

        def body(step, carry):
            mine = [step * 32 + j * 8 + row for j in range(4)]
            for half in range(2):
                cols = slice(half * 128, half * 128 + 128)
                totals = [[jnp.zeros((8, 128), jnp.int32)] * 4 for _ in range(words)]
                for k in range(fan):
                    theirs = keys[0, k, :, cols]
                    hits = [theirs == m for m in mine]
                    for g in range(words):
                        word = keys[1 + g, k, :, cols]
                        totals[g] = [t + jnp.where(hit, word, 0) for t, hit in zip(totals[g], hits)]
                theirs = keys[0, K1, :, cols]
                for part in range(4 * words):
                    for j in (0, 2):
                        first = part * low + step * 32 + j * 8
                        rows = pl.ds(pl.multiple_of(first, 16), 16)
                        both = [
                            lax.shift_right_logical(totals[part // 4][n], 8 * (part % 4)) & 255
                            for n in (j, j + 1)
                        ]
                        totals_of[rows, cols] = jnp.concatenate(both, axis=0).astype(F32).astype(BF)
                        both = [
                            jnp.where(theirs == mine[n] + part * low, 1.0, 0.0) for n in (j, j + 1)
                        ]
                        ones_of[rows, cols] = jnp.concatenate(both, axis=0).astype(BF)
            return carry

        lax.fori_loop(0, low // 32, body, 0)

    def swap(n):
        return ((n >> 2) & 7) * 32 + (n >> 5) * 4 + (n & 3)

    a = lax.broadcasted_iota(jnp.int32, (TGT, TGT), 0)
    b = lax.broadcasted_iota(jnp.int32, (TGT, TGT), 1)
    perm[...] = jnp.where(swap(a) == b, 1.0, 0.0).astype(BF)

    for n in range(5):
        loads[n].wait()
    for padded, first, given in ((lgp, 0, lg_v), (w2c, 0, w2s_v), (w2c, CP, w2n_v)):
        padded[first:first + CP] = jnp.zeros((CP, padded.shape[1]), BF)
        padded[first:first + C] = given[...]
    count(swap(snear_v[...]), swap(sid_v[...]), 64, 1, seedtally.at[1], seedtally.at[0])
    lg = lgp[...].astype(F32).T.astype(BF)
    back = jnp.concatenate([dot(seedtally[0], lg), dot(seedtally[1], lg) / K2], axis=1)
    bw_src[...] = back.astype(BF).reshape(Q, 32, 2 * CP)

    def to_w(src, dst, s_sem, r_sem):
        def copy_of(d):
            ww, where = w_peer(d)
            return remote(src.at[ww], dst.at[w], s_sem.at[d - 1], r_sem.at[d - 1], where)

        send_each(copy_of)
        dst[w] = src[w]

    def to_z(src, dst, s_sem, r_sem):
        def copy_of(d):
            zz, where = z_peer(d)
            return remote(src.at[zz], dst.at[z], s_sem.at[d - 1], r_sem.at[d - 1], where)

        send_each(copy_of)
        dst[z] = src[z]

    def from_w(dst, r_sem):
        each(lambda d: landed(dst.at[lax.rem(w + Q - d, Q)], r_sem.at[d - 1]))

    def from_z(dst, r_sem):
        each(lambda d: landed(dst.at[lax.rem(z + Q - d, Q)], r_sem.at[d - 1]))

    pl.semaphore_wait(barrier, 3 * (Q - 1))
    to_w(bw_src, bw_rcv, bw_s, bw_r)

    loads[5].wait()
    loads[6].wait()
    count(near_v[...], tid_v[...], 128, 2, tally, sel)

    loads[7].wait()
    x_self = (dot(feat_v[...], sel[...])).astype(BF)
    agg = (dot(feat_v[...], tally[...]) / K1).astype(BF)
    xt[0:FSL] = x_self
    xt[FSL:2 * FSL] = agg
    x_v[...] = jnp.concatenate([x_self.astype(F32), agg.astype(F32)], axis=0).T.astype(BF)

    loads[8].wait()
    loads[9].wait()

    def partial(dh, cc):
        col = pl.ds(pl.multiple_of((lax.rem(h + dh, 4) * 2 + cc) * HS, HS), HS)
        return dot(x_v[...], w1_v[:, col])

    for dh in (2, 1, 3, 0):
        pair_src[dh] = partial(dh, 1 - c).astype(BF)
        send(pair_src.at[dh], pair_rcv.at[dh], pair_s.at[dh], pair_r.at[dh], partner)
    for dh in (2, 1, 3, 0):
        p_own[dh] = partial(dh, c)
    from_w(bw_rcv, bw_r)
    turned = dot(perm[...], bw_rcv[...].reshape(TGT, 2 * CP)).astype(BF)
    bz_src[...] = turned.reshape(Q, 32, 2 * CP)
    to_z(bz_src, bz_rcv, bz_s, bz_r)

    lo, hi = pl.ds(0, 128), pl.ds(128, 128)
    landed(pair_rcv.at[2], pair_r.at[2])
    rs_src[0] = (p_own[2] + pair_rcv[2].astype(F32)).astype(BF)
    send(rs_src.at[0, lo], relay_rcv.at[0], rs_s.at[0], rs_r.at[0], up)
    send(rs_src.at[0, hi], relay_rcv.at[1], rs_s.at[1], rs_r.at[1], down)
    landed(pair_rcv.at[1], pair_r.at[1])
    rs_src[1, 128:256] = (p_own[1, 128:256] + pair_rcv[1, 128:256].astype(F32)).astype(BF)
    send(rs_src.at[1, hi], rs_rcv.at[0, hi], rs_s.at[2], rs_r.at[2], up)
    landed(pair_rcv.at[3], pair_r.at[3])
    rs_src[2, 0:128] = (p_own[3, 0:128] + pair_rcv[3, 0:128].astype(F32)).astype(BF)
    send(rs_src.at[2, lo], rs_rcv.at[1, lo], rs_s.at[3], rs_r.at[3], down)
    landed(relay_rcv.at[0], rs_r.at[0])
    rs_src[1, 0:128] = (
        p_own[1, 0:128] + pair_rcv[1, 0:128].astype(F32) + relay_rcv[0].astype(F32)
    ).astype(BF)
    send(rs_src.at[1, lo], rs_rcv.at[0, lo], rs_s.at[4], rs_r.at[4], up)
    landed(relay_rcv.at[1], rs_r.at[1])
    rs_src[2, 128:256] = (
        p_own[3, 128:256] + pair_rcv[3, 128:256].astype(F32) + relay_rcv[1].astype(F32)
    ).astype(BF)
    send(rs_src.at[2, hi], rs_rcv.at[1, hi], rs_s.at[5], rs_r.at[5], down)

    from_z(bz_rcv, bz_r)
    back = bz_rcv[...].reshape(TGT, 2 * CP)
    d_hid[...] = dot(back, w2c[...])
    dt[...] = back.astype(F32).T.astype(BF)

    landed(pair_rcv.at[0], pair_r.at[0])
    pre = p_own[0] + pair_rcv[0].astype(F32)
    landed(rs_rcv.at[0, hi], rs_r.at[2])
    landed(rs_rcv.at[1, lo], rs_r.at[3])
    landed(rs_rcv.at[0, lo], rs_r.at[4])
    landed(rs_rcv.at[1, hi], rs_r.at[5])
    pre = pre + rs_rcv[0].astype(F32) + rs_rcv[1].astype(F32)
    sigma = 1.0 / (1.0 + jnp.exp(-pre))
    ag[0, 0] = (d_hid[...] * (sigma * (1.0 + pre * (1.0 - sigma)))).astype(BF)
    send(ag.at[0, 0, lo], ag.at[3, 0, lo], ag_s.at[0], ag_r.at[0], up)
    send(ag.at[0, 0, hi], ag.at[1, 0, hi], ag_s.at[1], ag_r.at[1], down)
    send(ag.at[0, 0], ag.at[0, 1], agf_s.at[0], agf_r.at[0], partner)
    send(ag.at[0, 0, hi], ag.at[3, 0, hi], ag_s.at[2], ag_r.at[2], up)
    send(ag.at[0, 0, lo], ag.at[1, 0, lo], ag_s.at[3], ag_r.at[3], down)
    hidden = (pre * sigma).astype(BF)
    fz_src[...] = hidden.reshape(Q, 32, HS)
    to_z(fz_src, fz_rcv, fz_s, fz_r)
    gst[:, 0] = dot(dt[...], hidden).astype(BF).reshape(Q, PIECE, HS)

    slots = {0: 1, 1: 2, 3: 3, 2: 4}

    def lower(dh, dc):
        grad = dot(xt[...], ag[dh, dc]).astype(BF).reshape(4, PIECE, HS)
        cc = c if dc == 0 else 1 - c
        gst[pl.ds(cc * 4, 4), slots[dh]] = grad

    def scatter(n):
        span = pl.ds(*SETS[n])

        def copy_of(d):
            ww, where = w_peer(d)
            return remote(
                gst.at[ww, span], rw_rcv.at[d - 1, span], rw_s.at[n, d - 1], rw_r.at[n, d - 1], where
            )

        send_each(copy_of)

    def reduce_w(n):
        first, many = SETS[n]
        each(lambda d: landed(rw_rcv.at[d - 1, pl.ds(first, many)], rw_r.at[n, d - 1]))
        for slot in range(first, first + many):
            total = gst[w, slot].astype(F32)
            for d in range(1, Q):
                total = total + rw_rcv[d - 1, slot].astype(F32)
            zsrc[slot * 3:slot * 3 + 3] = total.astype(BF).reshape(3, 16, HS)

    def owned(n, zz):
        lo, hi = SETS[n][0] * 3, (SETS[n][0] + SETS[n][1]) * 3
        k = lo + lax.rem(zz + 16 - lo % Q, Q)
        return k < hi, jnp.minimum(k, hi - 1)

    def scatter_z(n):
        reduce_w(n)

        def copy_of(d):
            zz, where = z_peer(d)
            k = owned(n, zz)[1]
            return remote(zsrc.at[k], z_rcv.at[n, d - 1], z_s.at[n, d - 1], z_r.at[n, d - 1], where)

        send_each(copy_of, lambda d: owned(n, z_peer(d)[0])[0])

    def gather_z(n):
        test, k = owned(n, z)

        @pl.when(test)
        def _():
            each(lambda d: landed(z_rcv.at[n, d - 1], z_r.at[n, d - 1]))
            total = zsrc[k].astype(F32)
            for d in range(1, Q):
                total = total + z_rcv[n, d - 1].astype(F32)
            zfull[k] = total.astype(BF)

        def copy_of(d):
            return remote(zfull.at[k], zfull.at[k], az_s.at[n, d - 1], az_r.at[n, d - 1], z_peer(d)[1])

        send_each(copy_of, lambda d: test)

    def gather_w(n):
        pieces = pl.ds(SETS[n][0] * 3, SETS[n][1] * 3)

        def wait(d):
            test, k = owned(n, lax.rem(z + Q - d, Q))
            pl.when(test)(lambda: landed(zfull.at[k], az_r.at[n, d - 1]))

        if n < 2:
            each(wait)

        def copy_of(d):
            return remote(
                zfull.at[pieces], gath.at[w, pieces], aw_s.at[n, d - 1], aw_r.at[n, d - 1], w_peer(d)[1]
            )

        send_each(copy_of)
        pltpu.make_async_copy(zfull.at[pieces], gath.at[w, pieces], out_sem.at[n]).start()

    last = pl.ds(12, 3)

    def exchange_z():
        reduce_w(2)

        def copy_of(d):
            return remote(zsrc.at[last], zc_rcv.at[z], z_s.at[2, d - 1], z_r.at[2, d - 1], z_peer(d)[1])

        send_each(copy_of)
        zc_rcv[z] = zsrc[12:15]

    def sum_z():
        from_z(zc_rcv, z_r.at[2])
        total = zc_rcv[0].astype(F32)
        for zz in range(1, Q):
            total = total + zc_rcv[zz].astype(F32)
        zfull[12:15] = total.astype(BF)

    lower(0, 0)
    landed(ag.at[0, 1], agf_r.at[0])
    lower(0, 1)
    scatter(0)

    landed(ag.at[3, 0, lo], ag_r.at[0])
    send(ag.at[3, 0, lo], ag.at[2, 0, lo], ag_s.at[4], ag_r.at[4], up)
    landed(ag.at[1, 0, hi], ag_r.at[1])
    send(ag.at[1, 0, hi], ag.at[2, 0, hi], ag_s.at[5], ag_r.at[5], down)
    landed(ag.at[3, 0, hi], ag_r.at[2])
    send(ag.at[3, 0], ag.at[3, 1], agf_s.at[3], agf_r.at[3], partner)
    landed(ag.at[1, 0, lo], ag_r.at[3])
    send(ag.at[1, 0], ag.at[1, 1], agf_s.at[1], agf_r.at[1], partner)
    lower(3, 0)
    lower(1, 0)

    from_z(fz_rcv, fz_r)
    fw_src[...] = dot(perm[...], fz_rcv[...].reshape(TGT, HS)).astype(BF).reshape(Q, 32, HS)
    to_w(fw_src, fw_rcv, fw_s, fw_r)

    scatter_z(0)
    landed(ag.at[3, 1], agf_r.at[3])
    lower(3, 1)
    landed(ag.at[1, 1], agf_r.at[1])
    lower(1, 1)
    scatter(1)
    landed(ag.at[2, 0, lo], ag_r.at[4])
    landed(ag.at[2, 0, hi], ag_r.at[5])
    send(ag.at[2, 0], ag.at[2, 1], agf_s.at[2], agf_r.at[2], partner)
    lower(2, 0)
    gather_z(0)
    landed(ag.at[2, 1], agf_r.at[2])
    lower(2, 1)
    scatter(2)
    scatter_z(1)

    from_w(fw_rcv, fw_r)
    received = fw_rcv[...].reshape(TGT, HS).astype(F32).T.astype(BF)
    h_self = dot(received, seedtally[0]).astype(BF)
    agg_two = (dot(received, seedtally[1]) / K2).astype(BF)
    part = dot(w2c[0:CP], h_self) + dot(w2c[CP:2 * CP], agg_two)
    lst[...] = part[0:LP * 32].astype(BF).reshape(LP, 32, TGT)

    def logit_part(d):
        ff, where = f_peer(d)
        return remote(lst.at[lax.rem(ff, LP)], l_rcv.at[d - 1], l_s.at[d - 1], l_r.at[d - 1], where)

    send_each(logit_part, lambda d: f_peer(d)[0] < LP)

    gather_w(0)
    exchange_z()
    gather_z(1)

    fl = lax.rem(f, LP)

    @pl.when(f < LP)
    def _():
        each(lambda d: landed(l_rcv.at[d - 1], l_r.at[d - 1]))
        total = lst[fl].astype(F32)
        for d in range(1, Q):
            total = total + l_rcv[d - 1].astype(F32)
        ltot[...] = total.astype(BF)
        pltpu.make_async_copy(ltot, lout.at[fl], out_sem.at[3]).start()

    def logit_sum(d):
        return remote(ltot, lout.at[fl], la_s.at[d - 1], la_r.at[d - 1], f_peer(d)[1])

    send_each(logit_sum, lambda d: f < LP)

    gather_w(1)
    sum_z()
    gather_w(2)
    sent()

    def logits_in(d):
        ff = lax.rem(f + Q - d, Q)
        pl.when(ff < LP)(lambda: landed(lout.at[lax.rem(ff, LP)], la_r.at[d - 1]))

    each(logits_in)

    @pl.when(f < LP)
    def _():
        landed(lout.at[fl], out_sem.at[3])

    for n, (first, many) in enumerate(SETS):
        pieces = pl.ds(first * 3, many * 3)
        each(lambda d: landed(gath.at[lax.rem(w + Q - d, Q), pieces], aw_r.at[n, d - 1]))
        landed(gath.at[w, pieces], out_sem.at[n])


def finish_kernel(gath, lout, logits, g1s, g1n, g2s, g2n):
    h = lax.axis_index("feat") // 2
    logits[...] = lout[...].reshape(LP * 32, TGT)[0:C].astype(F32)
    for ww in range(Q):
        cc, k = ww // 4, ww % 4
        mine = gath[ww].reshape(5 * PIECE, HS).astype(F32)
        out = g2s if ww < 4 else g2n
        count = min(PIECE, C - k * PIECE)
        out[k * PIECE:k * PIECE + count] = mine[0:count]
        out = g1s if k < 2 else g1n
        for slot, dh in ((1, 0), (2, 1), (3, 3), (4, 2)):
            col = pl.ds(pl.multiple_of((2 * lax.rem(h + dh, 4) + cc) * HS, HS), HS)
            out[(k % 2) * PIECE:(k % 2 + 1) * PIECE, col] = mine[slot * PIECE:(slot + 1) * PIECE]


def local(
    features, target_ids, near_ids, seed_ids, seed_near, w1_self, w1_neigh, w2_self, w2_neigh, logit_grad
):
    vm = pltpu.VMEM
    dma = pltpu.SemaphoreType.DMA
    vspec = pl.BlockSpec(memory_space=pltpu.VMEM)
    hspec = pl.BlockSpec(memory_space=pltpu.HBM)
    blocks = vm((Q, 32, HS), BF)
    wide = vm((Q, 32, 2 * CP), BF)
    scratch = [
        vm((FSL, ND), BF), vm((K1, TGT), jnp.int32), vm((1, TGT), jnp.int32), vm((1, TGT), jnp.int32),
        vm((K2, TGT), jnp.int32), vm((2 * FSL, HID), BF), vm((C, HS), BF), vm((C, HS), BF), vm((C, TGT), BF),
        vm((3, K1 + 1, 8, TGT), jnp.int32), vm((ND, TGT), BF), vm((ND, TGT), BF), vm((TGT, 2 * FSL), BF),
        vm((2 * FSL, TGT), BF), vm((2, TGT, TGT), BF), vm((CP, TGT), BF), vm((2 * CP, HS), BF), vm((TGT, TGT), BF),
        vm((4, TGT, HS), BF), vm((4, TGT, HS), BF), vm((4, TGT, HS), F32), vm((3, TGT, HS), BF),
        vm((2, 128, HS), BF), vm((2, TGT, HS), BF),
        wide, wide, wide, wide, vm((2 * CP, TGT), BF), vm((TGT, HS), F32),
        blocks, blocks, blocks, blocks,
        vm((4, 2, TGT, HS), BF), vm((Q, 5, PIECE, HS), BF), vm((Q - 1, 5, PIECE, HS), BF),
        vm((15, 16, HS), BF), vm((2, Q - 1, 16, HS), BF), vm((Q, 3, 16, HS), BF), vm((15, 16, HS), BF),
        vm((LP, 32, TGT), BF), vm((Q - 1, 32, TGT), BF), vm((32, TGT), BF),
        dma((10,)), dma((4,)), dma((4,)), dma((4,)), dma((6,)), dma((6,)),
        dma((7,)), dma((7,)), dma((7,)), dma((7,)), dma((7,)), dma((7,)), dma((7,)), dma((7,)),
        dma((6,)), dma((6,)), dma((4,)), dma((4,)),
        dma((3, 7)), dma((3, 7)), dma((3, 7)), dma((3, 7)), dma((3, 7)), dma((3, 7)), dma((3, 7)), dma((3, 7)),
        dma((7,)), dma((7,)), dma((7,)), dma((7,)),
    ]
    gath, lout = pl.pallas_call(
        main_kernel,
        out_shape=(
            jax.ShapeDtypeStruct((Q, 15, 16, HS), BF),
            jax.ShapeDtypeStruct((LP, 32, TGT), BF),
        ),
        in_specs=[hspec] * 10,
        out_specs=(hspec, hspec),
        scratch_shapes=scratch,
        compiler_params=pltpu.CompilerParams(
            collective_id=0, has_side_effects=True, vmem_limit_bytes=62 * 1024 * 1024
        ),
        name="sage_step",
    )(
        features.T, near_ids.T, target_ids.reshape(1, TGT), seed_ids.reshape(1, TGT), seed_near.T,
        w1_self, w1_neigh, w2_self.T, w2_neigh.T, logit_grad.T,
    )
    logits, g1s, g1n, g2s, g2n = pl.pallas_call(
        finish_kernel,
        out_shape=(
            jax.ShapeDtypeStruct((C, TGT), F32),
            jax.ShapeDtypeStruct((FSL, HID), F32),
            jax.ShapeDtypeStruct((FSL, HID), F32),
            jax.ShapeDtypeStruct((C, HS), F32),
            jax.ShapeDtypeStruct((C, HS), F32),
        ),
        in_specs=[vspec, vspec],
        out_specs=(vspec,) * 5,
        compiler_params=pltpu.CompilerParams(vmem_limit_bytes=62 * 1024 * 1024),
        name="finish",
    )(gath, lout)
    return logits.T, g1s, g1n, g2s.T, g2n.T


def solution(mesh):
    return jax.shard_map(
        local,
        mesh=mesh,
        in_specs=(
            P("nodes", "feat"),
            P("nodes"),
            P("nodes", None),
            P("nodes"),
            P("nodes", None),
            P("feat", None),
            P("feat", None),
            P("feat", None),
            P("feat", None),
            P("nodes", None),
        ),
        out_specs=(
            P("nodes", None),
            P("feat", None),
            P("feat", None),
            P("feat", None),
            P("feat", None),
        ),
        check_vma=False,
    )
```

```python
import jax
import jax.numpy as jnp
from jax import lax
from jax.experimental import pallas as pl
from jax.experimental.pallas import tpu as pltpu
from jax.sharding import PartitionSpec as P

BF = jnp.bfloat16
F32 = jnp.float32
MESH = pl.DeviceIdType.MESH

TGT = 256
ND = 1024
FSL = 96
HID = 1024
HS = 128
C = 153
K1 = 25
K2 = 15
CP = 192
LP = 5
Q = 8
PIECE = 48
SETS = ((0, 2), (2, 2), (4, 1))


def dot(a, b):
    return jnp.dot(a, b, preferred_element_type=F32)


def dot_dims(a, b, ca, cb):
    return lax.dot_general(a, b, (((ca,), (cb,)), ((), ())), preferred_element_type=F32)


def main_kernel(
    features_hbm, near_hbm, tid_hbm, sid_hbm, snear_hbm,
    w1s_hbm, w1n_hbm, w2s_hbm, w2n_hbm, lg_hbm,
    gath, lout,
    feat_v, near_v, tid_v, sid_v, snear_v, w1_v, w2s_v, w2n_v, lg_v,
    keys, tally, sel, x_v, xt, seedtally, lgp, w2c, perm,
    pair_src, pair_rcv, p_own, rs_src, relay_rcv, rs_rcv,
    bz_src, bz_rcv, bw_src, bw_rcv, dt, d_hid,
    fw_src, fw_rcv, fz_src, fz_rcv,
    ag, gst, rw_rcv, zsrc, z_rcv, zc_rcv, zfull, lst, l_rcv, ltot,
    in_sem, out_sem, pair_s, pair_r, rs_s, rs_r, bz_s, bz_r, bw_s, bw_r,
    fw_s, fw_r, fz_s, fz_r, ag_s, ag_r, agf_s, agf_r,
    rw_s, rw_r, z_s, z_r, az_s, az_r, aw_s, aw_r, l_s, l_r, la_s, la_r,
):
    node = lax.axis_index("nodes")
    f = lax.axis_index("feat")
    z = node // Q
    w = node % Q
    h = f // 2
    c = f % 2

    def z_peer(d):
        return z ^ d, (node ^ (d * Q), f)

    def w_peer(d):
        return w ^ d, (node ^ d, f)

    def f_peer(d):
        return f ^ d, (node, f ^ d)

    partner = (node, h * 2 + (1 - c))

    up = (node, lax.rem(h + 1, 4) * 2 + c)
    down = (node, lax.rem(h + 3, 4) * 2 + c)

    def each(body):
        for d in range(1, Q):
            body(d)

    barrier = pltpu.get_barrier_semaphore()

    def greet(d):
        for where in (z_peer(d)[1], w_peer(d)[1], f_peer(d)[1]):
            pl.semaphore_signal(barrier, inc=1, device_id=where, device_id_type=MESH)

    each(greet)

    loads = [
        pltpu.make_async_copy(src, dst, in_sem.at[n])
        for n, (src, dst) in enumerate(
            (
                (snear_hbm, snear_v),
                (sid_hbm, sid_v),
                (lg_hbm, lg_v),
                (w2s_hbm, w2s_v),
                (w2n_hbm, w2n_v),
                (near_hbm, near_v),
                (tid_hbm, tid_v),
                (features_hbm, feat_v),
                (w1s_hbm, w1_v.at[pl.ds(0, FSL)]),
                (w1n_hbm, w1_v.at[pl.ds(FSL, FSL)]),
            )
        )
    ]
    for load in loads:
        load.start()

    pending = []

    def remote(src, dst, s_sem, r_sem, where):
        return pltpu.make_async_remote_copy(
            src_ref=src, dst_ref=dst, send_sem=s_sem, recv_sem=r_sem,
            device_id=where, device_id_type=MESH,
        )

    def send(*args):
        copy = remote(*args)
        copy.start()
        pending.append(copy.wait_send)

    def send_each(copy_of, test_of=None):
        def start(d):
            if test_of is None:
                copy_of(d).start()
            else:
                pl.when(test_of(d))(lambda: copy_of(d).start())

        def finish(d):
            if test_of is None:
                copy_of(d).wait_send()
            else:
                pl.when(test_of(d))(lambda: copy_of(d).wait_send())

        each(start)
        pending.append(lambda: each(finish))

    def sent():
        for finish in pending:
            finish()
        pending.clear()

    def landed(ref, r_sem):
        pltpu.make_async_copy(ref, ref, r_sem).wait()

    row = lax.broadcasted_iota(jnp.int32, (8, 128), 0)

    def count(ids, own, low, words, totals_of, ones_of):
        fan = ids.shape[0]
        high = lax.shift_right_logical(ids, low.bit_length() - 1)
        digit = lax.shift_left(jnp.ones_like(ids), (high & 3) * 8)
        tables = [ids & (low - 1)]
        tables += [jnp.where((high >> 2) == g, digit, 0) for g in range(words)]
        for n, table in enumerate(tables):
            for k in range(fan):
                keys[n, k] = jnp.broadcast_to(table[k:k + 1], (8, TGT))
        keys[0, K1] = jnp.broadcast_to(own, (8, TGT))

        def body(step, carry):
            mine = [step * 32 + j * 8 + row for j in range(4)]
            for half in range(2):
                cols = slice(half * 128, half * 128 + 128)
                totals = [[jnp.zeros((8, 128), jnp.int32)] * 4 for _ in range(words)]
                for k in range(fan):
                    theirs = keys[0, k, :, cols]
                    hits = [theirs == m for m in mine]
                    for g in range(words):
                        word = keys[1 + g, k, :, cols]
                        totals[g] = [t + jnp.where(hit, word, 0) for t, hit in zip(totals[g], hits)]
                theirs = keys[0, K1, :, cols]
                for part in range(4 * words):
                    for j in (0, 2):
                        first = part * low + step * 32 + j * 8
                        rows = pl.ds(pl.multiple_of(first, 16), 16)
                        both = [
                            lax.shift_right_logical(totals[part // 4][n], 8 * (part % 4)) & 255
                            for n in (j, j + 1)
                        ]
                        totals_of[rows, cols] = jnp.concatenate(both, axis=0).astype(F32).astype(BF)
                        both = [
                            jnp.where(theirs == mine[n] + part * low, 1.0, 0.0) for n in (j, j + 1)
                        ]
                        ones_of[rows, cols] = jnp.concatenate(both, axis=0).astype(BF)
            return carry

        lax.fori_loop(0, low // 32, body, 0)

    def swap(n):
        return ((n >> 2) & 7) * 32 + (n >> 5) * 4 + (n & 3)

    a = lax.broadcasted_iota(jnp.int32, (TGT, TGT), 0)
    b = lax.broadcasted_iota(jnp.int32, (TGT, TGT), 1)
    perm[...] = jnp.where(swap(a) == b, 1.0, 0.0).astype(BF)

    for n in range(5):
        loads[n].wait()
    for padded, first, given in ((lgp, 0, lg_v), (w2c, 0, w2s_v), (w2c, CP, w2n_v)):
        padded[first:first + CP] = jnp.zeros((CP, padded.shape[1]), BF)
        padded[first:first + C] = given[...]
    count(swap(snear_v[...]), swap(sid_v[...]), 64, 1, seedtally.at[1], seedtally.at[0])
    lg = lgp[...].astype(F32).T.astype(BF)
    back = jnp.concatenate([dot(seedtally[0], lg), dot(seedtally[1], lg) / K2], axis=1)
    bw_src[...] = back.astype(BF).reshape(Q, 32, 2 * CP)

    def to_w(src, dst, s_sem, r_sem):
        def copy_of(d):
            ww, where = w_peer(d)
            return remote(src.at[ww], dst.at[w], s_sem.at[d - 1], r_sem.at[d - 1], where)

        send_each(copy_of)
        dst[w] = src[w]

    def to_z(src, dst, s_sem, r_sem):
        def copy_of(d):
            zz, where = z_peer(d)
            return remote(src.at[zz], dst.at[z], s_sem.at[d - 1], r_sem.at[d - 1], where)

        send_each(copy_of)
        dst[z] = src[z]

    def from_w(dst, r_sem):
        each(lambda d: landed(dst.at[w ^ d], r_sem.at[d - 1]))

    def from_z(dst, r_sem):
        each(lambda d: landed(dst.at[z ^ d], r_sem.at[d - 1]))

    pl.semaphore_wait(barrier, 3 * (Q - 1))
    to_w(bw_src, bw_rcv, bw_s, bw_r)

    loads[5].wait()
    loads[6].wait()
    count(near_v[...], tid_v[...], 128, 2, tally, sel)

    loads[7].wait()
    x_self = (dot(feat_v[...], sel[...])).astype(BF)
    agg = (dot(feat_v[...], tally[...]) / K1).astype(BF)
    xt[0:FSL] = x_self
    xt[FSL:2 * FSL] = agg
    x_v[...] = jnp.concatenate([x_self.astype(F32), agg.astype(F32)], axis=0).T.astype(BF)

    loads[8].wait()
    loads[9].wait()

    def partial(dh, cc):
        col = pl.ds(pl.multiple_of((lax.rem(h + dh, 4) * 2 + cc) * HS, HS), HS)
        return dot(x_v[...], w1_v[:, col])

    for dh in (2, 1, 3, 0):
        pair_src[dh] = partial(dh, 1 - c).astype(BF)
        send(pair_src.at[dh], pair_rcv.at[dh], pair_s.at[dh], pair_r.at[dh], partner)
    for dh in (2, 1, 3, 0):
        p_own[dh] = partial(dh, c)
    from_w(bw_rcv, bw_r)
    turned = dot(perm[...], bw_rcv[...].reshape(TGT, 2 * CP)).astype(BF)
    bz_src[...] = turned.reshape(Q, 32, 2 * CP)
    to_z(bz_src, bz_rcv, bz_s, bz_r)

    lo, hi = pl.ds(0, 128), pl.ds(128, 128)
    landed(pair_rcv.at[2], pair_r.at[2])
    rs_src[0] = (p_own[2] + pair_rcv[2].astype(F32)).astype(BF)
    send(rs_src.at[0, lo], relay_rcv.at[0], rs_s.at[0], rs_r.at[0], up)
    send(rs_src.at[0, hi], relay_rcv.at[1], rs_s.at[1], rs_r.at[1], down)
    landed(pair_rcv.at[1], pair_r.at[1])
    rs_src[1, 128:256] = (p_own[1, 128:256] + pair_rcv[1, 128:256].astype(F32)).astype(BF)
    send(rs_src.at[1, hi], rs_rcv.at[0, hi], rs_s.at[2], rs_r.at[2], up)
    landed(pair_rcv.at[3], pair_r.at[3])
    rs_src[2, 0:128] = (p_own[3, 0:128] + pair_rcv[3, 0:128].astype(F32)).astype(BF)
    send(rs_src.at[2, lo], rs_rcv.at[1, lo], rs_s.at[3], rs_r.at[3], down)
    landed(relay_rcv.at[0], rs_r.at[0])
    rs_src[1, 0:128] = (
        p_own[1, 0:128] + pair_rcv[1, 0:128].astype(F32) + relay_rcv[0].astype(F32)
    ).astype(BF)
    send(rs_src.at[1, lo], rs_rcv.at[0, lo], rs_s.at[4], rs_r.at[4], up)
    landed(relay_rcv.at[1], rs_r.at[1])
    rs_src[2, 128:256] = (
        p_own[3, 128:256] + pair_rcv[3, 128:256].astype(F32) + relay_rcv[1].astype(F32)
    ).astype(BF)
    send(rs_src.at[2, hi], rs_rcv.at[1, hi], rs_s.at[5], rs_r.at[5], down)

    from_z(bz_rcv, bz_r)
    back = bz_rcv[...].reshape(TGT, 2 * CP)
    d_hid[...] = dot(back, w2c[...])
    dt[...] = back.astype(F32).T.astype(BF)

    landed(pair_rcv.at[0], pair_r.at[0])
    pre = p_own[0] + pair_rcv[0].astype(F32)
    landed(rs_rcv.at[0, hi], rs_r.at[2])
    landed(rs_rcv.at[1, lo], rs_r.at[3])
    landed(rs_rcv.at[0, lo], rs_r.at[4])
    landed(rs_rcv.at[1, hi], rs_r.at[5])
    pre = pre + rs_rcv[0].astype(F32) + rs_rcv[1].astype(F32)
    sigma = 1.0 / (1.0 + jnp.exp(-pre))
    ag[0, 0] = (d_hid[...] * (sigma * (1.0 + pre * (1.0 - sigma)))).astype(BF)
    send(ag.at[0, 0, lo], ag.at[3, 0, lo], ag_s.at[0], ag_r.at[0], up)
    send(ag.at[0, 0, hi], ag.at[1, 0, hi], ag_s.at[1], ag_r.at[1], down)
    send(ag.at[0, 0], ag.at[0, 1], agf_s.at[0], agf_r.at[0], partner)
    send(ag.at[0, 0, hi], ag.at[3, 0, hi], ag_s.at[2], ag_r.at[2], up)
    send(ag.at[0, 0, lo], ag.at[1, 0, lo], ag_s.at[3], ag_r.at[3], down)
    hidden = (pre * sigma).astype(BF)
    fz_src[...] = hidden.reshape(Q, 32, HS)
    to_z(fz_src, fz_rcv, fz_s, fz_r)
    gst[:, 0] = dot(dt[...], hidden).astype(BF).reshape(Q, PIECE, HS)

    slots = {0: 1, 1: 2, 3: 3, 2: 4}

    def lower(dh, dc):
        grad = dot(xt[...], ag[dh, dc]).astype(BF).reshape(4, PIECE, HS)
        cc = c if dc == 0 else 1 - c
        gst[pl.ds(cc * 4, 4), slots[dh]] = grad

    def scatter(n):
        span = pl.ds(*SETS[n])

        def copy_of(d):
            ww, where = w_peer(d)
            return remote(
                gst.at[ww, span], rw_rcv.at[d - 1, span], rw_s.at[n, d - 1], rw_r.at[n, d - 1], where
            )

        send_each(copy_of)

    def reduce_w(n):
        first, many = SETS[n]
        each(lambda d: landed(rw_rcv.at[d - 1, pl.ds(first, many)], rw_r.at[n, d - 1]))
        for slot in range(first, first + many):
            total = gst[w, slot].astype(F32)
            for d in range(1, Q):
                total = total + rw_rcv[d - 1, slot].astype(F32)
            piece = 8 * n + 3 * (slot - first)
            zsrc[piece:piece + 3] = total.astype(BF).reshape(3, 16, HS)

    def scatter_z(n):
        reduce_w(n)
        zsrc[8 * n + 6:8 * n + 8] = jnp.zeros((2, 16, HS), BF)

        def copy_of(d):
            zz, where = z_peer(d)
            return remote(zsrc.at[8 * n + zz], z_rcv.at[n, d - 1], z_s.at[n, d - 1], z_r.at[n, d - 1], where)

        send_each(copy_of)

    def gather_z(n):
        k = 8 * n + z
        each(lambda d: landed(z_rcv.at[n, d - 1], z_r.at[n, d - 1]))
        total = zsrc[k].astype(F32)
        for d in range(1, Q):
            total = total + z_rcv[n, d - 1].astype(F32)
        zfull[k] = total.astype(BF)

        def copy_of(d):
            return remote(zfull.at[k], zfull.at[k], az_s.at[n, d - 1], az_r.at[n, d - 1], z_peer(d)[1])

        send_each(copy_of)

    def gather_w(n):
        pieces = pl.ds(8 * n, 3 * SETS[n][1])
        if n < 2:
            each(lambda d: landed(zfull.at[8 * n + (z ^ d)], az_r.at[n, d - 1]))

        def copy_of(d):
            return remote(
                zfull.at[pieces], gath.at[w, pieces], aw_s.at[n, d - 1], aw_r.at[n, d - 1], w_peer(d)[1]
            )

        send_each(copy_of)
        pltpu.make_async_copy(zfull.at[pieces], gath.at[w, pieces], out_sem.at[n]).start()

    last = pl.ds(16, 3)

    def exchange_z():
        reduce_w(2)

        def copy_of(d):
            return remote(zsrc.at[last], zc_rcv.at[z], z_s.at[2, d - 1], z_r.at[2, d - 1], z_peer(d)[1])

        send_each(copy_of)
        zc_rcv[z] = zsrc[16:19]

    def sum_z():
        from_z(zc_rcv, z_r.at[2])
        total = zc_rcv[0].astype(F32)
        for zz in range(1, Q):
            total = total + zc_rcv[zz].astype(F32)
        zfull[16:19] = total.astype(BF)

    lower(0, 0)
    landed(ag.at[0, 1], agf_r.at[0])
    lower(0, 1)
    scatter(0)

    landed(ag.at[3, 0, lo], ag_r.at[0])
    send(ag.at[3, 0, lo], ag.at[2, 0, lo], ag_s.at[4], ag_r.at[4], up)
    landed(ag.at[1, 0, hi], ag_r.at[1])
    send(ag.at[1, 0, hi], ag.at[2, 0, hi], ag_s.at[5], ag_r.at[5], down)
    landed(ag.at[3, 0, hi], ag_r.at[2])
    send(ag.at[3, 0], ag.at[3, 1], agf_s.at[3], agf_r.at[3], partner)
    landed(ag.at[1, 0, lo], ag_r.at[3])
    send(ag.at[1, 0], ag.at[1, 1], agf_s.at[1], agf_r.at[1], partner)
    lower(3, 0)
    lower(1, 0)

    from_z(fz_rcv, fz_r)
    fw_src[...] = dot(perm[...], fz_rcv[...].reshape(TGT, HS)).astype(BF).reshape(Q, 32, HS)
    to_w(fw_src, fw_rcv, fw_s, fw_r)

    scatter_z(0)
    landed(ag.at[3, 1], agf_r.at[3])
    lower(3, 1)
    landed(ag.at[1, 1], agf_r.at[1])
    lower(1, 1)
    scatter(1)
    landed(ag.at[2, 0, lo], ag_r.at[4])
    landed(ag.at[2, 0, hi], ag_r.at[5])
    send(ag.at[2, 0], ag.at[2, 1], agf_s.at[2], agf_r.at[2], partner)
    lower(2, 0)
    gather_z(0)
    landed(ag.at[2, 1], agf_r.at[2])
    lower(2, 1)
    scatter(2)
    scatter_z(1)

    from_w(fw_rcv, fw_r)
    received = fw_rcv[...].reshape(TGT, HS).astype(F32).T.astype(BF)
    h_self = dot(received, seedtally[0]).astype(BF)
    agg_two = (dot(received, seedtally[1]) / K2).astype(BF)
    part = dot(w2c[0:CP], h_self) + dot(w2c[CP:2 * CP], agg_two)
    lst[...] = part[0:LP * 32].astype(BF).reshape(LP, 32, TGT)

    def logit_part(d):
        ff, where = f_peer(d)
        return remote(lst.at[lax.rem(ff, LP)], l_rcv.at[d - 1], l_s.at[d - 1], l_r.at[d - 1], where)

    send_each(logit_part, lambda d: f_peer(d)[0] < LP)

    gather_w(0)
    exchange_z()
    gather_z(1)

    fl = lax.rem(f, LP)

    @pl.when(f < LP)
    def _():
        each(lambda d: landed(l_rcv.at[d - 1], l_r.at[d - 1]))
        total = lst[fl].astype(F32)
        for d in range(1, Q):
            total = total + l_rcv[d - 1].astype(F32)
        ltot[...] = total.astype(BF)
        pltpu.make_async_copy(ltot, lout.at[fl], out_sem.at[3]).start()

    def logit_sum(d):
        return remote(ltot, lout.at[fl], la_s.at[d - 1], la_r.at[d - 1], f_peer(d)[1])

    send_each(logit_sum, lambda d: f < LP)

    gather_w(1)
    sum_z()
    gather_w(2)
    sent()

    def logits_in(d):
        ff = f ^ d
        pl.when(ff < LP)(lambda: landed(lout.at[lax.rem(ff, LP)], la_r.at[d - 1]))

    each(logits_in)

    @pl.when(f < LP)
    def _():
        landed(lout.at[fl], out_sem.at[3])

    for n, (first, many) in enumerate(SETS):
        pieces = pl.ds(8 * n, many * 3)
        each(lambda d: landed(gath.at[w ^ d, pieces], aw_r.at[n, d - 1]))
        landed(gath.at[w, pieces], out_sem.at[n])


def finish_kernel(gath, lout, logits, g1s, g1n, g2s, g2n):
    h = lax.axis_index("feat") // 2
    logits[...] = lout[...].reshape(LP * 32, TGT)[0:C].astype(F32)
    for ww in range(Q):
        cc, k = ww // 4, ww % 4
        mine = gath[ww].reshape(19 * 16, HS).astype(F32)
        out = g2s if ww < 4 else g2n
        count = min(PIECE, C - k * PIECE)
        out[k * PIECE:k * PIECE + count] = mine[0:count]
        out = g1s if k < 2 else g1n
        for first, dh in ((48, 0), (128, 1), (176, 3), (256, 2)):
            col = pl.ds(pl.multiple_of((2 * lax.rem(h + dh, 4) + cc) * HS, HS), HS)
            out[(k % 2) * PIECE:(k % 2 + 1) * PIECE, col] = mine[first:first + PIECE]


def local(
    features, target_ids, near_ids, seed_ids, seed_near, w1_self, w1_neigh, w2_self, w2_neigh, logit_grad
):
    vm = pltpu.VMEM
    dma = pltpu.SemaphoreType.DMA
    vspec = pl.BlockSpec(memory_space=pltpu.VMEM)
    hspec = pl.BlockSpec(memory_space=pltpu.HBM)
    blocks = vm((Q, 32, HS), BF)
    wide = vm((Q, 32, 2 * CP), BF)
    scratch = [
        vm((FSL, ND), BF), vm((K1, TGT), jnp.int32), vm((1, TGT), jnp.int32), vm((1, TGT), jnp.int32),
        vm((K2, TGT), jnp.int32), vm((2 * FSL, HID), BF), vm((C, HS), BF), vm((C, HS), BF), vm((C, TGT), BF),
        vm((3, K1 + 1, 8, TGT), jnp.int32), vm((ND, TGT), BF), vm((ND, TGT), BF), vm((TGT, 2 * FSL), BF),
        vm((2 * FSL, TGT), BF), vm((2, TGT, TGT), BF), vm((CP, TGT), BF), vm((2 * CP, HS), BF), vm((TGT, TGT), BF),
        vm((4, TGT, HS), BF), vm((4, TGT, HS), BF), vm((4, TGT, HS), F32), vm((3, TGT, HS), BF),
        vm((2, 128, HS), BF), vm((2, TGT, HS), BF),
        wide, wide, wide, wide, vm((2 * CP, TGT), BF), vm((TGT, HS), F32),
        blocks, blocks, blocks, blocks,
        vm((4, 2, TGT, HS), BF), vm((Q, 5, PIECE, HS), BF), vm((Q - 1, 5, PIECE, HS), BF),
        vm((19, 16, HS), BF), vm((2, Q - 1, 16, HS), BF), vm((Q, 3, 16, HS), BF), vm((19, 16, HS), BF),
        vm((LP, 32, TGT), BF), vm((Q - 1, 32, TGT), BF), vm((32, TGT), BF),
        dma((10,)), dma((4,)), dma((4,)), dma((4,)), dma((6,)), dma((6,)),
        dma((7,)), dma((7,)), dma((7,)), dma((7,)), dma((7,)), dma((7,)), dma((7,)), dma((7,)),
        dma((6,)), dma((6,)), dma((4,)), dma((4,)),
        dma((3, 7)), dma((3, 7)), dma((3, 7)), dma((3, 7)), dma((3, 7)), dma((3, 7)), dma((3, 7)), dma((3, 7)),
        dma((7,)), dma((7,)), dma((7,)), dma((7,)),
    ]
    gath, lout = pl.pallas_call(
        main_kernel,
        out_shape=(
            jax.ShapeDtypeStruct((Q, 19, 16, HS), BF),
            jax.ShapeDtypeStruct((LP, 32, TGT), BF),
        ),
        in_specs=[hspec] * 10,
        out_specs=(hspec, hspec),
        scratch_shapes=scratch,
        compiler_params=pltpu.CompilerParams(
            collective_id=0, has_side_effects=True, vmem_limit_bytes=62 * 1024 * 1024
        ),
        name="sage_step",
    )(
        features.T, near_ids.T, target_ids.reshape(1, TGT), seed_ids.reshape(1, TGT), seed_near.T,
        w1_self, w1_neigh, w2_self.T, w2_neigh.T, logit_grad.T,
    )
    logits, g1s, g1n, g2s, g2n = pl.pallas_call(
        finish_kernel,
        out_shape=(
            jax.ShapeDtypeStruct((C, TGT), F32),
            jax.ShapeDtypeStruct((FSL, HID), F32),
            jax.ShapeDtypeStruct((FSL, HID), F32),
            jax.ShapeDtypeStruct((C, HS), F32),
            jax.ShapeDtypeStruct((C, HS), F32),
        ),
        in_specs=[vspec, vspec],
        out_specs=(vspec,) * 5,
        compiler_params=pltpu.CompilerParams(vmem_limit_bytes=62 * 1024 * 1024),
        name="finish",
    )(gath, lout)
    return logits.T, g1s, g1n, g2s.T, g2n.T


def solution(mesh):
    return jax.shard_map(
        local,
        mesh=mesh,
        in_specs=(
            P("nodes", "feat"),
            P("nodes"),
            P("nodes", None),
            P("nodes"),
            P("nodes", None),
            P("feat", None),
            P("feat", None),
            P("feat", None),
            P("feat", None),
            P("nodes", None),
        ),
        out_specs=(
            P("nodes", None),
            P("feat", None),
            P("feat", None),
            P("feat", None),
            P("feat", None),
        ),
        check_vma=False,
    )
```

```python
import jax
import jax.numpy as jnp
from jax import lax
from jax.experimental import pallas as pl
from jax.experimental.pallas import tpu as pltpu
from jax.sharding import PartitionSpec as P

BF = jnp.bfloat16
F32 = jnp.float32
MESH = pl.DeviceIdType.MESH

TGT = 256
ND = 1024
FSL = 96
HID = 1024
HS = 128
C = 153
K1 = 25
K2 = 15
CP = 192
LP = 5
Q = 8
PIECE = 48
SETS = ((0, 1), (1, 2), (3, 1))
WIDTHS = (6, 6, 3)


def dot(a, b):
    return jnp.dot(a, b, preferred_element_type=F32)


def dot_dims(a, b, ca, cb):
    return lax.dot_general(a, b, (((ca,), (cb,)), ((), ())), preferred_element_type=F32)


def main_kernel(
    features_hbm, near_hbm, tid_hbm, sid_hbm, snear_hbm,
    w1s_hbm, w1n_hbm, w2s_hbm, w2n_hbm, lg_hbm,
    gath, lout,
    feat_v, near_v, tid_v, sid_v, snear_v, w1_v, w2s_v, w2n_v, lg_v,
    keys, tally, sel, x_v, xt, seedtally, lgp, w2c, perm,
    w1_p, p_own, rs_src, relay_rcv, rs_rcv,
    bw_src, bw_rcv, bz_src, bz_rcv, ew_src, ew_rcv, ez_src, ez_rcv,
    fw_src, fw_rcv, fz_src, fz_rcv,
    ag, gst, gup, rw_rcv, rg_rcv, zsrc, z_rcv, zc_rcv, zfull, lst, l_rcv, ltot,
    in_sem, out_sem, fx_s, fx_r, wx_s, wx_r, rs_s, rs_r, bw_s, bw_r, bz_s, bz_r,
    ew_s, ew_r, ez_s, ez_r, fw_s, fw_r, fz_s, fz_r, ag_s, ag_r,
    rw_s, rw_r, rg_s, rg_r, z_s, z_r, az_s, az_r, aw_s, aw_r, l_s, l_r, la_s, la_r,
):
    node = lax.axis_index("nodes")
    f = lax.axis_index("feat")
    z = node // Q
    w = node % Q
    h = f // 2
    c = f % 2

    def z_peer(d):
        return z ^ d, (node ^ (d * Q), f)

    def w_peer(d):
        return w ^ d, (node ^ d, f)

    def v_peer(d):
        return w ^ d, (node ^ d, f ^ 1)

    def f_peer(d):
        return f ^ d, (node, f ^ d)

    partner = (node, h * 2 + (1 - c))

    up = (node, lax.rem(h + 1, 4) * 2 + c)
    down = (node, lax.rem(h + 3, 4) * 2 + c)

    def each(body):
        for d in range(1, Q):
            body(d)

    loads = [
        pltpu.make_async_copy(src, dst, in_sem.at[n])
        for n, (src, dst) in enumerate(
            (
                (snear_hbm, snear_v),
                (sid_hbm, sid_v),
                (lg_hbm, lg_v),
                (w2s_hbm, w2s_v),
                (w2n_hbm, w2n_v),
                (near_hbm, near_v),
                (tid_hbm, tid_v),
                (features_hbm, feat_v.at[c]),
                (w1s_hbm, w1_v.at[pl.ds(0, FSL)]),
                (w1n_hbm, w1_v.at[pl.ds(FSL, FSL)]),
            )
        )
    ]
    for load in loads:
        load.start()

    barrier = pltpu.get_barrier_semaphore()

    def greet(d):
        for where in (z_peer(d)[1], w_peer(d)[1], f_peer(d)[1], v_peer(d)[1]):
            pl.semaphore_signal(barrier, inc=1, device_id=where, device_id_type=MESH)

    each(greet)

    pending = []

    def remote(src, dst, s_sem, r_sem, where):
        return pltpu.make_async_remote_copy(
            src_ref=src, dst_ref=dst, send_sem=s_sem, recv_sem=r_sem,
            device_id=where, device_id_type=MESH,
        )

    def send(*args):
        copy = remote(*args)
        copy.start()
        pending.append(copy.wait_send)

    def send_each(copy_of, test_of=None):
        def start(d):
            if test_of is None:
                copy_of(d).start()
            else:
                pl.when(test_of(d))(lambda: copy_of(d).start())

        def finish(d):
            if test_of is None:
                copy_of(d).wait_send()
            else:
                pl.when(test_of(d))(lambda: copy_of(d).wait_send())

        each(start)
        pending.append(lambda: each(finish))

    def sent():
        for finish in pending:
            finish()
        pending.clear()

    def landed(ref, r_sem):
        pltpu.make_async_copy(ref, ref, r_sem).wait()

    row = lax.broadcasted_iota(jnp.int32, (8, 128), 0)

    def count(ids, own, low, words, totals_of, ones_of):
        fan = ids.shape[0]
        high = lax.shift_right_logical(ids, low.bit_length() - 1)
        digit = lax.shift_left(jnp.ones_like(ids), (high & 3) * 8)
        tables = [ids & (low - 1)]
        tables += [jnp.where((high >> 2) == g, digit, 0) for g in range(words)]
        for n, table in enumerate(tables):
            for k in range(fan):
                keys[n, k] = jnp.broadcast_to(table[k:k + 1], (8, TGT))
        keys[0, K1] = jnp.broadcast_to(own, (8, TGT))

        def body(step, carry):
            mine = [step * 32 + j * 8 + row for j in range(4)]
            for half in range(2):
                cols = slice(half * 128, half * 128 + 128)
                totals = [[jnp.zeros((8, 128), jnp.int32)] * 4 for _ in range(words)]
                for k in range(fan):
                    theirs = keys[0, k, :, cols]
                    hits = [theirs == m for m in mine]
                    for g in range(words):
                        word = keys[1 + g, k, :, cols]
                        totals[g] = [t + jnp.where(hit, word, 0) for t, hit in zip(totals[g], hits)]
                theirs = keys[0, K1, :, cols]
                for part in range(4 * words):
                    for j in (0, 2):
                        first = part * low + step * 32 + j * 8
                        rows = pl.ds(pl.multiple_of(first, 16), 16)
                        both = [
                            lax.shift_right_logical(totals[part // 4][n], 8 * (part % 4)) & 255
                            for n in (j, j + 1)
                        ]
                        totals_of[rows, cols] = jnp.concatenate(both, axis=0).astype(F32).astype(BF)
                        both = [
                            jnp.where(theirs == mine[n] + part * low, 1.0, 0.0) for n in (j, j + 1)
                        ]
                        ones_of[rows, cols] = jnp.concatenate(both, axis=0).astype(BF)
            return carry

        lax.fori_loop(0, low // 32, body, 0)

    pl.semaphore_wait(barrier, 4 * (Q - 1))
    send(features_hbm, feat_v.at[c], fx_s.at[0], fx_r.at[0], partner)

    def cols_of(dh, cc):
        return pl.ds(pl.multiple_of((lax.rem(h + dh, 4) * 2 + cc) * HS, HS), HS)

    def swap(n):
        return ((n >> 2) & 7) * 32 + (n >> 5) * 4 + (n & 3)

    for n in range(5):
        loads[n].wait()
    for padded, first, given in ((lgp, 0, lg_v), (w2c, 0, w2s_v), (w2c, CP, w2n_v)):
        padded[first:first + CP] = jnp.zeros((CP, padded.shape[1]), BF)
        padded[first:first + C] = given[...]
    count(swap(snear_v[...]), swap(sid_v[...]), 64, 1, seedtally.at[1], seedtally.at[0])
    back = jnp.concatenate(
        [dot_dims(seedtally[0], lgp[...], 1, 1), dot_dims(seedtally[1], lgp[...], 1, 1) / K2], axis=1
    ).astype(BF)
    bw_src[...] = dot(back, w2c[...]).astype(BF).reshape(Q, 32, HS)
    ew_src[...] = back.reshape(Q, 32, 2 * CP)

    def to_w(src, dst, s_sem, r_sem):
        def copy_of(d):
            ww, where = w_peer(d)
            return remote(src.at[ww], dst.at[w], s_sem.at[d - 1], r_sem.at[d - 1], where)

        send_each(copy_of)
        dst[w] = src[w]

    def to_z(src, dst, s_sem, r_sem):
        def copy_of(d):
            zz, where = z_peer(d)
            return remote(src.at[zz], dst.at[z], s_sem.at[d - 1], r_sem.at[d - 1], where)

        send_each(copy_of)
        dst[z] = src[z]

    def from_w(dst, r_sem):
        each(lambda d: landed(dst.at[w ^ d], r_sem.at[d - 1]))

    def from_z(dst, r_sem):
        each(lambda d: landed(dst.at[z ^ d], r_sem.at[d - 1]))

    to_w(bw_src, bw_rcv, bw_s, bw_r)
    loads[8].wait()
    loads[9].wait()
    for place, dh in enumerate((2, 1, 3, 0)):
        send(w1_v.at[:, cols_of(dh, 1 - c)], w1_p.at[place], wx_s.at[place], wx_r.at[place], partner)
    to_w(ew_src, ew_rcv, ew_s, ew_r)

    loads[5].wait()
    loads[6].wait()
    count(near_v[...], tid_v[...], 128, 2, tally, sel)

    loads[7].wait()
    landed(feat_v.at[1 - c], fx_r.at[0])
    both = feat_v[...].reshape(2 * FSL, ND)
    x_self = dot(both, sel[...]).astype(BF)
    agg = (dot(both, tally[...]) / K1).astype(BF)
    for cc in range(2):
        part = slice(cc * FSL, cc * FSL + FSL)
        mine = jnp.concatenate([x_self[part], agg[part]], axis=0)
        xt[cc] = mine
        x_v[cc] = mine.astype(F32).T.astype(BF)

    for place, dh in enumerate((2, 1, 3, 0)):
        landed(w1_p.at[place], wx_r.at[place])
        p_own[place] = dot(x_v[c], w1_v[:, cols_of(dh, c)]) + dot(x_v[1 - c], w1_p[place])

    lo, hi = pl.ds(0, 128), pl.ds(128, 128)
    rs_src[0] = p_own[0].astype(BF)
    send(rs_src.at[0, lo], relay_rcv.at[0], rs_s.at[0], rs_r.at[0], up)
    send(rs_src.at[0, hi], relay_rcv.at[1], rs_s.at[1], rs_r.at[1], down)
    rs_src[1, 128:256] = p_own[1, 128:256].astype(BF)
    send(rs_src.at[1, hi], rs_rcv.at[0, hi], rs_s.at[2], rs_r.at[2], up)
    rs_src[2, 0:128] = p_own[2, 0:128].astype(BF)
    send(rs_src.at[2, lo], rs_rcv.at[1, lo], rs_s.at[3], rs_r.at[3], down)

    a = lax.broadcasted_iota(jnp.int32, (TGT, TGT), 0)
    b = lax.broadcasted_iota(jnp.int32, (TGT, TGT), 1)
    perm[...] = jnp.where(swap(a) == b, 1.0, 0.0).astype(BF)
    from_w(bw_rcv, bw_r)
    bz_src[...] = dot(perm[...], bw_rcv[...].reshape(TGT, HS)).astype(BF).reshape(Q, 32, HS)
    to_z(bz_src, bz_rcv, bz_s, bz_r)
    from_w(ew_rcv, ew_r)
    turned = dot(perm[...], ew_rcv[...].reshape(TGT, 2 * CP)).astype(BF)
    ez_src[...] = turned.reshape(Q, 32, 2 * CP)
    to_z(ez_src, ez_rcv, ez_s, ez_r)

    landed(relay_rcv.at[0], rs_r.at[0])
    rs_src[1, 0:128] = (p_own[1, 0:128] + relay_rcv[0].astype(F32)).astype(BF)
    send(rs_src.at[1, lo], rs_rcv.at[0, lo], rs_s.at[4], rs_r.at[4], up)
    landed(relay_rcv.at[1], rs_r.at[1])
    rs_src[2, 128:256] = (p_own[2, 128:256] + relay_rcv[1].astype(F32)).astype(BF)
    send(rs_src.at[2, hi], rs_rcv.at[1, hi], rs_s.at[5], rs_r.at[5], down)
    from_z(bz_rcv, bz_r)

    pre = p_own[3]
    landed(rs_rcv.at[0, hi], rs_r.at[2])
    landed(rs_rcv.at[1, lo], rs_r.at[3])
    landed(rs_rcv.at[0, lo], rs_r.at[4])
    landed(rs_rcv.at[1, hi], rs_r.at[5])
    pre = pre + rs_rcv[0].astype(F32) + rs_rcv[1].astype(F32)
    sigma = 1.0 / (1.0 + jnp.exp(-pre))
    d_hidden = bz_rcv[...].reshape(TGT, HS).astype(F32)
    ag[0] = (d_hidden * (sigma * (1.0 + pre * (1.0 - sigma)))).astype(BF)
    send(ag.at[0, lo], ag.at[3, lo], ag_s.at[0], ag_r.at[0], up)
    send(ag.at[0, hi], ag.at[1, hi], ag_s.at[1], ag_r.at[1], down)
    send(ag.at[0, hi], ag.at[3, hi], ag_s.at[2], ag_r.at[2], up)
    send(ag.at[0, lo], ag.at[1, lo], ag_s.at[3], ag_r.at[3], down)
    fz_src[...] = (pre * sigma).astype(BF).reshape(Q, 32, HS)
    to_z(fz_src, fz_rcv, fz_s, fz_r)

    slots = {0: 0, 1: 1, 3: 2, 2: 3}

    def lower(dh):
        grad = dot(xt[...].reshape(4 * FSL, TGT), ag[dh])
        gst[:, slots[dh]] = grad.astype(BF).reshape(Q, PIECE, HS)

    def scatter(n):
        span = pl.ds(*SETS[n])

        def copy_of(d):
            ww, where = w_peer(d)
            return remote(
                gst.at[ww, span], rw_rcv.at[d - 1, span], rw_s.at[n, d - 1], rw_r.at[n, d - 1], where
            )

        send_each(copy_of)

    def scatter_upper():
        for kk in range(Q):
            ww, cc = 4 * c + kk // 2, kk % 2
            here = jnp.logical_and(w == ww, c == cc)
            there = jnp.logical_not(here)
            far = remote(
                gup.at[kk], rg_rcv.at[w], rg_s.at[kk], rg_r.at[w], (node - w + ww, 2 * h + cc)
            )
            near = pltpu.make_async_copy(gup.at[kk], rg_rcv.at[w], rg_r.at[w])
            pl.when(there)(far.start)
            pl.when(here)(near.start)
            pending.append(lambda there=there, far=far: pl.when(there)(far.wait_send))

    def reduce_w(n):
        first, many = SETS[n]
        each(lambda d: landed(rw_rcv.at[d - 1, pl.ds(first, many)], rw_r.at[n, d - 1]))
        for slot in range(first, first + many):
            total = gst[w, slot].astype(F32)
            for d in range(1, Q):
                total = total + rw_rcv[d - 1, slot].astype(F32)
            piece = 8 * n + 3 * (slot - first)
            zsrc[piece:piece + 3] = total.astype(BF).reshape(3, 16, HS)
        if n == 0:
            for ww in range(Q):
                landed(rg_rcv.at[ww], rg_r.at[ww])
            total = rg_rcv[0].astype(F32)
            for ww in range(1, Q):
                total = total + rg_rcv[ww].astype(F32)
            zsrc[3:6] = total.astype(BF).reshape(3, 16, HS)

    def scatter_z(n):
        reduce_w(n)
        zsrc[8 * n + 6:8 * n + 8] = jnp.zeros((2, 16, HS), BF)

        def copy_of(d):
            zz, where = z_peer(d)
            return remote(zsrc.at[8 * n + zz], z_rcv.at[n, d - 1], z_s.at[n, d - 1], z_r.at[n, d - 1], where)

        send_each(copy_of)

    def gather_z(n):
        k = 8 * n + z
        each(lambda d: landed(z_rcv.at[n, d - 1], z_r.at[n, d - 1]))
        total = zsrc[k].astype(F32)
        for d in range(1, Q):
            total = total + z_rcv[n, d - 1].astype(F32)
        zfull[k] = total.astype(BF)

        def copy_of(d):
            return remote(zfull.at[k], zfull.at[k], az_s.at[n, d - 1], az_r.at[n, d - 1], z_peer(d)[1])

        send_each(copy_of)

    def gather_w(n):
        pieces = pl.ds(8 * n, WIDTHS[n])
        if n < 2:
            each(lambda d: landed(zfull.at[8 * n + (z ^ d)], az_r.at[n, d - 1]))
        cc, place = w // 4, c * 4 + w % 4

        def copy_of(d):
            return remote(
                zfull.at[pieces], gath.at[place, pieces], aw_s.at[n, d], aw_r.at[n, place],
                (node ^ d, 2 * h + cc),
            )

        send_each(copy_of)
        far = copy_of(0)
        near = pltpu.make_async_copy(zfull.at[pieces], gath.at[place, pieces], aw_r.at[n, place])
        pl.when(c != cc)(far.start)
        pl.when(c == cc)(near.start)
        pending.append(lambda: pl.when(c != cc)(far.wait_send))

    last = pl.ds(16, 3)

    def exchange_z():
        reduce_w(2)

        def copy_of(d):
            return remote(zsrc.at[last], zc_rcv.at[z], z_s.at[2, d - 1], z_r.at[2, d - 1], z_peer(d)[1])

        send_each(copy_of)
        zc_rcv[z] = zsrc[16:19]

    def sum_z():
        from_z(zc_rcv, z_r.at[2])
        total = zc_rcv[0].astype(F32)
        for zz in range(1, Q):
            total = total + zc_rcv[zz].astype(F32)
        zfull[16:19] = total.astype(BF)

    lower(0)
    scatter(0)

    landed(ag.at[3, lo], ag_r.at[0])
    send(ag.at[3, lo], ag.at[2, lo], ag_s.at[4], ag_r.at[4], up)
    landed(ag.at[1, hi], ag_r.at[1])
    send(ag.at[1, hi], ag.at[2, hi], ag_s.at[5], ag_r.at[5], down)

    from_z(ez_rcv, ez_r)
    collected = ez_rcv[...].reshape(TGT, 2 * CP).astype(F32).T.astype(BF)
    gup[...] = dot(collected, fz_src[...].reshape(TGT, HS)).astype(BF).reshape(Q, PIECE, HS)
    scatter_upper()

    landed(ag.at[3, hi], ag_r.at[2])
    lower(3)
    landed(ag.at[1, lo], ag_r.at[3])
    lower(1)
    scatter(1)

    from_z(fz_rcv, fz_r)
    fw_src[...] = dot(perm[...], fz_rcv[...].reshape(TGT, HS)).astype(BF).reshape(Q, 32, HS)
    to_w(fw_src, fw_rcv, fw_s, fw_r)

    landed(ag.at[2, lo], ag_r.at[4])
    landed(ag.at[2, hi], ag_r.at[5])
    lower(2)
    scatter(2)
    scatter_z(0)
    scatter_z(1)

    from_w(fw_rcv, fw_r)
    received = fw_rcv[...].reshape(TGT, HS).astype(F32).T.astype(BF)
    h_self = dot(received, seedtally[0]).astype(BF)
    agg_two = (dot(received, seedtally[1]) / K2).astype(BF)
    part = dot(w2c[0:CP], h_self) + dot(w2c[CP:2 * CP], agg_two)
    lst[...] = part[0:LP * 32].astype(BF).reshape(LP, 32, TGT)

    def logit_part(d):
        ff, where = f_peer(d)
        return remote(lst.at[lax.rem(ff, LP)], l_rcv.at[d - 1], l_s.at[d - 1], l_r.at[d - 1], where)

    send_each(logit_part, lambda d: f_peer(d)[0] < LP)

    exchange_z()
    gather_z(0)
    gather_z(1)

    fl = lax.rem(f, LP)

    @pl.when(f < LP)
    def _():
        each(lambda d: landed(l_rcv.at[d - 1], l_r.at[d - 1]))
        total = lst[fl].astype(F32)
        for d in range(1, Q):
            total = total + l_rcv[d - 1].astype(F32)
        ltot[...] = total.astype(BF)
        pltpu.make_async_copy(ltot, lout.at[fl], out_sem.at[3]).start()

    def logit_sum(d):
        return remote(ltot, lout.at[fl], la_s.at[d - 1], la_r.at[d - 1], f_peer(d)[1])

    send_each(logit_sum, lambda d: f < LP)

    gather_w(0)
    gather_w(1)
    sum_z()
    gather_w(2)
    sent()

    def logits_in(d):
        ff = f ^ d
        pl.when(ff < LP)(lambda: landed(lout.at[lax.rem(ff, LP)], la_r.at[d - 1]))

    each(logits_in)

    @pl.when(f < LP)
    def _():
        landed(lout.at[fl], out_sem.at[3])

    for n in range(3):
        for place in range(Q):
            landed(gath.at[place, pl.ds(8 * n, WIDTHS[n])], aw_r.at[n, place])


def finish_kernel(gath, lout, logits, g1s, g1n, g2s, g2n):
    h = lax.axis_index("feat") // 2
    logits[...] = lout[...].reshape(LP * 32, TGT)[0:C].astype(F32)
    for place in range(Q):
        cc, k = place // 4, place % 4
        mine = gath[place].reshape(19 * 16, HS).astype(F32)
        out = g1s if k < 2 else g1n
        for first, dh in ((0, 0), (128, 1), (176, 3), (256, 2)):
            col = pl.ds(pl.multiple_of((2 * lax.rem(h + dh, 4) + cc) * HS, HS), HS)
            out[(k % 2) * PIECE:(k % 2 + 1) * PIECE, col] = mine[first:first + PIECE]
        kk = 2 * k + cc
        out = g2s if kk < 4 else g2n
        first = (kk % 4) * PIECE
        count = min(PIECE, C - first)
        out[first:first + count] = mine[PIECE:PIECE + count]


def local(
    features, target_ids, near_ids, seed_ids, seed_near, w1_self, w1_neigh, w2_self, w2_neigh, logit_grad
):
    vm = pltpu.VMEM
    dma = pltpu.SemaphoreType.DMA
    vspec = pl.BlockSpec(memory_space=pltpu.VMEM)
    hspec = pl.BlockSpec(memory_space=pltpu.HBM)
    blocks = vm((Q, 32, HS), BF)
    wide = vm((Q, 32, 2 * CP), BF)
    scratch = [
        vm((2, FSL, ND), BF), vm((K1, TGT), jnp.int32), vm((1, TGT), jnp.int32), vm((1, TGT), jnp.int32),
        vm((K2, TGT), jnp.int32), vm((2 * FSL, HID), BF), vm((C, HS), BF), vm((C, HS), BF), vm((C, TGT), BF),
        vm((3, K1 + 1, 8, TGT), jnp.int32), vm((ND, TGT), BF), vm((ND, TGT), BF), vm((2, TGT, 2 * FSL), BF),
        vm((2, 2 * FSL, TGT), BF), vm((2, TGT, TGT), BF), vm((CP, TGT), BF), vm((2 * CP, HS), BF),
        vm((TGT, TGT), BF),
        vm((4, 2 * FSL, HS), BF), vm((4, TGT, HS), F32), vm((3, TGT, HS), BF),
        vm((2, 128, HS), BF), vm((2, TGT, HS), BF),
        blocks, blocks, blocks, blocks, wide, wide, wide, wide,
        blocks, blocks, blocks, blocks,
        vm((4, TGT, HS), BF), vm((Q, 4, PIECE, HS), BF), vm((Q, PIECE, HS), BF),
        vm((Q - 1, 4, PIECE, HS), BF), vm((Q, PIECE, HS), BF),
        vm((19, 16, HS), BF), vm((2, Q - 1, 16, HS), BF), vm((Q, 3, 16, HS), BF), vm((19, 16, HS), BF),
        vm((LP, 32, TGT), BF), vm((Q - 1, 32, TGT), BF), vm((32, TGT), BF),
        dma((10,)), dma((4,)), dma((1,)), dma((1,)), dma((4,)), dma((4,)), dma((6,)), dma((6,)),
        dma((7,)), dma((7,)), dma((7,)), dma((7,)), dma((7,)), dma((7,)), dma((7,)), dma((7,)),
        dma((7,)), dma((7,)), dma((7,)), dma((7,)), dma((6,)), dma((6,)),
        dma((3, 7)), dma((3, 7)), dma((8,)), dma((8,)), dma((3, 7)), dma((3, 7)), dma((3, 7)), dma((3, 7)),
        dma((3, 8)), dma((3, 8)), dma((7,)), dma((7,)), dma((7,)), dma((7,)),
    ]
    gath, lout = pl.pallas_call(
        main_kernel,
        out_shape=(
            jax.ShapeDtypeStruct((Q, 19, 16, HS), BF),
            jax.ShapeDtypeStruct((LP, 32, TGT), BF),
        ),
        in_specs=[hspec] * 10,
        out_specs=(hspec, hspec),
        scratch_shapes=scratch,
        compiler_params=pltpu.CompilerParams(
            collective_id=0, has_side_effects=True, vmem_limit_bytes=62 * 1024 * 1024
        ),
        name="sage_step",
    )(
        features.T, near_ids.T, target_ids.reshape(1, TGT), seed_ids.reshape(1, TGT), seed_near.T,
        w1_self, w1_neigh, w2_self.T, w2_neigh.T, logit_grad.T,
    )
    logits, g1s, g1n, g2s, g2n = pl.pallas_call(
        finish_kernel,
        out_shape=(
            jax.ShapeDtypeStruct((C, TGT), F32),
            jax.ShapeDtypeStruct((FSL, HID), F32),
            jax.ShapeDtypeStruct((FSL, HID), F32),
            jax.ShapeDtypeStruct((C, HS), F32),
            jax.ShapeDtypeStruct((C, HS), F32),
        ),
        in_specs=[vspec, vspec],
        out_specs=(vspec,) * 5,
        compiler_params=pltpu.CompilerParams(vmem_limit_bytes=62 * 1024 * 1024),
        name="finish",
    )(gath, lout)
    return logits.T, g1s, g1n, g2s.T, g2n.T


def solution(mesh):
    return jax.shard_map(
        local,
        mesh=mesh,
        in_specs=(
            P("nodes", "feat"),
            P("nodes"),
            P("nodes", None),
            P("nodes"),
            P("nodes", None),
            P("feat", None),
            P("feat", None),
            P("feat", None),
            P("feat", None),
            P("nodes", None),
        ),
        out_specs=(
            P("nodes", None),
            P("feat", None),
            P("feat", None),
            P("feat", None),
            P("feat", None),
        ),
        check_vma=False,
    )
```

```python
import jax
import jax.numpy as jnp
from jax import lax
from jax.experimental import pallas as pl
from jax.experimental.pallas import tpu as pltpu
from jax.sharding import PartitionSpec as P

BF = jnp.bfloat16
F32 = jnp.float32
MESH = pl.DeviceIdType.MESH

TGT = 256
ND = 1024
FSL = 96
HID = 1024
HS = 128
C = 153
K1 = 25
K2 = 15
CP = 192
LR = 80
Q = 8
PIECE = 48
SETS = ((0, 1), (1, 2), (3, 1))
WIDTHS = (6, 6, 3)


def dot(a, b):
    return jnp.dot(a, b, preferred_element_type=F32)


def dot_dims(a, b, ca, cb):
    return lax.dot_general(a, b, (((ca,), (cb,)), ((), ())), preferred_element_type=F32)


def main_kernel(
    features_hbm, near_hbm, tid_hbm, sid_hbm, snear_hbm,
    w1s_hbm, w1n_hbm, w2s_hbm, w2n_hbm, lg_hbm,
    gath, lout,
    feat_v, near_v, tid_v, sid_v, snear_v, w1_v, w2s_v, w2n_v, lg_v,
    keys, tally, sel, x_v, xt, seedtally, lgp, w2c, perm,
    w1_p, p_own, rs_src, relay_rcv, rs_rcv,
    bw_src, bw_rcv, bz_src, bz_rcv, ew_src, ew_rcv, ez_src, ez_rcv,
    fw_src, fw_rcv, fz_src, fz_rcv,
    ag, gst, gup, rw_rcv, rg_rcv, zsrc, z_rcv, zc_rcv, zfull, lst, l_rcv, l_chip, ltot,
    in_sem, out_sem, fx_s, fx_r, wx_s, wx_r, rs_s, rs_r, bw_s, bw_r, bz_s, bz_r,
    ew_s, ew_r, ez_s, ez_r, fw_s, fw_r, fz_s, fz_r, ag_s, ag_r,
    rw_s, rw_r, rg_s, rg_r, z_s, z_r, az_s, az_r, aw_s, aw_r, l_s, l_r,
):
    node = lax.axis_index("nodes")
    f = lax.axis_index("feat")
    z = node // Q
    w = node % Q
    h = f // 2
    c = f % 2

    def z_peer(d):
        return z ^ d, (node ^ (d * Q), f)

    def w_peer(d):
        return w ^ d, (node ^ d, f)

    def v_peer(d):
        return w ^ d, (node ^ d, f ^ 1)

    partner = (node, h * 2 + (1 - c))

    up = (node, lax.rem(h + 1, 4) * 2 + c)
    down = (node, lax.rem(h + 3, 4) * 2 + c)
    across = (node, lax.rem(h + 2, 4) * 2 + c)

    def each(body):
        for d in range(1, Q):
            body(d)

    loads = [
        pltpu.make_async_copy(src, dst, in_sem.at[n])
        for n, (src, dst) in enumerate(
            (
                (snear_hbm, snear_v),
                (sid_hbm, sid_v),
                (lg_hbm, lg_v),
                (w2s_hbm, w2s_v),
                (w2n_hbm, w2n_v),
                (near_hbm, near_v),
                (tid_hbm, tid_v),
                (features_hbm, feat_v.at[c]),
                (w1s_hbm, w1_v.at[pl.ds(0, FSL)]),
                (w1n_hbm, w1_v.at[pl.ds(FSL, FSL)]),
            )
        )
    ]
    for load in loads:
        load.start()

    barrier = pltpu.get_barrier_semaphore()

    def greet(d):
        for where in (z_peer(d)[1], w_peer(d)[1], v_peer(d)[1]):
            pl.semaphore_signal(barrier, inc=1, device_id=where, device_id_type=MESH)

    each(greet)
    for where in (partner, up, down, across):
        pl.semaphore_signal(barrier, inc=1, device_id=where, device_id_type=MESH)

    pending = []

    def remote(src, dst, s_sem, r_sem, where):
        return pltpu.make_async_remote_copy(
            src_ref=src, dst_ref=dst, send_sem=s_sem, recv_sem=r_sem,
            device_id=where, device_id_type=MESH,
        )

    def send(*args):
        copy = remote(*args)
        copy.start()
        pending.append(copy.wait_send)

    def send_each(copy_of, test_of=None):
        def start(d):
            if test_of is None:
                copy_of(d).start()
            else:
                pl.when(test_of(d))(lambda: copy_of(d).start())

        def finish(d):
            if test_of is None:
                copy_of(d).wait_send()
            else:
                pl.when(test_of(d))(lambda: copy_of(d).wait_send())

        each(start)
        pending.append(lambda: each(finish))

    def sent():
        for finish in pending:
            finish()
        pending.clear()

    def landed(ref, r_sem):
        pltpu.make_async_copy(ref, ref, r_sem).wait()

    row = lax.broadcasted_iota(jnp.int32, (8, 128), 0)

    def count(ids, own, low, words, totals_of, ones_of):
        fan = ids.shape[0]
        high = lax.shift_right_logical(ids, low.bit_length() - 1)
        digit = lax.shift_left(jnp.ones_like(ids), (high & 3) * 8)
        tables = [ids & (low - 1)]
        tables += [jnp.where((high >> 2) == g, digit, 0) for g in range(words)]
        for n, table in enumerate(tables):
            for k in range(fan):
                keys[n, k] = jnp.broadcast_to(table[k:k + 1], (8, TGT))
        keys[0, K1] = jnp.broadcast_to(own, (8, TGT))

        def body(step, carry):
            mine = [step * 32 + j * 8 + row for j in range(4)]
            for half in range(2):
                cols = slice(half * 128, half * 128 + 128)
                totals = [[jnp.zeros((8, 128), jnp.int32)] * 4 for _ in range(words)]
                for k in range(fan):
                    theirs = keys[0, k, :, cols]
                    hits = [theirs == m for m in mine]
                    for g in range(words):
                        word = keys[1 + g, k, :, cols]
                        totals[g] = [t + jnp.where(hit, word, 0) for t, hit in zip(totals[g], hits)]
                theirs = keys[0, K1, :, cols]
                for part in range(4 * words):
                    for j in (0, 2):
                        first = part * low + step * 32 + j * 8
                        rows = pl.ds(pl.multiple_of(first, 16), 16)
                        both = [
                            lax.shift_right_logical(totals[part // 4][n], 8 * (part % 4)) & 255
                            for n in (j, j + 1)
                        ]
                        totals_of[rows, cols] = jnp.concatenate(both, axis=0).astype(F32).astype(BF)
                        both = [
                            jnp.where(theirs == mine[n] + part * low, 1.0, 0.0) for n in (j, j + 1)
                        ]
                        ones_of[rows, cols] = jnp.concatenate(both, axis=0).astype(BF)
            return carry

        lax.fori_loop(0, low // 32, body, 0)

    pl.semaphore_wait(barrier, 3 * (Q - 1) + 4)
    send(features_hbm, feat_v.at[c], fx_s.at[0], fx_r.at[0], partner)

    def cols_of(dh, cc):
        return pl.ds(pl.multiple_of((lax.rem(h + dh, 4) * 2 + cc) * HS, HS), HS)

    def swap(n):
        return ((n >> 2) & 7) * 32 + (n >> 5) * 4 + (n & 3)

    for n in range(5):
        loads[n].wait()
    for padded, first, given in ((lgp, 0, lg_v), (w2c, 0, w2s_v), (w2c, CP, w2n_v)):
        padded[first:first + CP] = jnp.zeros((CP, padded.shape[1]), BF)
        padded[first:first + C] = given[...]
    count(swap(snear_v[...]), swap(sid_v[...]), 64, 1, seedtally.at[1], seedtally.at[0])
    back = jnp.concatenate(
        [dot_dims(seedtally[0], lgp[...], 1, 1), dot_dims(seedtally[1], lgp[...], 1, 1) / K2], axis=1
    ).astype(BF)
    bw_src[...] = dot(back, w2c[...]).astype(BF).reshape(Q, 32, HS)
    ew_src[...] = back.reshape(Q, 32, 2 * CP)

    def to_w(src, dst, s_sem, r_sem):
        def copy_of(d):
            ww, where = w_peer(d)
            return remote(src.at[ww], dst.at[w], s_sem.at[d - 1], r_sem.at[d - 1], where)

        send_each(copy_of)
        dst[w] = src[w]

    def to_z(src, dst, s_sem, r_sem):
        def copy_of(d):
            zz, where = z_peer(d)
            return remote(src.at[zz], dst.at[z], s_sem.at[d - 1], r_sem.at[d - 1], where)

        send_each(copy_of)
        dst[z] = src[z]

    def from_w(dst, r_sem):
        each(lambda d: landed(dst.at[w ^ d], r_sem.at[d - 1]))

    def from_z(dst, r_sem):
        each(lambda d: landed(dst.at[z ^ d], r_sem.at[d - 1]))

    to_w(bw_src, bw_rcv, bw_s, bw_r)
    loads[8].wait()
    loads[9].wait()
    for place, dh in enumerate((2, 1, 3, 0)):
        send(w1_v.at[:, cols_of(dh, 1 - c)], w1_p.at[place], wx_s.at[place], wx_r.at[place], partner)
    to_w(ew_src, ew_rcv, ew_s, ew_r)

    loads[5].wait()
    loads[6].wait()
    count(near_v[...], tid_v[...], 128, 2, tally, sel)

    loads[7].wait()
    landed(feat_v.at[1 - c], fx_r.at[0])
    both = feat_v[...].reshape(2 * FSL, ND)
    x_self = dot(both, sel[...]).astype(BF)
    agg = (dot(both, tally[...]) / K1).astype(BF)
    for cc in range(2):
        part = slice(cc * FSL, cc * FSL + FSL)
        mine = jnp.concatenate([x_self[part], agg[part]], axis=0)
        xt[cc] = mine
        x_v[cc] = mine.astype(F32).T.astype(BF)

    lo, hi = pl.ds(0, 128), pl.ds(128, 128)

    def form(place, dh):
        landed(w1_p.at[place], wx_r.at[place])
        p_own[place] = dot(x_v[c], w1_v[:, cols_of(dh, c)]) + dot(x_v[1 - c], w1_p[place])

    form(0, 2)
    rs_src[0] = p_own[0].astype(BF)
    send(rs_src.at[0, lo], relay_rcv.at[0], rs_s.at[0], rs_r.at[0], up)
    send(rs_src.at[0, hi], relay_rcv.at[1], rs_s.at[1], rs_r.at[1], down)
    form(1, 1)
    rs_src[1, 128:256] = p_own[1, 128:256].astype(BF)
    send(rs_src.at[1, hi], rs_rcv.at[0, hi], rs_s.at[2], rs_r.at[2], up)
    form(2, 3)
    rs_src[2, 0:128] = p_own[2, 0:128].astype(BF)
    send(rs_src.at[2, lo], rs_rcv.at[1, lo], rs_s.at[3], rs_r.at[3], down)
    form(3, 0)

    a = lax.broadcasted_iota(jnp.int32, (TGT, TGT), 0)
    b = lax.broadcasted_iota(jnp.int32, (TGT, TGT), 1)
    perm[...] = jnp.where(swap(a) == b, 1.0, 0.0).astype(BF)
    from_w(bw_rcv, bw_r)
    bz_src[...] = dot(perm[...], bw_rcv[...].reshape(TGT, HS)).astype(BF).reshape(Q, 32, HS)
    to_z(bz_src, bz_rcv, bz_s, bz_r)
    from_w(ew_rcv, ew_r)
    turned = dot(perm[...], ew_rcv[...].reshape(TGT, 2 * CP)).astype(BF)
    ez_src[...] = turned.reshape(Q, 32, 2 * CP)
    to_z(ez_src, ez_rcv, ez_s, ez_r)

    landed(relay_rcv.at[0], rs_r.at[0])
    rs_src[1, 0:128] = (p_own[1, 0:128] + relay_rcv[0].astype(F32)).astype(BF)
    send(rs_src.at[1, lo], rs_rcv.at[0, lo], rs_s.at[4], rs_r.at[4], up)
    landed(relay_rcv.at[1], rs_r.at[1])
    rs_src[2, 128:256] = (p_own[2, 128:256] + relay_rcv[1].astype(F32)).astype(BF)
    send(rs_src.at[2, hi], rs_rcv.at[1, hi], rs_s.at[5], rs_r.at[5], down)
    from_z(bz_rcv, bz_r)

    pre = p_own[3]
    landed(rs_rcv.at[0, hi], rs_r.at[2])
    landed(rs_rcv.at[1, lo], rs_r.at[3])
    landed(rs_rcv.at[0, lo], rs_r.at[4])
    landed(rs_rcv.at[1, hi], rs_r.at[5])
    pre = pre + rs_rcv[0].astype(F32) + rs_rcv[1].astype(F32)
    sigma = 1.0 / (1.0 + jnp.exp(-pre))
    d_hidden = bz_rcv[...].reshape(TGT, HS).astype(F32)
    ag[0] = (d_hidden * (sigma * (1.0 + pre * (1.0 - sigma)))).astype(BF)
    send(ag.at[0, lo], ag.at[3, lo], ag_s.at[0], ag_r.at[0], up)
    send(ag.at[0, hi], ag.at[1, hi], ag_s.at[1], ag_r.at[1], down)
    send(ag.at[0, hi], ag.at[3, hi], ag_s.at[2], ag_r.at[2], up)
    send(ag.at[0, lo], ag.at[1, lo], ag_s.at[3], ag_r.at[3], down)
    fz_src[...] = (pre * sigma).astype(BF).reshape(Q, 32, HS)
    to_z(fz_src, fz_rcv, fz_s, fz_r)

    slots = {0: 0, 1: 1, 3: 2, 2: 3}

    def lower(dh):
        grad = dot(xt[...].reshape(4 * FSL, TGT), ag[dh])
        gst[:, slots[dh]] = grad.astype(BF).reshape(Q, PIECE, HS)

    def scatter(n):
        span = pl.ds(*SETS[n])

        def copy_of(d):
            ww, where = w_peer(d)
            return remote(
                gst.at[ww, span], rw_rcv.at[d - 1, span], rw_s.at[n, d - 1], rw_r.at[n, d - 1], where
            )

        send_each(copy_of)

    def scatter_upper():
        for kk in range(Q):
            ww, cc = 4 * c + kk // 2, kk % 2
            here = jnp.logical_and(w == ww, c == cc)
            there = jnp.logical_not(here)
            far = remote(
                gup.at[kk], rg_rcv.at[w], rg_s.at[kk], rg_r.at[w], (node - w + ww, 2 * h + cc)
            )
            near = pltpu.make_async_copy(gup.at[kk], rg_rcv.at[w], rg_r.at[w])
            pl.when(there)(far.start)
            pl.when(here)(near.start)
            pending.append(lambda there=there, far=far: pl.when(there)(far.wait_send))

    def reduce_w(n):
        first, many = SETS[n]
        each(lambda d: landed(rw_rcv.at[d - 1, pl.ds(first, many)], rw_r.at[n, d - 1]))
        for slot in range(first, first + many):
            total = gst[w, slot].astype(F32)
            for d in range(1, Q):
                total = total + rw_rcv[d - 1, slot].astype(F32)
            piece = 8 * n + 3 * (slot - first)
            zsrc[piece:piece + 3] = total.astype(BF).reshape(3, 16, HS)
        if n == 0:
            for ww in range(Q):
                landed(rg_rcv.at[ww], rg_r.at[ww])
            total = rg_rcv[0].astype(F32)
            for ww in range(1, Q):
                total = total + rg_rcv[ww].astype(F32)
            zsrc[3:6] = total.astype(BF).reshape(3, 16, HS)

    def scatter_z(n):
        reduce_w(n)
        zsrc[8 * n + 6:8 * n + 8] = jnp.zeros((2, 16, HS), BF)

        def copy_of(d):
            zz, where = z_peer(d)
            return remote(zsrc.at[8 * n + zz], z_rcv.at[n, d - 1], z_s.at[n, d - 1], z_r.at[n, d - 1], where)

        send_each(copy_of)

    def gather_z(n):
        k = 8 * n + z
        each(lambda d: landed(z_rcv.at[n, d - 1], z_r.at[n, d - 1]))
        total = zsrc[k].astype(F32)
        for d in range(1, Q):
            total = total + z_rcv[n, d - 1].astype(F32)
        zfull[k] = total.astype(BF)

        def copy_of(d):
            return remote(zfull.at[k], zfull.at[k], az_s.at[n, d - 1], az_r.at[n, d - 1], z_peer(d)[1])

        send_each(copy_of)

    def gather_w(n):
        pieces = pl.ds(8 * n, WIDTHS[n])
        if n < 2:
            each(lambda d: landed(zfull.at[8 * n + (z ^ d)], az_r.at[n, d - 1]))
        cc, place = w // 4, c * 4 + w % 4

        def copy_of(d):
            return remote(
                zfull.at[pieces], gath.at[place, pieces], aw_s.at[n, d], aw_r.at[n, place],
                (node ^ d, 2 * h + cc),
            )

        send_each(copy_of)
        far = copy_of(0)
        near = pltpu.make_async_copy(zfull.at[pieces], gath.at[place, pieces], aw_r.at[n, place])
        pl.when(c != cc)(far.start)
        pl.when(c == cc)(near.start)
        pending.append(lambda: pl.when(c != cc)(far.wait_send))

    last = pl.ds(16, 3)

    def exchange_z():
        reduce_w(2)

        def copy_of(d):
            return remote(zsrc.at[last], zc_rcv.at[z], z_s.at[2, d - 1], z_r.at[2, d - 1], z_peer(d)[1])

        send_each(copy_of)
        zc_rcv[z] = zsrc[16:19]

    def sum_z():
        from_z(zc_rcv, z_r.at[2])
        total = zc_rcv[0].astype(F32)
        for zz in range(1, Q):
            total = total + zc_rcv[zz].astype(F32)
        zfull[16:19] = total.astype(BF)

    lower(0)
    scatter(0)

    landed(ag.at[3, lo], ag_r.at[0])
    send(ag.at[3, lo], ag.at[2, lo], ag_s.at[4], ag_r.at[4], up)
    landed(ag.at[1, hi], ag_r.at[1])
    send(ag.at[1, hi], ag.at[2, hi], ag_s.at[5], ag_r.at[5], down)

    from_z(ez_rcv, ez_r)
    collected = ez_rcv[...].reshape(TGT, 2 * CP).astype(F32).T.astype(BF)
    gup[...] = dot(collected, fz_src[...].reshape(TGT, HS)).astype(BF).reshape(Q, PIECE, HS)
    scatter_upper()

    landed(ag.at[3, hi], ag_r.at[2])
    lower(3)
    landed(ag.at[1, lo], ag_r.at[3])
    lower(1)
    scatter(1)

    from_z(fz_rcv, fz_r)
    fw_src[...] = dot(perm[...], fz_rcv[...].reshape(TGT, HS)).astype(BF).reshape(Q, 32, HS)
    to_w(fw_src, fw_rcv, fw_s, fw_r)

    landed(ag.at[2, lo], ag_r.at[4])
    landed(ag.at[2, hi], ag_r.at[5])
    lower(2)
    scatter(2)
    scatter_z(0)
    scatter_z(1)

    from_w(fw_rcv, fw_r)
    received = fw_rcv[...].reshape(TGT, HS).astype(F32).T.astype(BF)
    h_self = dot(received, seedtally[0]).astype(BF)
    agg_two = (dot(received, seedtally[1]) / K2).astype(BF)
    part = dot(w2c[0:CP], h_self) + dot(w2c[CP:2 * CP], agg_two)
    lst[...] = part[0:2 * LR].astype(BF).reshape(2, LR, TGT)
    send(lst.at[1 - c], l_rcv, l_s.at[0], l_r.at[0], partner)

    exchange_z()
    gather_z(0)
    gather_z(1)

    landed(l_rcv, l_r.at[0])
    l_chip[h] = (lst[c].astype(F32) + l_rcv[...].astype(F32)).astype(BF)
    for n, where in enumerate((up, down, across)):
        send(l_chip.at[h], l_chip.at[h], l_s.at[n + 1], l_r.at[n + 1], where)

    gather_w(0)
    for n, dh in enumerate((3, 1, 2)):
        landed(l_chip.at[lax.rem(h + dh, 4)], l_r.at[n + 1])
    total = l_chip[0].astype(F32)
    for n in range(1, 4):
        total = total + l_chip[n].astype(F32)
    ltot[...] = total.astype(BF)
    send(ltot, lout.at[c], l_s.at[4], l_r.at[4], partner)
    own_logits = pltpu.make_async_copy(ltot, lout.at[c], out_sem.at[3])
    own_logits.start()
    gather_w(1)
    sum_z()
    gather_w(2)
    sent()

    landed(lout.at[1 - c], l_r.at[4])
    own_logits.wait()
    for n in range(3):
        for place in range(Q):
            landed(gath.at[place, pl.ds(8 * n, WIDTHS[n])], aw_r.at[n, place])


def finish_kernel(gath, lout, logits, g1s, g1n, g2s, g2n):
    h = lax.axis_index("feat") // 2
    logits[...] = lout[...].reshape(2 * LR, TGT)[0:C].astype(F32)
    for place in range(Q):
        cc, k = place // 4, place % 4
        mine = gath[place].reshape(19 * 16, HS).astype(F32)
        out = g1s if k < 2 else g1n
        for first, dh in ((0, 0), (128, 1), (176, 3), (256, 2)):
            col = pl.ds(pl.multiple_of((2 * lax.rem(h + dh, 4) + cc) * HS, HS), HS)
            out[(k % 2) * PIECE:(k % 2 + 1) * PIECE, col] = mine[first:first + PIECE]
        kk = 2 * k + cc
        out = g2s if kk < 4 else g2n
        first = (kk % 4) * PIECE
        count = min(PIECE, C - first)
        out[first:first + count] = mine[PIECE:PIECE + count]


def local(
    features, target_ids, near_ids, seed_ids, seed_near, w1_self, w1_neigh, w2_self, w2_neigh, logit_grad
):
    vm = pltpu.VMEM
    dma = pltpu.SemaphoreType.DMA
    vspec = pl.BlockSpec(memory_space=pltpu.VMEM)
    hspec = pl.BlockSpec(memory_space=pltpu.HBM)
    blocks = vm((Q, 32, HS), BF)
    wide = vm((Q, 32, 2 * CP), BF)
    scratch = [
        vm((2, FSL, ND), BF), vm((K1, TGT), jnp.int32), vm((1, TGT), jnp.int32), vm((1, TGT), jnp.int32),
        vm((K2, TGT), jnp.int32), vm((2 * FSL, HID), BF), vm((C, HS), BF), vm((C, HS), BF), vm((C, TGT), BF),
        vm((3, K1 + 1, 8, TGT), jnp.int32), vm((ND, TGT), BF), vm((ND, TGT), BF), vm((2, TGT, 2 * FSL), BF),
        vm((2, 2 * FSL, TGT), BF), vm((2, TGT, TGT), BF), vm((CP, TGT), BF), vm((2 * CP, HS), BF),
        vm((TGT, TGT), BF),
        vm((4, 2 * FSL, HS), BF), vm((4, TGT, HS), F32), vm((3, TGT, HS), BF),
        vm((2, 128, HS), BF), vm((2, TGT, HS), BF),
        blocks, blocks, blocks, blocks, wide, wide, wide, wide,
        blocks, blocks, blocks, blocks,
        vm((4, TGT, HS), BF), vm((Q, 4, PIECE, HS), BF), vm((Q, PIECE, HS), BF),
        vm((Q - 1, 4, PIECE, HS), BF), vm((Q, PIECE, HS), BF),
        vm((19, 16, HS), BF), vm((2, Q - 1, 16, HS), BF), vm((Q, 3, 16, HS), BF), vm((19, 16, HS), BF),
        vm((2, LR, TGT), BF), vm((LR, TGT), BF), vm((4, LR, TGT), BF), vm((LR, TGT), BF),
        dma((10,)), dma((4,)), dma((1,)), dma((1,)), dma((4,)), dma((4,)), dma((6,)), dma((6,)),
        dma((7,)), dma((7,)), dma((7,)), dma((7,)), dma((7,)), dma((7,)), dma((7,)), dma((7,)),
        dma((7,)), dma((7,)), dma((7,)), dma((7,)), dma((6,)), dma((6,)),
        dma((3, 7)), dma((3, 7)), dma((8,)), dma((8,)), dma((3, 7)), dma((3, 7)), dma((3, 7)), dma((3, 7)),
        dma((3, 8)), dma((3, 8)), dma((5,)), dma((5,)),
    ]
    gath, lout = pl.pallas_call(
        main_kernel,
        out_shape=(
            jax.ShapeDtypeStruct((Q, 19, 16, HS), BF),
            jax.ShapeDtypeStruct((2, LR, TGT), BF),
        ),
        in_specs=[hspec] * 10,
        out_specs=(hspec, hspec),
        scratch_shapes=scratch,
        compiler_params=pltpu.CompilerParams(
            collective_id=0, has_side_effects=True, vmem_limit_bytes=62 * 1024 * 1024
        ),
        name="sage_step",
    )(
        features.T, near_ids.T, target_ids.reshape(1, TGT), seed_ids.reshape(1, TGT), seed_near.T,
        w1_self, w1_neigh, w2_self.T, w2_neigh.T, logit_grad.T,
    )
    logits, g1s, g1n, g2s, g2n = pl.pallas_call(
        finish_kernel,
        out_shape=(
            jax.ShapeDtypeStruct((C, TGT), F32),
            jax.ShapeDtypeStruct((FSL, HID), F32),
            jax.ShapeDtypeStruct((FSL, HID), F32),
            jax.ShapeDtypeStruct((C, HS), F32),
            jax.ShapeDtypeStruct((C, HS), F32),
        ),
        in_specs=[vspec, vspec],
        out_specs=(vspec,) * 5,
        compiler_params=pltpu.CompilerParams(vmem_limit_bytes=62 * 1024 * 1024),
        name="finish",
    )(gath, lout)
    return logits.T, g1s, g1n, g2s.T, g2n.T


def solution(mesh):
    return jax.shard_map(
        local,
        mesh=mesh,
        in_specs=(
            P("nodes", "feat"),
            P("nodes"),
            P("nodes", None),
            P("nodes"),
            P("nodes", None),
            P("feat", None),
            P("feat", None),
            P("feat", None),
            P("feat", None),
            P("nodes", None),
        ),
        out_specs=(
            P("nodes", None),
            P("feat", None),
            P("feat", None),
            P("feat", None),
            P("feat", None),
        ),
        check_vma=False,
    )
```

```python
import jax
import jax.numpy as jnp
from jax import lax
from jax.experimental import pallas as pl
from jax.experimental.pallas import tpu as pltpu
from jax.sharding import PartitionSpec as P

BF = jnp.bfloat16
F32 = jnp.float32
MESH = pl.DeviceIdType.MESH

TGT = 256
ND = 1024
FSL = 96
HID = 1024
HS = 128
C = 153
K1 = 25
K2 = 15
CP = 192
LP = 5
Q = 8
PIECE = 48
SETS = ((0, 1), (1, 2), (3, 1))
WIDTHS = (6, 6, 3)


def dot(a, b):
    return jnp.dot(a, b, preferred_element_type=F32)


def dot_dims(a, b, ca, cb):
    return lax.dot_general(a, b, (((ca,), (cb,)), ((), ())), preferred_element_type=F32)


def main_kernel(
    features_hbm, near_hbm, tid_hbm, sid_hbm, snear_hbm,
    w1s_hbm, w1n_hbm, w2s_hbm, w2n_hbm, lg_hbm,
    gath, lout,
    feat_v, near_v, tid_v, sid_v, snear_v, w1_v, w2s_v, w2n_v, lg_v,
    keys, tally, sel, x_v, xt, seedtally, lgp, w2c, perm,
    w1_p, p_own, rs_src, relay_rcv, rs_rcv,
    bw_src, bw_rcv, bz_src, bz_rcv, ew_src, ew_rcv, ez_src, ez_rcv,
    fw_src, fw_rcv, fz_src, fz_rcv,
    ag, gst, gup, rw_rcv, rg_rcv, zsrc, z_rcv, zc_rcv, zfull, lst, l_rcv, ltot,
    in_sem, out_sem, fx_s, fx_r, wx_s, wx_r, rs_s, rs_r, bw_s, bw_r, bz_s, bz_r,
    ew_s, ew_r, ez_s, ez_r, fw_s, fw_r, fz_s, fz_r, ag_s, ag_r,
    rw_s, rw_r, rg_s, rg_r, z_s, z_r, az_s, az_r, aw_s, aw_r, l_s, l_r, la_s, la_r,
):
    node = lax.axis_index("nodes")
    f = lax.axis_index("feat")
    z = node // Q
    w = node % Q
    h = f // 2
    c = f % 2

    def z_peer(d):
        return z ^ d, (node ^ (d * Q), f)

    def w_peer(d):
        return w ^ d, (node ^ d, f)

    def v_peer(d):
        return w ^ d, (node ^ d, f ^ 1)

    def f_peer(d):
        return f ^ d, (node, f ^ d)

    partner = (node, h * 2 + (1 - c))

    up = (node, lax.rem(h + 1, 4) * 2 + c)
    down = (node, lax.rem(h + 3, 4) * 2 + c)

    def each(body):
        for d in range(1, Q):
            body(d)

    loads = [
        pltpu.make_async_copy(src, dst, in_sem.at[n])
        for n, (src, dst) in enumerate(
            (
                (snear_hbm, snear_v),
                (sid_hbm, sid_v),
                (lg_hbm, lg_v),
                (w2s_hbm, w2s_v),
                (w2n_hbm, w2n_v),
                (near_hbm, near_v),
                (tid_hbm, tid_v),
                (features_hbm, feat_v.at[c]),
                (w1s_hbm, w1_v.at[pl.ds(0, FSL)]),
                (w1n_hbm, w1_v.at[pl.ds(FSL, FSL)]),
            )
        )
    ]
    for load in loads:
        load.start()

    barrier = pltpu.get_barrier_semaphore()

    def greet(d):
        for where in (z_peer(d)[1], w_peer(d)[1], f_peer(d)[1], v_peer(d)[1]):
            pl.semaphore_signal(barrier, inc=1, device_id=where, device_id_type=MESH)

    each(greet)

    pending = []

    def remote(src, dst, s_sem, r_sem, where):
        return pltpu.make_async_remote_copy(
            src_ref=src, dst_ref=dst, send_sem=s_sem, recv_sem=r_sem,
            device_id=where, device_id_type=MESH,
        )

    def send(*args):
        copy = remote(*args)
        copy.start()
        pending.append(copy.wait_send)

    def send_each(copy_of, test_of=None):
        def start(d):
            if test_of is None:
                copy_of(d).start()
            else:
                pl.when(test_of(d))(lambda: copy_of(d).start())

        def finish(d):
            if test_of is None:
                copy_of(d).wait_send()
            else:
                pl.when(test_of(d))(lambda: copy_of(d).wait_send())

        each(start)
        pending.append(lambda: each(finish))

    def sent():
        for finish in pending:
            finish()
        pending.clear()

    def landed(ref, r_sem):
        pltpu.make_async_copy(ref, ref, r_sem).wait()

    row = lax.broadcasted_iota(jnp.int32, (8, 128), 0)

    def count(ids, own, low, words, totals_of, ones_of):
        fan = ids.shape[0]
        high = lax.shift_right_logical(ids, low.bit_length() - 1)
        digit = lax.shift_left(jnp.ones_like(ids), (high & 3) * 8)
        tables = [ids & (low - 1)]
        tables += [jnp.where((high >> 2) == g, digit, 0) for g in range(words)]
        for n, table in enumerate(tables):
            for k in range(fan):
                keys[n, k] = jnp.broadcast_to(table[k:k + 1], (8, TGT))
        keys[0, K1] = jnp.broadcast_to(own, (8, TGT))

        def body(step, carry):
            mine = [step * 32 + j * 8 + row for j in range(4)]
            for half in range(2):
                cols = slice(half * 128, half * 128 + 128)
                totals = [[jnp.zeros((8, 128), jnp.int32)] * 4 for _ in range(words)]
                for k in range(fan):
                    theirs = keys[0, k, :, cols]
                    hits = [theirs == m for m in mine]
                    for g in range(words):
                        word = keys[1 + g, k, :, cols]
                        totals[g] = [t + jnp.where(hit, word, 0) for t, hit in zip(totals[g], hits)]
                theirs = keys[0, K1, :, cols]
                for part in range(4 * words):
                    for j in (0, 2):
                        first = part * low + step * 32 + j * 8
                        rows = pl.ds(pl.multiple_of(first, 16), 16)
                        both = [
                            lax.shift_right_logical(totals[part // 4][n], 8 * (part % 4)) & 255
                            for n in (j, j + 1)
                        ]
                        totals_of[rows, cols] = jnp.concatenate(both, axis=0).astype(F32).astype(BF)
                        both = [
                            jnp.where(theirs == mine[n] + part * low, 1.0, 0.0) for n in (j, j + 1)
                        ]
                        ones_of[rows, cols] = jnp.concatenate(both, axis=0).astype(BF)
            return carry

        lax.fori_loop(0, low // 32, body, 0)

    pl.semaphore_wait(barrier, 4 * (Q - 1))
    send(features_hbm, feat_v.at[c], fx_s.at[0], fx_r.at[0], partner)

    def cols_of(dh, cc):
        return pl.ds(pl.multiple_of((lax.rem(h + dh, 4) * 2 + cc) * HS, HS), HS)

    def swap(n):
        return ((n >> 2) & 7) * 32 + (n >> 5) * 4 + (n & 3)

    for n in range(5):
        loads[n].wait()
    for padded, first, given in ((lgp, 0, lg_v), (w2c, 0, w2s_v), (w2c, CP, w2n_v)):
        padded[first:first + CP] = jnp.zeros((CP, padded.shape[1]), BF)
        padded[first:first + C] = given[...]
    count(swap(snear_v[...]), swap(sid_v[...]), 64, 1, seedtally.at[1], seedtally.at[0])
    back = jnp.concatenate(
        [dot_dims(seedtally[0], lgp[...], 1, 1), dot_dims(seedtally[1], lgp[...], 1, 1) / K2], axis=1
    ).astype(BF)
    bw_src[...] = dot(back, w2c[...]).astype(BF).reshape(Q, 32, HS)
    ew_src[...] = back.reshape(Q, 32, 2 * CP)

    def to_w(src, dst, s_sem, r_sem):
        def copy_of(d):
            ww, where = w_peer(d)
            return remote(src.at[ww], dst.at[w], s_sem.at[d - 1], r_sem.at[d - 1], where)

        send_each(copy_of)
        dst[w] = src[w]

    def to_z(src, dst, s_sem, r_sem):
        def copy_of(d):
            zz, where = z_peer(d)
            return remote(src.at[zz], dst.at[z], s_sem.at[d - 1], r_sem.at[d - 1], where)

        send_each(copy_of)
        dst[z] = src[z]

    def from_w(dst, r_sem):
        each(lambda d: landed(dst.at[w ^ d], r_sem.at[d - 1]))

    def from_z(dst, r_sem):
        each(lambda d: landed(dst.at[z ^ d], r_sem.at[d - 1]))

    to_w(bw_src, bw_rcv, bw_s, bw_r)
    loads[8].wait()
    loads[9].wait()
    for place, dh in enumerate((2, 1, 3, 0)):
        send(w1_v.at[:, cols_of(dh, 1 - c)], w1_p.at[place], wx_s.at[place], wx_r.at[place], partner)
    to_w(ew_src, ew_rcv, ew_s, ew_r)

    loads[5].wait()
    loads[6].wait()
    count(near_v[...], tid_v[...], 128, 2, tally, sel)

    loads[7].wait()
    landed(feat_v.at[1 - c], fx_r.at[0])
    both = feat_v[...].reshape(2 * FSL, ND)
    x_self = dot(both, sel[...]).astype(BF)
    agg = (dot(both, tally[...]) / K1).astype(BF)
    for cc in range(2):
        part = slice(cc * FSL, cc * FSL + FSL)
        mine = jnp.concatenate([x_self[part], agg[part]], axis=0)
        xt[cc] = mine
        x_v[cc] = mine.astype(F32).T.astype(BF)

    lo, hi = pl.ds(0, 128), pl.ds(128, 128)

    def form(place, dh):
        landed(w1_p.at[place], wx_r.at[place])
        p_own[place] = dot(x_v[c], w1_v[:, cols_of(dh, c)]) + dot(x_v[1 - c], w1_p[place])

    form(0, 2)
    rs_src[0] = p_own[0].astype(BF)
    send(rs_src.at[0, lo], relay_rcv.at[0], rs_s.at[0], rs_r.at[0], up)
    send(rs_src.at[0, hi], relay_rcv.at[1], rs_s.at[1], rs_r.at[1], down)
    form(1, 1)
    rs_src[1, 128:256] = p_own[1, 128:256].astype(BF)
    send(rs_src.at[1, hi], rs_rcv.at[0, hi], rs_s.at[2], rs_r.at[2], up)
    form(2, 3)
    rs_src[2, 0:128] = p_own[2, 0:128].astype(BF)
    send(rs_src.at[2, lo], rs_rcv.at[1, lo], rs_s.at[3], rs_r.at[3], down)
    form(3, 0)

    a = lax.broadcasted_iota(jnp.int32, (TGT, TGT), 0)
    b = lax.broadcasted_iota(jnp.int32, (TGT, TGT), 1)
    perm[...] = jnp.where(swap(a) == b, 1.0, 0.0).astype(BF)
    from_w(bw_rcv, bw_r)
    bz_src[...] = dot(perm[...], bw_rcv[...].reshape(TGT, HS)).astype(BF).reshape(Q, 32, HS)
    to_z(bz_src, bz_rcv, bz_s, bz_r)
    from_w(ew_rcv, ew_r)
    turned = dot(perm[...], ew_rcv[...].reshape(TGT, 2 * CP)).astype(BF)
    ez_src[...] = turned.reshape(Q, 32, 2 * CP)
    to_z(ez_src, ez_rcv, ez_s, ez_r)

    landed(relay_rcv.at[0], rs_r.at[0])
    rs_src[1, 0:128] = (p_own[1, 0:128] + relay_rcv[0].astype(F32)).astype(BF)
    send(rs_src.at[1, lo], rs_rcv.at[0, lo], rs_s.at[4], rs_r.at[4], up)
    landed(relay_rcv.at[1], rs_r.at[1])
    rs_src[2, 128:256] = (p_own[2, 128:256] + relay_rcv[1].astype(F32)).astype(BF)
    send(rs_src.at[2, hi], rs_rcv.at[1, hi], rs_s.at[5], rs_r.at[5], down)
    from_z(bz_rcv, bz_r)

    pre = p_own[3]
    landed(rs_rcv.at[0, hi], rs_r.at[2])
    landed(rs_rcv.at[1, lo], rs_r.at[3])
    landed(rs_rcv.at[0, lo], rs_r.at[4])
    landed(rs_rcv.at[1, hi], rs_r.at[5])
    pre = pre + rs_rcv[0].astype(F32) + rs_rcv[1].astype(F32)
    sigma = 1.0 / (1.0 + jnp.exp(-pre))
    d_hidden = bz_rcv[...].reshape(TGT, HS).astype(F32)
    ag[0] = (d_hidden * (sigma * (1.0 + pre * (1.0 - sigma)))).astype(BF)
    send(ag.at[0, lo], ag.at[3, lo], ag_s.at[0], ag_r.at[0], up)
    send(ag.at[0, hi], ag.at[1, hi], ag_s.at[1], ag_r.at[1], down)
    send(ag.at[0, hi], ag.at[3, hi], ag_s.at[2], ag_r.at[2], up)
    send(ag.at[0, lo], ag.at[1, lo], ag_s.at[3], ag_r.at[3], down)
    fz_src[...] = (pre * sigma).astype(BF).reshape(Q, 32, HS)
    to_z(fz_src, fz_rcv, fz_s, fz_r)

    slots = {0: 0, 1: 1, 3: 2, 2: 3}

    def lower(dh):
        grad = dot(xt[...].reshape(4 * FSL, TGT), ag[dh])
        gst[:, slots[dh]] = grad.astype(BF).reshape(Q, PIECE, HS)

    def scatter(n):
        span = pl.ds(*SETS[n])

        def copy_of(d):
            ww, where = w_peer(d)
            return remote(
                gst.at[ww, span], rw_rcv.at[d - 1, span], rw_s.at[n, d - 1], rw_r.at[n, d - 1], where
            )

        send_each(copy_of)

    def scatter_upper():
        for kk in range(Q):
            ww, cc = 4 * c + kk // 2, kk % 2
            here = jnp.logical_and(w == ww, c == cc)
            there = jnp.logical_not(here)
            far = remote(
                gup.at[kk], rg_rcv.at[w], rg_s.at[kk], rg_r.at[w], (node - w + ww, 2 * h + cc)
            )
            near = pltpu.make_async_copy(gup.at[kk], rg_rcv.at[w], rg_r.at[w])
            pl.when(there)(far.start)
            pl.when(here)(near.start)
            pending.append(lambda there=there, far=far: pl.when(there)(far.wait_send))

    def reduce_w(n):
        first, many = SETS[n]
        each(lambda d: landed(rw_rcv.at[d - 1, pl.ds(first, many)], rw_r.at[n, d - 1]))
        for slot in range(first, first + many):
            total = gst[w, slot].astype(F32)
            for d in range(1, Q):
                total = total + rw_rcv[d - 1, slot].astype(F32)
            piece = 8 * n + 3 * (slot - first)
            zsrc[piece:piece + 3] = total.astype(BF).reshape(3, 16, HS)
        if n == 0:
            for ww in range(Q):
                landed(rg_rcv.at[ww], rg_r.at[ww])
            total = rg_rcv[0].astype(F32)
            for ww in range(1, Q):
                total = total + rg_rcv[ww].astype(F32)
            zsrc[3:6] = total.astype(BF).reshape(3, 16, HS)

    def scatter_z(n):
        reduce_w(n)
        zsrc[8 * n + 6:8 * n + 8] = jnp.zeros((2, 16, HS), BF)

        def copy_of(d):
            zz, where = z_peer(d)
            return remote(zsrc.at[8 * n + zz], z_rcv.at[n, d - 1], z_s.at[n, d - 1], z_r.at[n, d - 1], where)

        send_each(copy_of)

    def gather_z(n):
        k = 8 * n + z
        each(lambda d: landed(z_rcv.at[n, d - 1], z_r.at[n, d - 1]))
        total = zsrc[k].astype(F32)
        for d in range(1, Q):
            total = total + z_rcv[n, d - 1].astype(F32)
        zfull[k] = total.astype(BF)

        def copy_of(d):
            return remote(zfull.at[k], zfull.at[k], az_s.at[n, d - 1], az_r.at[n, d - 1], z_peer(d)[1])

        send_each(copy_of)

    def gather_w(n):
        pieces = pl.ds(8 * n, WIDTHS[n])
        if n < 2:
            each(lambda d: landed(zfull.at[8 * n + (z ^ d)], az_r.at[n, d - 1]))
        cc, place = w // 4, c * 4 + w % 4

        def copy_of(d):
            return remote(
                zfull.at[pieces], gath.at[place, pieces], aw_s.at[n, d], aw_r.at[n, place],
                (node ^ d, 2 * h + cc),
            )

        send_each(copy_of)
        far = copy_of(0)
        near = pltpu.make_async_copy(zfull.at[pieces], gath.at[place, pieces], aw_r.at[n, place])
        pl.when(c != cc)(far.start)
        pl.when(c == cc)(near.start)
        pending.append(lambda: pl.when(c != cc)(far.wait_send))

    last = pl.ds(16, 3)

    def exchange_z():
        reduce_w(2)

        def copy_of(d):
            return remote(zsrc.at[last], zc_rcv.at[z], z_s.at[2, d - 1], z_r.at[2, d - 1], z_peer(d)[1])

        send_each(copy_of)
        zc_rcv[z] = zsrc[16:19]

    def sum_z():
        from_z(zc_rcv, z_r.at[2])
        total = zc_rcv[0].astype(F32)
        for zz in range(1, Q):
            total = total + zc_rcv[zz].astype(F32)
        zfull[16:19] = total.astype(BF)

    lower(0)
    scatter(0)

    landed(ag.at[3, lo], ag_r.at[0])
    send(ag.at[3, lo], ag.at[2, lo], ag_s.at[4], ag_r.at[4], up)
    landed(ag.at[1, hi], ag_r.at[1])
    send(ag.at[1, hi], ag.at[2, hi], ag_s.at[5], ag_r.at[5], down)

    landed(ag.at[3, hi], ag_r.at[2])
    lower(3)
    landed(ag.at[1, lo], ag_r.at[3])
    lower(1)
    scatter(1)

    from_z(fz_rcv, fz_r)
    fw_src[...] = dot(perm[...], fz_rcv[...].reshape(TGT, HS)).astype(BF).reshape(Q, 32, HS)
    to_w(fw_src, fw_rcv, fw_s, fw_r)

    from_z(ez_rcv, ez_r)
    collected = ez_rcv[...].reshape(TGT, 2 * CP).astype(F32).T.astype(BF)
    gup[...] = dot(collected, fz_src[...].reshape(TGT, HS)).astype(BF).reshape(Q, PIECE, HS)
    scatter_upper()

    landed(ag.at[2, lo], ag_r.at[4])
    landed(ag.at[2, hi], ag_r.at[5])
    lower(2)
    scatter(2)

    from_w(fw_rcv, fw_r)
    received = fw_rcv[...].reshape(TGT, HS).astype(F32).T.astype(BF)
    h_self = dot(received, seedtally[0]).astype(BF)
    agg_two = (dot(received, seedtally[1]) / K2).astype(BF)
    part = dot(w2c[0:CP], h_self) + dot(w2c[CP:2 * CP], agg_two)
    lst[...] = part[0:LP * 32].astype(BF).reshape(LP, 32, TGT)

    def logit_part(d):
        ff, where = f_peer(d)
        return remote(lst.at[lax.rem(ff, LP)], l_rcv.at[d - 1], l_s.at[d - 1], l_r.at[d - 1], where)

    send_each(logit_part, lambda d: f_peer(d)[0] < LP)

    scatter_z(1)
    scatter_z(0)
    exchange_z()
    gather_z(1)
    gather_z(0)

    fl = lax.rem(f, LP)

    @pl.when(f < LP)
    def _():
        each(lambda d: landed(l_rcv.at[d - 1], l_r.at[d - 1]))
        total = lst[fl].astype(F32)
        for d in range(1, Q):
            total = total + l_rcv[d - 1].astype(F32)
        ltot[...] = total.astype(BF)
        pltpu.make_async_copy(ltot, lout.at[fl], out_sem.at[3]).start()

    def logit_sum(d):
        return remote(ltot, lout.at[fl], la_s.at[d - 1], la_r.at[d - 1], f_peer(d)[1])

    send_each(logit_sum, lambda d: f < LP)

    gather_w(1)
    gather_w(0)
    sum_z()
    gather_w(2)
    sent()

    def logits_in(d):
        ff = f ^ d
        pl.when(ff < LP)(lambda: landed(lout.at[lax.rem(ff, LP)], la_r.at[d - 1]))

    each(logits_in)

    @pl.when(f < LP)
    def _():
        landed(lout.at[fl], out_sem.at[3])

    for n in range(3):
        for place in range(Q):
            landed(gath.at[place, pl.ds(8 * n, WIDTHS[n])], aw_r.at[n, place])


def finish_kernel(gath, lout, logits, g1s, g1n, g2s, g2n):
    h = lax.axis_index("feat") // 2
    logits[...] = lout[...].reshape(LP * 32, TGT)[0:C].astype(F32)
    for place in range(Q):
        cc, k = place // 4, place % 4
        mine = gath[place].reshape(19 * 16, HS).astype(F32)
        out = g1s if k < 2 else g1n
        for first, dh in ((0, 0), (128, 1), (176, 3), (256, 2)):
            col = pl.ds(pl.multiple_of((2 * lax.rem(h + dh, 4) + cc) * HS, HS), HS)
            out[(k % 2) * PIECE:(k % 2 + 1) * PIECE, col] = mine[first:first + PIECE]
        kk = 2 * k + cc
        out = g2s if kk < 4 else g2n
        first = (kk % 4) * PIECE
        count = min(PIECE, C - first)
        out[first:first + count] = mine[PIECE:PIECE + count]


def local(
    features, target_ids, near_ids, seed_ids, seed_near, w1_self, w1_neigh, w2_self, w2_neigh, logit_grad
):
    vm = pltpu.VMEM
    dma = pltpu.SemaphoreType.DMA
    vspec = pl.BlockSpec(memory_space=pltpu.VMEM)
    hspec = pl.BlockSpec(memory_space=pltpu.HBM)
    blocks = vm((Q, 32, HS), BF)
    wide = vm((Q, 32, 2 * CP), BF)
    scratch = [
        vm((2, FSL, ND), BF), vm((K1, TGT), jnp.int32), vm((1, TGT), jnp.int32), vm((1, TGT), jnp.int32),
        vm((K2, TGT), jnp.int32), vm((2 * FSL, HID), BF), vm((C, HS), BF), vm((C, HS), BF), vm((C, TGT), BF),
        vm((3, K1 + 1, 8, TGT), jnp.int32), vm((ND, TGT), BF), vm((ND, TGT), BF), vm((2, TGT, 2 * FSL), BF),
        vm((2, 2 * FSL, TGT), BF), vm((2, TGT, TGT), BF), vm((CP, TGT), BF), vm((2 * CP, HS), BF),
        vm((TGT, TGT), BF),
        vm((4, 2 * FSL, HS), BF), vm((4, TGT, HS), F32), vm((3, TGT, HS), BF),
        vm((2, 128, HS), BF), vm((2, TGT, HS), BF),
        blocks, blocks, blocks, blocks, wide, wide, wide, wide,
        blocks, blocks, blocks, blocks,
        vm((4, TGT, HS), BF), vm((Q, 4, PIECE, HS), BF), vm((Q, PIECE, HS), BF),
        vm((Q - 1, 4, PIECE, HS), BF), vm((Q, PIECE, HS), BF),
        vm((19, 16, HS), BF), vm((2, Q - 1, 16, HS), BF), vm((Q, 3, 16, HS), BF), vm((19, 16, HS), BF),
        vm((LP, 32, TGT), BF), vm((Q - 1, 32, TGT), BF), vm((32, TGT), BF),
        dma((10,)), dma((4,)), dma((1,)), dma((1,)), dma((4,)), dma((4,)), dma((6,)), dma((6,)),
        dma((7,)), dma((7,)), dma((7,)), dma((7,)), dma((7,)), dma((7,)), dma((7,)), dma((7,)),
        dma((7,)), dma((7,)), dma((7,)), dma((7,)), dma((6,)), dma((6,)),
        dma((3, 7)), dma((3, 7)), dma((8,)), dma((8,)), dma((3, 7)), dma((3, 7)), dma((3, 7)), dma((3, 7)),
        dma((3, 8)), dma((3, 8)), dma((7,)), dma((7,)), dma((7,)), dma((7,)),
    ]
    gath, lout = pl.pallas_call(
        main_kernel,
        out_shape=(
            jax.ShapeDtypeStruct((Q, 19, 16, HS), BF),
            jax.ShapeDtypeStruct((LP, 32, TGT), BF),
        ),
        in_specs=[hspec] * 10,
        out_specs=(hspec, hspec),
        scratch_shapes=scratch,
        compiler_params=pltpu.CompilerParams(
            collective_id=0, has_side_effects=True, vmem_limit_bytes=62 * 1024 * 1024
        ),
        name="sage_step",
    )(
        features.T, near_ids.T, target_ids.reshape(1, TGT), seed_ids.reshape(1, TGT), seed_near.T,
        w1_self, w1_neigh, w2_self.T, w2_neigh.T, logit_grad.T,
    )
    logits, g1s, g1n, g2s, g2n = pl.pallas_call(
        finish_kernel,
        out_shape=(
            jax.ShapeDtypeStruct((C, TGT), F32),
            jax.ShapeDtypeStruct((FSL, HID), F32),
            jax.ShapeDtypeStruct((FSL, HID), F32),
            jax.ShapeDtypeStruct((C, HS), F32),
            jax.ShapeDtypeStruct((C, HS), F32),
        ),
        in_specs=[vspec, vspec],
        out_specs=(vspec,) * 5,
        compiler_params=pltpu.CompilerParams(vmem_limit_bytes=62 * 1024 * 1024),
        name="finish",
    )(gath, lout)
    return logits.T, g1s, g1n, g2s.T, g2n.T


def solution(mesh):
    return jax.shard_map(
        local,
        mesh=mesh,
        in_specs=(
            P("nodes", "feat"),
            P("nodes"),
            P("nodes", None),
            P("nodes"),
            P("nodes", None),
            P("feat", None),
            P("feat", None),
            P("feat", None),
            P("feat", None),
            P("nodes", None),
        ),
        out_specs=(
            P("nodes", None),
            P("feat", None),
            P("feat", None),
            P("feat", None),
            P("feat", None),
        ),
        check_vma=False,
    )
```

```python
import jax
import jax.numpy as jnp
from jax import lax
from jax.experimental import pallas as pl
from jax.experimental.pallas import tpu as pltpu
from jax.sharding import PartitionSpec as P

BF = jnp.bfloat16
F32 = jnp.float32
MESH = pl.DeviceIdType.MESH

TGT = 256
ND = 1024
FSL = 96
HID = 1024
HS = 128
C = 153
K1 = 25
K2 = 15
CP = 192
LP = 5
Q = 8
PIECE = 48
SETS = ((0, 1), (1, 2), (3, 1))
WIDTHS = (6, 6, 3)


def dot(a, b):
    return jnp.dot(a, b, preferred_element_type=F32)


def dot_dims(a, b, ca, cb):
    return lax.dot_general(a, b, (((ca,), (cb,)), ((), ())), preferred_element_type=F32)


def main_kernel(
    features_hbm, near_hbm, tid_hbm, sid_hbm, snear_hbm,
    w1s_hbm, w1n_hbm, w2s_hbm, w2n_hbm, lg_hbm,
    gath, lout,
    feat_v, near_v, tid_v, sid_v, snear_v, w1_v, w2s_v, w2n_v, lg_v,
    keys, tally, sel, x_v, xt, seedtally, lgp, w2c, perm,
    w1_p, p_own, rs_src, relay_rcv, rs_rcv,
    bw_src, bw_rcv, bz_src, bz_rcv, ew_src, ew_rcv, ez_src, ez_rcv,
    fw_src, fw_rcv, fz_src, fz_rcv,
    ag, gst, gup, rw_rcv, rg_rcv, zsrc, z_rcv, zc_rcv, zfull, lst, l_rcv, ltot,
    in_sem, out_sem, fx_s, fx_r, wx_s, wx_r, rs_s, rs_r, bw_s, bw_r, bz_s, bz_r,
    ew_s, ew_r, ez_s, ez_r, fw_s, fw_r, fz_s, fz_r, ag_s, ag_r,
    rw_s, rw_r, rg_s, rg_r, z_s, z_r, az_s, az_r, aw_s, aw_r, l_s, l_r, la_s, la_r,
):
    node = lax.axis_index("nodes")
    f = lax.axis_index("feat")
    z = node // Q
    w = node % Q
    h = f // 2
    c = f % 2

    def z_peer(d):
        return z ^ d, (node ^ (d * Q), f)

    def w_peer(d):
        return w ^ d, (node ^ d, f)

    def v_peer(d):
        return w ^ d, (node ^ d, f ^ 1)

    def f_peer(d):
        return f ^ d, (node, f ^ d)

    partner = (node, h * 2 + (1 - c))

    up = (node, lax.rem(h + 1, 4) * 2 + c)
    down = (node, lax.rem(h + 3, 4) * 2 + c)

    def each(body):
        for d in range(1, Q):
            body(d)

    loads = [
        pltpu.make_async_copy(src, dst, in_sem.at[n])
        for n, (src, dst) in enumerate(
            (
                (snear_hbm, snear_v),
                (sid_hbm, sid_v),
                (lg_hbm, lg_v),
                (w2s_hbm, w2s_v),
                (w2n_hbm, w2n_v),
                (near_hbm, near_v),
                (tid_hbm, tid_v),
                (features_hbm, feat_v.at[c]),
                (w1s_hbm, w1_v.at[pl.ds(0, FSL)]),
                (w1n_hbm, w1_v.at[pl.ds(FSL, FSL)]),
            )
        )
    ]
    for load in loads:
        load.start()

    barrier = pltpu.get_barrier_semaphore()

    def greet(d):
        for where in (z_peer(d)[1], w_peer(d)[1], f_peer(d)[1], v_peer(d)[1]):
            pl.semaphore_signal(barrier, inc=1, device_id=where, device_id_type=MESH)

    each(greet)

    pending = []

    def remote(src, dst, s_sem, r_sem, where):
        return pltpu.make_async_remote_copy(
            src_ref=src, dst_ref=dst, send_sem=s_sem, recv_sem=r_sem,
            device_id=where, device_id_type=MESH,
        )

    def send(*args):
        copy = remote(*args)
        copy.start()
        pending.append(copy.wait_send)

    def send_each(copy_of, test_of=None):
        def start(d):
            if test_of is None:
                copy_of(d).start()
            else:
                pl.when(test_of(d))(lambda: copy_of(d).start())

        def finish(d):
            if test_of is None:
                copy_of(d).wait_send()
            else:
                pl.when(test_of(d))(lambda: copy_of(d).wait_send())

        each(start)
        pending.append(lambda: each(finish))

    def sent():
        for finish in pending:
            finish()
        pending.clear()

    def landed(ref, r_sem):
        pltpu.make_async_copy(ref, ref, r_sem).wait()

    row = lax.broadcasted_iota(jnp.int32, (8, 128), 0)

    def count(ids, own, low, words, totals_of, ones_of):
        fan = ids.shape[0]
        high = lax.shift_right_logical(ids, low.bit_length() - 1)
        digit = lax.shift_left(jnp.ones_like(ids), (high & 3) * 8)
        tables = [ids & (low - 1)]
        tables += [jnp.where((high >> 2) == g, digit, 0) for g in range(words)]
        for n, table in enumerate(tables):
            for k in range(fan):
                keys[n, k] = jnp.broadcast_to(table[k:k + 1], (8, TGT))
        keys[0, K1] = jnp.broadcast_to(own, (8, TGT))

        def body(step, carry):
            mine = [step * 32 + j * 8 + row for j in range(4)]
            for half in range(2):
                cols = slice(half * 128, half * 128 + 128)
                totals = [[jnp.zeros((8, 128), jnp.int32)] * 4 for _ in range(words)]
                for k in range(fan):
                    theirs = keys[0, k, :, cols]
                    hits = [theirs == m for m in mine]
                    for g in range(words):
                        word = keys[1 + g, k, :, cols]
                        totals[g] = [t + jnp.where(hit, word, 0) for t, hit in zip(totals[g], hits)]
                theirs = keys[0, K1, :, cols]
                for part in range(4 * words):
                    for j in (0, 2):
                        first = part * low + step * 32 + j * 8
                        rows = pl.ds(pl.multiple_of(first, 16), 16)
                        both = [
                            lax.shift_right_logical(totals[part // 4][n], 8 * (part % 4)) & 255
                            for n in (j, j + 1)
                        ]
                        totals_of[rows, cols] = jnp.concatenate(both, axis=0).astype(F32).astype(BF)
                        both = [
                            jnp.where(theirs == mine[n] + part * low, 1.0, 0.0) for n in (j, j + 1)
                        ]
                        ones_of[rows, cols] = jnp.concatenate(both, axis=0).astype(BF)
            return carry

        lax.fori_loop(0, low // 32, body, 0)

    pl.semaphore_wait(barrier, 4 * (Q - 1))
    send(features_hbm, feat_v.at[c], fx_s.at[0], fx_r.at[0], partner)

    def cols_of(dh, cc):
        return pl.ds(pl.multiple_of((lax.rem(h + dh, 4) * 2 + cc) * HS, HS), HS)

    def swap(n):
        return ((n >> 2) & 7) * 32 + (n >> 5) * 4 + (n & 3)

    for n in range(5):
        loads[n].wait()
    for padded, first, given in ((lgp, 0, lg_v), (w2c, 0, w2s_v), (w2c, CP, w2n_v)):
        padded[first:first + CP] = jnp.zeros((CP, padded.shape[1]), BF)
        padded[first:first + C] = given[...]
    count(swap(snear_v[...]), swap(sid_v[...]), 64, 1, seedtally.at[1], seedtally.at[0])
    back = jnp.concatenate(
        [dot_dims(seedtally[0], lgp[...], 1, 1), dot_dims(seedtally[1], lgp[...], 1, 1) / K2], axis=1
    ).astype(BF)
    bw_src[...] = dot(back, w2c[...]).astype(BF).reshape(Q, 32, HS)
    ew_src[...] = back.reshape(Q, 32, 2 * CP)

    def to_w(src, dst, s_sem, r_sem):
        def copy_of(d):
            ww, where = w_peer(d)
            return remote(src.at[ww], dst.at[w], s_sem.at[d - 1], r_sem.at[d - 1], where)

        send_each(copy_of)
        dst[w] = src[w]

    def to_z(src, dst, s_sem, r_sem):
        def copy_of(d):
            zz, where = z_peer(d)
            return remote(src.at[zz], dst.at[z], s_sem.at[d - 1], r_sem.at[d - 1], where)

        send_each(copy_of)
        dst[z] = src[z]

    def from_w(dst, r_sem):
        each(lambda d: landed(dst.at[w ^ d], r_sem.at[d - 1]))

    def from_z(dst, r_sem):
        each(lambda d: landed(dst.at[z ^ d], r_sem.at[d - 1]))

    to_w(bw_src, bw_rcv, bw_s, bw_r)
    loads[8].wait()
    loads[9].wait()
    for place, dh in enumerate((2, 1, 3, 0)):
        send(w1_v.at[:, cols_of(dh, 1 - c)], w1_p.at[place], wx_s.at[place], wx_r.at[place], partner)
    to_w(ew_src, ew_rcv, ew_s, ew_r)

    loads[5].wait()
    loads[6].wait()
    count(near_v[...], tid_v[...], 128, 2, tally, sel)

    loads[7].wait()
    landed(feat_v.at[1 - c], fx_r.at[0])
    both = feat_v[...].reshape(2 * FSL, ND)
    x_self = dot(both, sel[...]).astype(BF)
    agg = (dot(both, tally[...]) / K1).astype(BF)
    for cc in range(2):
        part = slice(cc * FSL, cc * FSL + FSL)
        mine = jnp.concatenate([x_self[part], agg[part]], axis=0)
        xt[cc] = mine
        x_v[cc] = mine.astype(F32).T.astype(BF)

    for place in range(4):
        landed(w1_p.at[place], wx_r.at[place])
    own_rows = jnp.concatenate([w1_v[:, cols_of(dh, c)] for dh in (2, 1, 3, 0)], axis=1)
    partner_rows = jnp.concatenate([w1_p[place] for place in range(4)], axis=1)
    partials = dot(x_v[c], own_rows) + dot(x_v[1 - c], partner_rows)
    for place in range(4):
        p_own[place] = partials[:, place * HS:(place + 1) * HS]

    lo, hi = pl.ds(0, 128), pl.ds(128, 128)
    rs_src[0] = p_own[0].astype(BF)
    send(rs_src.at[0, lo], relay_rcv.at[0], rs_s.at[0], rs_r.at[0], up)
    send(rs_src.at[0, hi], relay_rcv.at[1], rs_s.at[1], rs_r.at[1], down)
    rs_src[1, 128:256] = p_own[1, 128:256].astype(BF)
    send(rs_src.at[1, hi], rs_rcv.at[0, hi], rs_s.at[2], rs_r.at[2], up)
    rs_src[2, 0:128] = p_own[2, 0:128].astype(BF)
    send(rs_src.at[2, lo], rs_rcv.at[1, lo], rs_s.at[3], rs_r.at[3], down)

    a = lax.broadcasted_iota(jnp.int32, (TGT, TGT), 0)
    b = lax.broadcasted_iota(jnp.int32, (TGT, TGT), 1)
    perm[...] = jnp.where(swap(a) == b, 1.0, 0.0).astype(BF)
    from_w(bw_rcv, bw_r)
    bz_src[...] = dot(perm[...], bw_rcv[...].reshape(TGT, HS)).astype(BF).reshape(Q, 32, HS)
    to_z(bz_src, bz_rcv, bz_s, bz_r)
    from_w(ew_rcv, ew_r)
    turned = dot(perm[...], ew_rcv[...].reshape(TGT, 2 * CP)).astype(BF)
    ez_src[...] = turned.reshape(Q, 32, 2 * CP)
    to_z(ez_src, ez_rcv, ez_s, ez_r)

    landed(relay_rcv.at[0], rs_r.at[0])
    rs_src[1, 0:128] = (p_own[1, 0:128] + relay_rcv[0].astype(F32)).astype(BF)
    send(rs_src.at[1, lo], rs_rcv.at[0, lo], rs_s.at[4], rs_r.at[4], up)
    landed(relay_rcv.at[1], rs_r.at[1])
    rs_src[2, 128:256] = (p_own[2, 128:256] + relay_rcv[1].astype(F32)).astype(BF)
    send(rs_src.at[2, hi], rs_rcv.at[1, hi], rs_s.at[5], rs_r.at[5], down)
    from_z(bz_rcv, bz_r)

    pre = p_own[3]
    landed(rs_rcv.at[0, hi], rs_r.at[2])
    landed(rs_rcv.at[1, lo], rs_r.at[3])
    landed(rs_rcv.at[0, lo], rs_r.at[4])
    landed(rs_rcv.at[1, hi], rs_r.at[5])
    pre = pre + rs_rcv[0].astype(F32) + rs_rcv[1].astype(F32)
    sigma = 1.0 / (1.0 + jnp.exp(-pre))
    d_hidden = bz_rcv[...].reshape(TGT, HS).astype(F32)
    ag[0] = (d_hidden * (sigma * (1.0 + pre * (1.0 - sigma)))).astype(BF)
    send(ag.at[0, lo], ag.at[3, lo], ag_s.at[0], ag_r.at[0], up)
    send(ag.at[0, hi], ag.at[1, hi], ag_s.at[1], ag_r.at[1], down)
    send(ag.at[0, hi], ag.at[3, hi], ag_s.at[2], ag_r.at[2], up)
    send(ag.at[0, lo], ag.at[1, lo], ag_s.at[3], ag_r.at[3], down)
    fz_src[...] = (pre * sigma).astype(BF).reshape(Q, 32, HS)
    to_z(fz_src, fz_rcv, fz_s, fz_r)

    slots = {0: 0, 1: 1, 3: 2, 2: 3}

    def lower(dh):
        grad = dot(xt[...].reshape(4 * FSL, TGT), ag[dh])
        gst[:, slots[dh]] = grad.astype(BF).reshape(Q, PIECE, HS)

    def scatter(n):
        span = pl.ds(*SETS[n])

        def copy_of(d):
            ww, where = w_peer(d)
            return remote(
                gst.at[ww, span], rw_rcv.at[d - 1, span], rw_s.at[n, d - 1], rw_r.at[n, d - 1], where
            )

        send_each(copy_of)

    def scatter_upper():
        for kk in range(Q):
            ww, cc = 4 * c + kk // 2, kk % 2
            here = jnp.logical_and(w == ww, c == cc)
            there = jnp.logical_not(here)
            far = remote(
                gup.at[kk], rg_rcv.at[w], rg_s.at[kk], rg_r.at[w], (node - w + ww, 2 * h + cc)
            )
            near = pltpu.make_async_copy(gup.at[kk], rg_rcv.at[w], rg_r.at[w])
            pl.when(there)(far.start)
            pl.when(here)(near.start)
            pending.append(lambda there=there, far=far: pl.when(there)(far.wait_send))

    def reduce_w(n):
        first, many = SETS[n]
        each(lambda d: landed(rw_rcv.at[d - 1, pl.ds(first, many)], rw_r.at[n, d - 1]))
        for slot in range(first, first + many):
            total = gst[w, slot].astype(F32)
            for d in range(1, Q):
                total = total + rw_rcv[d - 1, slot].astype(F32)
            piece = 8 * n + 3 * (slot - first)
            zsrc[piece:piece + 3] = total.astype(BF).reshape(3, 16, HS)
        if n == 0:
            for ww in range(Q):
                landed(rg_rcv.at[ww], rg_r.at[ww])
            total = rg_rcv[0].astype(F32)
            for ww in range(1, Q):
                total = total + rg_rcv[ww].astype(F32)
            zsrc[3:6] = total.astype(BF).reshape(3, 16, HS)

    def scatter_z(n):
        reduce_w(n)
        zsrc[8 * n + 6:8 * n + 8] = jnp.zeros((2, 16, HS), BF)

        def copy_of(d):
            zz, where = z_peer(d)
            return remote(zsrc.at[8 * n + zz], z_rcv.at[n, d - 1], z_s.at[n, d - 1], z_r.at[n, d - 1], where)

        send_each(copy_of)

    def gather_z(n):
        k = 8 * n + z
        each(lambda d: landed(z_rcv.at[n, d - 1], z_r.at[n, d - 1]))
        total = zsrc[k].astype(F32)
        for d in range(1, Q):
            total = total + z_rcv[n, d - 1].astype(F32)
        zfull[k] = total.astype(BF)

        def copy_of(d):
            return remote(zfull.at[k], zfull.at[k], az_s.at[n, d - 1], az_r.at[n, d - 1], z_peer(d)[1])

        send_each(copy_of)

    def gather_w(n):
        pieces = pl.ds(8 * n, WIDTHS[n])
        if n < 2:
            each(lambda d: landed(zfull.at[8 * n + (z ^ d)], az_r.at[n, d - 1]))
        cc, place = w // 4, c * 4 + w % 4

        def copy_of(d):
            return remote(
                zfull.at[pieces], gath.at[place, pieces], aw_s.at[n, d], aw_r.at[n, place],
                (node ^ d, 2 * h + cc),
            )

        send_each(copy_of)
        far = copy_of(0)
        near = pltpu.make_async_copy(zfull.at[pieces], gath.at[place, pieces], aw_r.at[n, place])
        pl.when(c != cc)(far.start)
        pl.when(c == cc)(near.start)
        pending.append(lambda: pl.when(c != cc)(far.wait_send))

    last = pl.ds(16, 3)

    def exchange_z():
        reduce_w(2)

        def copy_of(d):
            return remote(zsrc.at[last], zc_rcv.at[z], z_s.at[2, d - 1], z_r.at[2, d - 1], z_peer(d)[1])

        send_each(copy_of)
        zc_rcv[z] = zsrc[16:19]

    def sum_z():
        from_z(zc_rcv, z_r.at[2])
        total = zc_rcv[0].astype(F32)
        for zz in range(1, Q):
            total = total + zc_rcv[zz].astype(F32)
        zfull[16:19] = total.astype(BF)

    lower(0)
    scatter(0)

    landed(ag.at[3, lo], ag_r.at[0])
    send(ag.at[3, lo], ag.at[2, lo], ag_s.at[4], ag_r.at[4], up)
    landed(ag.at[1, hi], ag_r.at[1])
    send(ag.at[1, hi], ag.at[2, hi], ag_s.at[5], ag_r.at[5], down)

    from_z(ez_rcv, ez_r)
    collected = ez_rcv[...].reshape(TGT, 2 * CP).astype(F32).T.astype(BF)
    gup[...] = dot(collected, fz_src[...].reshape(TGT, HS)).astype(BF).reshape(Q, PIECE, HS)
    scatter_upper()

    landed(ag.at[3, hi], ag_r.at[2])
    landed(ag.at[1, lo], ag_r.at[3])
    grads = dot(xt[...].reshape(4 * FSL, TGT), jnp.concatenate([ag[3], ag[1]], axis=1)).astype(BF)
    gst[:, slots[3]] = grads[:, 0:HS].reshape(Q, PIECE, HS)
    gst[:, slots[1]] = grads[:, HS:2 * HS].reshape(Q, PIECE, HS)
    scatter(1)

    from_z(fz_rcv, fz_r)
    fw_src[...] = dot(perm[...], fz_rcv[...].reshape(TGT, HS)).astype(BF).reshape(Q, 32, HS)
    to_w(fw_src, fw_rcv, fw_s, fw_r)

    landed(ag.at[2, lo], ag_r.at[4])
    landed(ag.at[2, hi], ag_r.at[5])
    lower(2)
    scatter(2)
    scatter_z(0)
    scatter_z(1)

    from_w(fw_rcv, fw_r)
    received = fw_rcv[...].reshape(TGT, HS).astype(F32).T.astype(BF)
    h_self = dot(received, seedtally[0]).astype(BF)
    agg_two = (dot(received, seedtally[1]) / K2).astype(BF)
    part = dot(w2c[0:CP], h_self) + dot(w2c[CP:2 * CP], agg_two)
    lst[...] = part[0:LP * 32].astype(BF).reshape(LP, 32, TGT)

    def logit_part(d):
        ff, where = f_peer(d)
        return remote(lst.at[lax.rem(ff, LP)], l_rcv.at[d - 1], l_s.at[d - 1], l_r.at[d - 1], where)

    send_each(logit_part, lambda d: f_peer(d)[0] < LP)

    exchange_z()
    gather_z(0)
    gather_z(1)

    fl = lax.rem(f, LP)

    @pl.when(f < LP)
    def _():
        each(lambda d: landed(l_rcv.at[d - 1], l_r.at[d - 1]))
        total = lst[fl].astype(F32)
        for d in range(1, Q):
            total = total + l_rcv[d - 1].astype(F32)
        ltot[...] = total.astype(BF)
        pltpu.make_async_copy(ltot, lout.at[fl], out_sem.at[3]).start()

    def logit_sum(d):
        return remote(ltot, lout.at[fl], la_s.at[d - 1], la_r.at[d - 1], f_peer(d)[1])

    send_each(logit_sum, lambda d: f < LP)

    gather_w(0)
    gather_w(1)
    sum_z()
    gather_w(2)
    sent()

    def logits_in(d):
        ff = f ^ d
        pl.when(ff < LP)(lambda: landed(lout.at[lax.rem(ff, LP)], la_r.at[d - 1]))

    each(logits_in)

    @pl.when(f < LP)
    def _():
        landed(lout.at[fl], out_sem.at[3])

    for n in range(3):
        for place in range(Q):
            landed(gath.at[place, pl.ds(8 * n, WIDTHS[n])], aw_r.at[n, place])


def finish_kernel(gath, lout, logits, g1s, g1n, g2s, g2n):
    h = lax.axis_index("feat") // 2
    logits[...] = lout[...].reshape(LP * 32, TGT)[0:C].astype(F32)
    for place in range(Q):
        cc, k = place // 4, place % 4
        mine = gath[place].reshape(19 * 16, HS).astype(F32)
        out = g1s if k < 2 else g1n
        for first, dh in ((0, 0), (128, 1), (176, 3), (256, 2)):
            col = pl.ds(pl.multiple_of((2 * lax.rem(h + dh, 4) + cc) * HS, HS), HS)
            out[(k % 2) * PIECE:(k % 2 + 1) * PIECE, col] = mine[first:first + PIECE]
        kk = 2 * k + cc
        out = g2s if kk < 4 else g2n
        first = (kk % 4) * PIECE
        count = min(PIECE, C - first)
        out[first:first + count] = mine[PIECE:PIECE + count]


def local(
    features, target_ids, near_ids, seed_ids, seed_near, w1_self, w1_neigh, w2_self, w2_neigh, logit_grad
):
    vm = pltpu.VMEM
    dma = pltpu.SemaphoreType.DMA
    vspec = pl.BlockSpec(memory_space=pltpu.VMEM)
    hspec = pl.BlockSpec(memory_space=pltpu.HBM)
    blocks = vm((Q, 32, HS), BF)
    wide = vm((Q, 32, 2 * CP), BF)
    scratch = [
        vm((2, FSL, ND), BF), vm((K1, TGT), jnp.int32), vm((1, TGT), jnp.int32), vm((1, TGT), jnp.int32),
        vm((K2, TGT), jnp.int32), vm((2 * FSL, HID), BF), vm((C, HS), BF), vm((C, HS), BF), vm((C, TGT), BF),
        vm((3, K1 + 1, 8, TGT), jnp.int32), vm((ND, TGT), BF), vm((ND, TGT), BF), vm((2, TGT, 2 * FSL), BF),
        vm((2, 2 * FSL, TGT), BF), vm((2, TGT, TGT), BF), vm((CP, TGT), BF), vm((2 * CP, HS), BF),
        vm((TGT, TGT), BF),
        vm((4, 2 * FSL, HS), BF), vm((4, TGT, HS), F32), vm((3, TGT, HS), BF),
        vm((2, 128, HS), BF), vm((2, TGT, HS), BF),
        blocks, blocks, blocks, blocks, wide, wide, wide, wide,
        blocks, blocks, blocks, blocks,
        vm((4, TGT, HS), BF), vm((Q, 4, PIECE, HS), BF), vm((Q, PIECE, HS), BF),
        vm((Q - 1, 4, PIECE, HS), BF), vm((Q, PIECE, HS), BF),
        vm((19, 16, HS), BF), vm((2, Q - 1, 16, HS), BF), vm((Q, 3, 16, HS), BF), vm((19, 16, HS), BF),
        vm((LP, 32, TGT), BF), vm((Q - 1, 32, TGT), BF), vm((32, TGT), BF),
        dma((10,)), dma((4,)), dma((1,)), dma((1,)), dma((4,)), dma((4,)), dma((6,)), dma((6,)),
        dma((7,)), dma((7,)), dma((7,)), dma((7,)), dma((7,)), dma((7,)), dma((7,)), dma((7,)),
        dma((7,)), dma((7,)), dma((7,)), dma((7,)), dma((6,)), dma((6,)),
        dma((3, 7)), dma((3, 7)), dma((8,)), dma((8,)), dma((3, 7)), dma((3, 7)), dma((3, 7)), dma((3, 7)),
        dma((3, 8)), dma((3, 8)), dma((7,)), dma((7,)), dma((7,)), dma((7,)),
    ]
    gath, lout = pl.pallas_call(
        main_kernel,
        out_shape=(
            jax.ShapeDtypeStruct((Q, 19, 16, HS), BF),
            jax.ShapeDtypeStruct((LP, 32, TGT), BF),
        ),
        in_specs=[hspec] * 10,
        out_specs=(hspec, hspec),
        scratch_shapes=scratch,
        compiler_params=pltpu.CompilerParams(
            collective_id=0, has_side_effects=True, vmem_limit_bytes=62 * 1024 * 1024
        ),
        name="sage_step",
    )(
        features.T, near_ids.T, target_ids.reshape(1, TGT), seed_ids.reshape(1, TGT), seed_near.T,
        w1_self, w1_neigh, w2_self.T, w2_neigh.T, logit_grad.T,
    )
    logits, g1s, g1n, g2s, g2n = pl.pallas_call(
        finish_kernel,
        out_shape=(
            jax.ShapeDtypeStruct((C, TGT), F32),
            jax.ShapeDtypeStruct((FSL, HID), F32),
            jax.ShapeDtypeStruct((FSL, HID), F32),
            jax.ShapeDtypeStruct((C, HS), F32),
            jax.ShapeDtypeStruct((C, HS), F32),
        ),
        in_specs=[vspec, vspec],
        out_specs=(vspec,) * 5,
        compiler_params=pltpu.CompilerParams(vmem_limit_bytes=62 * 1024 * 1024),
        name="finish",
    )(gath, lout)
    return logits.T, g1s, g1n, g2s.T, g2n.T


def solution(mesh):
    return jax.shard_map(
        local,
        mesh=mesh,
        in_specs=(
            P("nodes", "feat"),
            P("nodes"),
            P("nodes", None),
            P("nodes"),
            P("nodes", None),
            P("feat", None),
            P("feat", None),
            P("feat", None),
            P("feat", None),
            P("nodes", None),
        ),
        out_specs=(
            P("nodes", None),
            P("feat", None),
            P("feat", None),
            P("feat", None),
            P("feat", None),
        ),
        check_vma=False,
    )
```

```python
import jax
import jax.numpy as jnp
from jax import lax
from jax.experimental import pallas as pl
from jax.experimental.pallas import tpu as pltpu
from jax.sharding import PartitionSpec as P

BF = jnp.bfloat16
F32 = jnp.float32
MESH = pl.DeviceIdType.MESH

TGT = 256
ND = 1024
FSL = 96
HID = 1024
HS = 128
C = 153
K1 = 25
K2 = 15
CP = 192
LP = 5
Q = 8
PIECE = 48
SETS = ((0, 1), (1, 2), (3, 1))
WIDTHS = (6, 6, 3)


def dot(a, b):
    return jnp.dot(a, b, preferred_element_type=F32)


def dot_dims(a, b, ca, cb):
    return lax.dot_general(a, b, (((ca,), (cb,)), ((), ())), preferred_element_type=F32)


def main_kernel(
    features_hbm, near_hbm, tid_hbm, sid_hbm, snear_hbm,
    w1s_hbm, w1n_hbm, w2s_hbm, w2n_hbm, lg_hbm,
    gath, lout,
    feat_v, near_v, tid_v, sid_v, snear_v, w1_v, w2s_v, w2n_v, lg_v,
    keys, tally, sel, x_v, xt, seedtally, lgp, w2c, perm,
    w1_p, p_own, rs_src, rs_rcv,
    bw_src, bw_rcv, bz_src, bz_rcv, ew_src, ew_rcv, ez_src, ez_rcv,
    fw_src, fw_rcv, fz_src, fz_rcv,
    ag, gst, gup, rw_rcv, rg_rcv, zsrc, z_rcv, zc_rcv, zfull, lst, l_rcv, ltot,
    in_sem, out_sem, fx_s, fx_r, wx_s, wx_r, rs_s, rs_r, bw_s, bw_r, bz_s, bz_r,
    ew_s, ew_r, ez_s, ez_r, fw_s, fw_r, fz_s, fz_r, ag_s, ag_r,
    rw_s, rw_r, rg_s, rg_r, z_s, z_r, az_s, az_r, aw_s, aw_r, l_s, l_r, la_s, la_r,
):
    node = lax.axis_index("nodes")
    f = lax.axis_index("feat")
    z = node // Q
    w = node % Q
    h = f // 2
    c = f % 2

    def z_peer(d):
        return z ^ d, (node ^ (d * Q), f)

    def w_peer(d):
        return w ^ d, (node ^ d, f)

    def v_peer(d):
        return w ^ d, (node ^ d, f ^ 1)

    def f_peer(d):
        return f ^ d, (node, f ^ d)

    partner = (node, h * 2 + (1 - c))

    up = (node, lax.rem(h + 1, 4) * 2 + c)
    down = (node, lax.rem(h + 3, 4) * 2 + c)
    across = (node, lax.rem(h + 2, 4) * 2 + c)

    def each(body):
        for d in range(1, Q):
            body(d)

    loads = [
        pltpu.make_async_copy(src, dst, in_sem.at[n])
        for n, (src, dst) in enumerate(
            (
                (snear_hbm, snear_v),
                (sid_hbm, sid_v),
                (lg_hbm, lg_v),
                (w2s_hbm, w2s_v),
                (w2n_hbm, w2n_v),
                (near_hbm, near_v),
                (tid_hbm, tid_v),
                (features_hbm, feat_v.at[c]),
                (w1s_hbm, w1_v.at[pl.ds(0, FSL)]),
                (w1n_hbm, w1_v.at[pl.ds(FSL, FSL)]),
            )
        )
    ]
    for load in loads:
        load.start()

    barrier = pltpu.get_barrier_semaphore()

    def greet(d):
        for where in (z_peer(d)[1], w_peer(d)[1], f_peer(d)[1], v_peer(d)[1]):
            pl.semaphore_signal(barrier, inc=1, device_id=where, device_id_type=MESH)

    each(greet)

    pending = []

    def remote(src, dst, s_sem, r_sem, where):
        return pltpu.make_async_remote_copy(
            src_ref=src, dst_ref=dst, send_sem=s_sem, recv_sem=r_sem,
            device_id=where, device_id_type=MESH,
        )

    def send(*args):
        copy = remote(*args)
        copy.start()
        pending.append(copy.wait_send)

    def send_each(copy_of, test_of=None):
        def start(d):
            if test_of is None:
                copy_of(d).start()
            else:
                pl.when(test_of(d))(lambda: copy_of(d).start())

        def finish(d):
            if test_of is None:
                copy_of(d).wait_send()
            else:
                pl.when(test_of(d))(lambda: copy_of(d).wait_send())

        each(start)
        pending.append(lambda: each(finish))

    def sent():
        for finish in pending:
            finish()
        pending.clear()

    def landed(ref, r_sem):
        pltpu.make_async_copy(ref, ref, r_sem).wait()

    row = lax.broadcasted_iota(jnp.int32, (8, 128), 0)

    def count(ids, own, low, words, totals_of, ones_of):
        fan = ids.shape[0]
        high = lax.shift_right_logical(ids, low.bit_length() - 1)
        digit = lax.shift_left(jnp.ones_like(ids), (high & 3) * 8)
        tables = [ids & (low - 1)]
        tables += [jnp.where((high >> 2) == g, digit, 0) for g in range(words)]
        for n, table in enumerate(tables):
            for k in range(fan):
                keys[n, k] = jnp.broadcast_to(table[k:k + 1], (8, TGT))
        keys[0, K1] = jnp.broadcast_to(own, (8, TGT))

        def body(step, carry):
            mine = [step * 32 + j * 8 + row for j in range(4)]
            for half in range(2):
                cols = slice(half * 128, half * 128 + 128)
                totals = [[jnp.zeros((8, 128), jnp.int32)] * 4 for _ in range(words)]
                for k in range(fan):
                    theirs = keys[0, k, :, cols]
                    hits = [theirs == m for m in mine]
                    for g in range(words):
                        word = keys[1 + g, k, :, cols]
                        totals[g] = [t + jnp.where(hit, word, 0) for t, hit in zip(totals[g], hits)]
                theirs = keys[0, K1, :, cols]
                for part in range(4 * words):
                    for j in (0, 2):
                        first = part * low + step * 32 + j * 8
                        rows = pl.ds(pl.multiple_of(first, 16), 16)
                        both = [
                            lax.shift_right_logical(totals[part // 4][n], 8 * (part % 4)) & 255
                            for n in (j, j + 1)
                        ]
                        totals_of[rows, cols] = jnp.concatenate(both, axis=0).astype(F32).astype(BF)
                        both = [
                            jnp.where(theirs == mine[n] + part * low, 1.0, 0.0) for n in (j, j + 1)
                        ]
                        ones_of[rows, cols] = jnp.concatenate(both, axis=0).astype(BF)
            return carry

        lax.fori_loop(0, low // 32, body, 0)

    pl.semaphore_wait(barrier, 4 * (Q - 1))
    send(features_hbm, feat_v.at[c], fx_s.at[0], fx_r.at[0], partner)

    def cols_of(dh, cc):
        return pl.ds(pl.multiple_of((lax.rem(h + dh, 4) * 2 + cc) * HS, HS), HS)

    def swap(n):
        return ((n >> 2) & 7) * 32 + (n >> 5) * 4 + (n & 3)

    for n in range(5):
        loads[n].wait()
    for padded, first, given in ((lgp, 0, lg_v), (w2c, 0, w2s_v), (w2c, CP, w2n_v)):
        padded[first:first + CP] = jnp.zeros((CP, padded.shape[1]), BF)
        padded[first:first + C] = given[...]
    count(swap(snear_v[...]), swap(sid_v[...]), 64, 1, seedtally.at[1], seedtally.at[0])
    back = jnp.concatenate(
        [dot_dims(seedtally[0], lgp[...], 1, 1), dot_dims(seedtally[1], lgp[...], 1, 1) / K2], axis=1
    ).astype(BF)
    bw_src[...] = dot(back, w2c[...]).astype(BF).reshape(Q, 32, HS)
    ew_src[...] = back.reshape(Q, 32, 2 * CP)

    def to_w(src, dst, s_sem, r_sem):
        def copy_of(d):
            ww, where = w_peer(d)
            return remote(src.at[ww], dst.at[w], s_sem.at[d - 1], r_sem.at[d - 1], where)

        send_each(copy_of)
        dst[w] = src[w]

    def to_z(src, dst, s_sem, r_sem):
        def copy_of(d):
            zz, where = z_peer(d)
            return remote(src.at[zz], dst.at[z], s_sem.at[d - 1], r_sem.at[d - 1], where)

        send_each(copy_of)
        dst[z] = src[z]

    def from_w(dst, r_sem):
        each(lambda d: landed(dst.at[w ^ d], r_sem.at[d - 1]))

    def from_z(dst, r_sem):
        each(lambda d: landed(dst.at[z ^ d], r_sem.at[d - 1]))

    to_w(bw_src, bw_rcv, bw_s, bw_r)
    loads[8].wait()
    loads[9].wait()
    for place, dh in enumerate((2, 1, 3, 0)):
        send(w1_v.at[:, cols_of(dh, 1 - c)], w1_p.at[place], wx_s.at[place], wx_r.at[place], partner)
    to_w(ew_src, ew_rcv, ew_s, ew_r)

    loads[5].wait()
    loads[6].wait()
    count(near_v[...], tid_v[...], 128, 2, tally, sel)

    loads[7].wait()
    landed(feat_v.at[1 - c], fx_r.at[0])
    both = feat_v[...].reshape(2 * FSL, ND)
    x_self = dot(both, sel[...]).astype(BF)
    agg = (dot(both, tally[...]) / K1).astype(BF)
    for cc in range(2):
        part = slice(cc * FSL, cc * FSL + FSL)
        mine = jnp.concatenate([x_self[part], agg[part]], axis=0)
        xt[cc] = mine
        x_v[cc] = mine.astype(F32).T.astype(BF)

    for place in range(4):
        landed(w1_p.at[place], wx_r.at[place])
    own_rows = jnp.concatenate([w1_v[:, cols_of(dh, c)] for dh in (2, 1, 3, 0)], axis=1)
    partner_rows = jnp.concatenate([w1_p[place] for place in range(4)], axis=1)
    partials = dot(x_v[c], own_rows) + dot(x_v[1 - c], partner_rows)
    for place in range(4):
        p_own[place] = partials[:, place * HS:(place + 1) * HS]

    for place, where in enumerate((across, up, down)):
        rs_src[place] = p_own[place].astype(BF)
        send(rs_src.at[place], rs_rcv.at[place], rs_s.at[place], rs_r.at[place], where)

    a = lax.broadcasted_iota(jnp.int32, (TGT, TGT), 0)
    b = lax.broadcasted_iota(jnp.int32, (TGT, TGT), 1)
    perm[...] = jnp.where(swap(a) == b, 1.0, 0.0).astype(BF)
    from_w(bw_rcv, bw_r)
    bz_src[...] = dot(perm[...], bw_rcv[...].reshape(TGT, HS)).astype(BF).reshape(Q, 32, HS)
    to_z(bz_src, bz_rcv, bz_s, bz_r)
    from_w(ew_rcv, ew_r)
    turned = dot(perm[...], ew_rcv[...].reshape(TGT, 2 * CP)).astype(BF)
    ez_src[...] = turned.reshape(Q, 32, 2 * CP)
    to_z(ez_src, ez_rcv, ez_s, ez_r)

    from_z(bz_rcv, bz_r)

    pre = p_own[3]
    for place in range(3):
        landed(rs_rcv.at[place], rs_r.at[place])
        pre = pre + rs_rcv[place].astype(F32)
    sigma = 1.0 / (1.0 + jnp.exp(-pre))
    d_hidden = bz_rcv[...].reshape(TGT, HS).astype(F32)
    ag[0] = (d_hidden * (sigma * (1.0 + pre * (1.0 - sigma)))).astype(BF)
    send(ag.at[0], ag.at[3], ag_s.at[0], ag_r.at[0], up)
    send(ag.at[0], ag.at[1], ag_s.at[1], ag_r.at[1], down)
    send(ag.at[0], ag.at[2], ag_s.at[2], ag_r.at[2], across)
    fz_src[...] = (pre * sigma).astype(BF).reshape(Q, 32, HS)
    to_z(fz_src, fz_rcv, fz_s, fz_r)

    slots = {0: 0, 1: 1, 3: 2, 2: 3}

    def lower(dh):
        grad = dot(xt[...].reshape(4 * FSL, TGT), ag[dh])
        gst[:, slots[dh]] = grad.astype(BF).reshape(Q, PIECE, HS)

    def scatter(n):
        span = pl.ds(*SETS[n])

        def copy_of(d):
            ww, where = w_peer(d)
            return remote(
                gst.at[ww, span], rw_rcv.at[d - 1, span], rw_s.at[n, d - 1], rw_r.at[n, d - 1], where
            )

        send_each(copy_of)

    def scatter_upper():
        for kk in range(Q):
            ww, cc = 4 * c + kk // 2, kk % 2
            here = jnp.logical_and(w == ww, c == cc)
            there = jnp.logical_not(here)
            far = remote(
                gup.at[kk], rg_rcv.at[w], rg_s.at[kk], rg_r.at[w], (node - w + ww, 2 * h + cc)
            )
            near = pltpu.make_async_copy(gup.at[kk], rg_rcv.at[w], rg_r.at[w])
            pl.when(there)(far.start)
            pl.when(here)(near.start)
            pending.append(lambda there=there, far=far: pl.when(there)(far.wait_send))

    def reduce_w(n):
        first, many = SETS[n]
        each(lambda d: landed(rw_rcv.at[d - 1, pl.ds(first, many)], rw_r.at[n, d - 1]))
        for slot in range(first, first + many):
            total = gst[w, slot].astype(F32)
            for d in range(1, Q):
                total = total + rw_rcv[d - 1, slot].astype(F32)
            piece = 8 * n + 3 * (slot - first)
            zsrc[piece:piece + 3] = total.astype(BF).reshape(3, 16, HS)
        if n == 0:
            for ww in range(Q):
                landed(rg_rcv.at[ww], rg_r.at[ww])
            total = rg_rcv[0].astype(F32)
            for ww in range(1, Q):
                total = total + rg_rcv[ww].astype(F32)
            zsrc[3:6] = total.astype(BF).reshape(3, 16, HS)

    def scatter_z(n):
        reduce_w(n)
        zsrc[8 * n + 6:8 * n + 8] = jnp.zeros((2, 16, HS), BF)

        def copy_of(d):
            zz, where = z_peer(d)
            return remote(zsrc.at[8 * n + zz], z_rcv.at[n, d - 1], z_s.at[n, d - 1], z_r.at[n, d - 1], where)

        send_each(copy_of)

    def gather_z(n):
        k = 8 * n + z
        each(lambda d: landed(z_rcv.at[n, d - 1], z_r.at[n, d - 1]))
        total = zsrc[k].astype(F32)
        for d in range(1, Q):
            total = total + z_rcv[n, d - 1].astype(F32)
        zfull[k] = total.astype(BF)

        def copy_of(d):
            return remote(zfull.at[k], zfull.at[k], az_s.at[n, d - 1], az_r.at[n, d - 1], z_peer(d)[1])

        send_each(copy_of)

    def gather_w(n):
        pieces = pl.ds(8 * n, WIDTHS[n])
        if n < 2:
            each(lambda d: landed(zfull.at[8 * n + (z ^ d)], az_r.at[n, d - 1]))
        cc, place = w // 4, c * 4 + w % 4

        def copy_of(d):
            return remote(
                zfull.at[pieces], gath.at[place, pieces], aw_s.at[n, d], aw_r.at[n, place],
                (node ^ d, 2 * h + cc),
            )

        send_each(copy_of)
        far = copy_of(0)
        near = pltpu.make_async_copy(zfull.at[pieces], gath.at[place, pieces], aw_r.at[n, place])
        pl.when(c != cc)(far.start)
        pl.when(c == cc)(near.start)
        pending.append(lambda: pl.when(c != cc)(far.wait_send))

    last = pl.ds(16, 3)

    def exchange_z():
        reduce_w(2)

        def copy_of(d):
            return remote(zsrc.at[last], zc_rcv.at[z], z_s.at[2, d - 1], z_r.at[2, d - 1], z_peer(d)[1])

        send_each(copy_of)
        zc_rcv[z] = zsrc[16:19]

    def sum_z():
        from_z(zc_rcv, z_r.at[2])
        total = zc_rcv[0].astype(F32)
        for zz in range(1, Q):
            total = total + zc_rcv[zz].astype(F32)
        zfull[16:19] = total.astype(BF)

    lower(0)
    scatter(0)

    from_z(ez_rcv, ez_r)
    collected = ez_rcv[...].reshape(TGT, 2 * CP).astype(F32).T.astype(BF)
    gup[...] = dot(collected, fz_src[...].reshape(TGT, HS)).astype(BF).reshape(Q, PIECE, HS)
    scatter_upper()

    landed(ag.at[3], ag_r.at[0])
    landed(ag.at[1], ag_r.at[1])
    grads = dot(xt[...].reshape(4 * FSL, TGT), jnp.concatenate([ag[3], ag[1]], axis=1)).astype(BF)
    gst[:, slots[3]] = grads[:, 0:HS].reshape(Q, PIECE, HS)
    gst[:, slots[1]] = grads[:, HS:2 * HS].reshape(Q, PIECE, HS)
    scatter(1)

    from_z(fz_rcv, fz_r)
    fw_src[...] = dot(perm[...], fz_rcv[...].reshape(TGT, HS)).astype(BF).reshape(Q, 32, HS)
    to_w(fw_src, fw_rcv, fw_s, fw_r)

    landed(ag.at[2], ag_r.at[2])
    lower(2)
    scatter(2)
    scatter_z(0)
    scatter_z(1)

    from_w(fw_rcv, fw_r)
    received = fw_rcv[...].reshape(TGT, HS).astype(F32).T.astype(BF)
    h_self = dot(received, seedtally[0]).astype(BF)
    agg_two = (dot(received, seedtally[1]) / K2).astype(BF)
    part = dot(w2c[0:CP], h_self) + dot(w2c[CP:2 * CP], agg_two)
    lst[...] = part[0:LP * 32].astype(BF).reshape(LP, 32, TGT)

    def logit_part(d):
        ff, where = f_peer(d)
        return remote(lst.at[lax.rem(ff, LP)], l_rcv.at[d - 1], l_s.at[d - 1], l_r.at[d - 1], where)

    send_each(logit_part, lambda d: f_peer(d)[0] < LP)

    exchange_z()
    gather_z(0)
    gather_z(1)

    fl = lax.rem(f, LP)

    @pl.when(f < LP)
    def _():
        each(lambda d: landed(l_rcv.at[d - 1], l_r.at[d - 1]))
        total = lst[fl].astype(F32)
        for d in range(1, Q):
            total = total + l_rcv[d - 1].astype(F32)
        ltot[...] = total.astype(BF)
        pltpu.make_async_copy(ltot, lout.at[fl], out_sem.at[3]).start()

    def logit_sum(d):
        return remote(ltot, lout.at[fl], la_s.at[d - 1], la_r.at[d - 1], f_peer(d)[1])

    send_each(logit_sum, lambda d: f < LP)

    gather_w(0)
    gather_w(1)
    sum_z()
    gather_w(2)
    sent()

    def logits_in(d):
        ff = f ^ d
        pl.when(ff < LP)(lambda: landed(lout.at[lax.rem(ff, LP)], la_r.at[d - 1]))

    each(logits_in)

    @pl.when(f < LP)
    def _():
        landed(lout.at[fl], out_sem.at[3])

    for n in range(3):
        for place in range(Q):
            landed(gath.at[place, pl.ds(8 * n, WIDTHS[n])], aw_r.at[n, place])


def finish_kernel(gath, lout, logits, g1s, g1n, g2s, g2n):
    h = lax.axis_index("feat") // 2
    logits[...] = lout[...].reshape(LP * 32, TGT)[0:C].astype(F32)
    for place in range(Q):
        cc, k = place // 4, place % 4
        mine = gath[place].reshape(19 * 16, HS).astype(F32)
        out = g1s if k < 2 else g1n
        for first, dh in ((0, 0), (128, 1), (176, 3), (256, 2)):
            col = pl.ds(pl.multiple_of((2 * lax.rem(h + dh, 4) + cc) * HS, HS), HS)
            out[(k % 2) * PIECE:(k % 2 + 1) * PIECE, col] = mine[first:first + PIECE]
        kk = 2 * k + cc
        out = g2s if kk < 4 else g2n
        first = (kk % 4) * PIECE
        count = min(PIECE, C - first)
        out[first:first + count] = mine[PIECE:PIECE + count]


def local(
    features, target_ids, near_ids, seed_ids, seed_near, w1_self, w1_neigh, w2_self, w2_neigh, logit_grad
):
    vm = pltpu.VMEM
    dma = pltpu.SemaphoreType.DMA
    vspec = pl.BlockSpec(memory_space=pltpu.VMEM)
    hspec = pl.BlockSpec(memory_space=pltpu.HBM)
    blocks = vm((Q, 32, HS), BF)
    wide = vm((Q, 32, 2 * CP), BF)
    scratch = [
        vm((2, FSL, ND), BF), vm((K1, TGT), jnp.int32), vm((1, TGT), jnp.int32), vm((1, TGT), jnp.int32),
        vm((K2, TGT), jnp.int32), vm((2 * FSL, HID), BF), vm((C, HS), BF), vm((C, HS), BF), vm((C, TGT), BF),
        vm((3, K1 + 1, 8, TGT), jnp.int32), vm((ND, TGT), BF), vm((ND, TGT), BF), vm((2, TGT, 2 * FSL), BF),
        vm((2, 2 * FSL, TGT), BF), vm((2, TGT, TGT), BF), vm((CP, TGT), BF), vm((2 * CP, HS), BF),
        vm((TGT, TGT), BF),
        vm((4, 2 * FSL, HS), BF), vm((4, TGT, HS), F32), vm((3, TGT, HS), BF),
        vm((3, TGT, HS), BF),
        blocks, blocks, blocks, blocks, wide, wide, wide, wide,
        blocks, blocks, blocks, blocks,
        vm((4, TGT, HS), BF), vm((Q, 4, PIECE, HS), BF), vm((Q, PIECE, HS), BF),
        vm((Q - 1, 4, PIECE, HS), BF), vm((Q, PIECE, HS), BF),
        vm((19, 16, HS), BF), vm((2, Q - 1, 16, HS), BF), vm((Q, 3, 16, HS), BF), vm((19, 16, HS), BF),
        vm((LP, 32, TGT), BF), vm((Q - 1, 32, TGT), BF), vm((32, TGT), BF),
        dma((10,)), dma((4,)), dma((1,)), dma((1,)), dma((4,)), dma((4,)), dma((6,)), dma((6,)),
        dma((7,)), dma((7,)), dma((7,)), dma((7,)), dma((7,)), dma((7,)), dma((7,)), dma((7,)),
        dma((7,)), dma((7,)), dma((7,)), dma((7,)), dma((6,)), dma((6,)),
        dma((3, 7)), dma((3, 7)), dma((8,)), dma((8,)), dma((3, 7)), dma((3, 7)), dma((3, 7)), dma((3, 7)),
        dma((3, 8)), dma((3, 8)), dma((7,)), dma((7,)), dma((7,)), dma((7,)),
    ]
    gath, lout = pl.pallas_call(
        main_kernel,
        out_shape=(
            jax.ShapeDtypeStruct((Q, 19, 16, HS), BF),
            jax.ShapeDtypeStruct((LP, 32, TGT), BF),
        ),
        in_specs=[hspec] * 10,
        out_specs=(hspec, hspec),
        scratch_shapes=scratch,
        compiler_params=pltpu.CompilerParams(
            collective_id=0, has_side_effects=True, vmem_limit_bytes=62 * 1024 * 1024
        ),
        name="sage_step",
    )(
        features.T, near_ids.T, target_ids.reshape(1, TGT), seed_ids.reshape(1, TGT), seed_near.T,
        w1_self, w1_neigh, w2_self.T, w2_neigh.T, logit_grad.T,
    )
    logits, g1s, g1n, g2s, g2n = pl.pallas_call(
        finish_kernel,
        out_shape=(
            jax.ShapeDtypeStruct((C, TGT), F32),
            jax.ShapeDtypeStruct((FSL, HID), F32),
            jax.ShapeDtypeStruct((FSL, HID), F32),
            jax.ShapeDtypeStruct((C, HS), F32),
            jax.ShapeDtypeStruct((C, HS), F32),
        ),
        in_specs=[vspec, vspec],
        out_specs=(vspec,) * 5,
        compiler_params=pltpu.CompilerParams(vmem_limit_bytes=62 * 1024 * 1024),
        name="finish",
    )(gath, lout)
    return logits.T, g1s, g1n, g2s.T, g2n.T


def solution(mesh):
    return jax.shard_map(
        local,
        mesh=mesh,
        in_specs=(
            P("nodes", "feat"),
            P("nodes"),
            P("nodes", None),
            P("nodes"),
            P("nodes", None),
            P("feat", None),
            P("feat", None),
            P("feat", None),
            P("feat", None),
            P("nodes", None),
        ),
        out_specs=(
            P("nodes", None),
            P("feat", None),
            P("feat", None),
            P("feat", None),
            P("feat", None),
        ),
        check_vma=False,
    )
```

```python
import jax
import jax.numpy as jnp
from jax import lax
from jax.experimental import pallas as pl
from jax.experimental.pallas import tpu as pltpu
from jax.sharding import PartitionSpec as P

BF = jnp.bfloat16
F32 = jnp.float32
MESH = pl.DeviceIdType.MESH

TGT = 256
ND = 1024
FSL = 96
HID = 1024
HS = 128
C = 153
K1 = 25
K2 = 15
CP = 192
LP = 5
Q = 8
PIECE = 48
SETS = ((0, 1), (1, 2), (3, 1))
WIDTHS = (6, 6, 3)


def dot(a, b):
    return jnp.dot(a, b, preferred_element_type=F32)


def dot_dims(a, b, ca, cb):
    return lax.dot_general(a, b, (((ca,), (cb,)), ((), ())), preferred_element_type=F32)


def main_kernel(
    features_hbm, near_hbm, tid_hbm, sid_hbm, snear_hbm,
    w1s_hbm, w1n_hbm, w2s_hbm, w2n_hbm, lg_hbm,
    gath, lout,
    feat_v, near_v, tid_v, sid_v, snear_v, w1_v, w2s_v, w2n_v, lg_v,
    keys, tally, sel, x_v, xt, seedtally, lgp, w2c, perm,
    w1_p, p_own, rs_src, rs_rcv,
    bw_src, bw_rcv, bz_src, bz_rcv, ew_src, ew_rcv, ez_src, ez_rcv,
    fw_src, fw_rcv, fz_src, fz_rcv,
    ag, gst, gup, rw_rcv, rg_rcv, zsrc, z_rcv, zc_rcv, zfull, lst, l_rcv, ltot,
    in_sem, out_sem, fx_s, fx_r, wx_s, wx_r, rs_s, rs_r, bw_s, bw_r, bz_s, bz_r,
    ew_s, ew_r, ez_s, ez_r, fw_s, fw_r, fz_s, fz_r, ag_s, ag_r,
    rw_s, rw_r, rg_s, rg_r, z_s, z_r, az_s, az_r, aw_s, aw_r, l_s, l_r, la_s, la_r,
):
    node = lax.axis_index("nodes")
    f = lax.axis_index("feat")
    z = node // Q
    w = node % Q
    h = f // 2
    c = f % 2

    def z_peer(d):
        return z ^ d, (node ^ (d * Q), f)

    def w_peer(d):
        return w ^ d, (node ^ d, f)

    def v_peer(d):
        return w ^ d, (node ^ d, f ^ 1)

    def f_peer(d):
        return f ^ d, (node, f ^ d)

    partner = (node, h * 2 + (1 - c))

    up = (node, lax.rem(h + 1, 4) * 2 + c)
    down = (node, lax.rem(h + 3, 4) * 2 + c)
    across = (node, lax.rem(h + 2, 4) * 2 + c)

    def each(body):
        for d in range(1, Q):
            body(d)

    loads = [
        pltpu.make_async_copy(src, dst, in_sem.at[n])
        for n, (src, dst) in enumerate(
            (
                (snear_hbm, snear_v),
                (sid_hbm, sid_v),
                (lg_hbm, lg_v),
                (w2s_hbm, w2s_v),
                (w2n_hbm, w2n_v),
                (near_hbm, near_v),
                (tid_hbm, tid_v),
                (features_hbm, feat_v.at[c]),
                (w1s_hbm, w1_v.at[pl.ds(0, FSL)]),
                (w1n_hbm, w1_v.at[pl.ds(FSL, FSL)]),
            )
        )
    ]
    for load in loads:
        load.start()

    barrier = pltpu.get_barrier_semaphore()

    def greet(d):
        for where in (z_peer(d)[1], w_peer(d)[1], f_peer(d)[1], v_peer(d)[1]):
            pl.semaphore_signal(barrier, inc=1, device_id=where, device_id_type=MESH)

    each(greet)

    pending = []

    def remote(src, dst, s_sem, r_sem, where):
        return pltpu.make_async_remote_copy(
            src_ref=src, dst_ref=dst, send_sem=s_sem, recv_sem=r_sem,
            device_id=where, device_id_type=MESH,
        )

    def send(*args):
        copy = remote(*args)
        copy.start()
        pending.append(copy.wait_send)

    def send_each(copy_of, test_of=None):
        def start(d):
            if test_of is None:
                copy_of(d).start()
            else:
                pl.when(test_of(d))(lambda: copy_of(d).start())

        def finish(d):
            if test_of is None:
                copy_of(d).wait_send()
            else:
                pl.when(test_of(d))(lambda: copy_of(d).wait_send())

        each(start)
        pending.append(lambda: each(finish))

    def sent():
        for finish in pending:
            finish()
        pending.clear()

    def landed(ref, r_sem):
        pltpu.make_async_copy(ref, ref, r_sem).wait()

    row = lax.broadcasted_iota(jnp.int32, (8, 128), 0)

    def count(ids, own, low, words, totals_of, ones_of):
        fan = ids.shape[0]
        high = lax.shift_right_logical(ids, low.bit_length() - 1)
        digit = lax.shift_left(jnp.ones_like(ids), (high & 3) * 8)
        tables = [ids & (low - 1)]
        tables += [jnp.where((high >> 2) == g, digit, 0) for g in range(words)]
        for n, table in enumerate(tables):
            for k in range(fan):
                keys[n, k] = jnp.broadcast_to(table[k:k + 1], (8, TGT))
        keys[0, K1] = jnp.broadcast_to(own, (8, TGT))

        def body(step, carry):
            mine = [step * 32 + j * 8 + row for j in range(4)]
            for half in range(2):
                cols = slice(half * 128, half * 128 + 128)
                totals = [[jnp.zeros((8, 128), jnp.int32)] * 4 for _ in range(words)]
                for k in range(fan):
                    theirs = keys[0, k, :, cols]
                    hits = [theirs == m for m in mine]
                    for g in range(words):
                        word = keys[1 + g, k, :, cols]
                        totals[g] = [t + jnp.where(hit, word, 0) for t, hit in zip(totals[g], hits)]
                theirs = keys[0, K1, :, cols]
                for part in range(4 * words):
                    for j in (0, 2):
                        first = part * low + step * 32 + j * 8
                        rows = pl.ds(pl.multiple_of(first, 16), 16)
                        both = [
                            lax.shift_right_logical(totals[part // 4][n], 8 * (part % 4)) & 255
                            for n in (j, j + 1)
                        ]
                        totals_of[rows, cols] = jnp.concatenate(both, axis=0).astype(F32).astype(BF)
                        both = [
                            jnp.where(theirs == mine[n] + part * low, 1.0, 0.0) for n in (j, j + 1)
                        ]
                        ones_of[rows, cols] = jnp.concatenate(both, axis=0).astype(BF)
            return carry

        lax.fori_loop(0, low // 32, body, 0)

    pl.semaphore_wait(barrier, 4 * (Q - 1))
    send(features_hbm, feat_v.at[c], fx_s.at[0], fx_r.at[0], partner)

    def cols_of(dh, cc):
        return pl.ds(pl.multiple_of((lax.rem(h + dh, 4) * 2 + cc) * HS, HS), HS)

    def swap(n):
        return ((n >> 2) & 7) * 32 + (n >> 5) * 4 + (n & 3)

    for n in range(5):
        loads[n].wait()
    for padded, first, given in ((lgp, 0, lg_v), (w2c, 0, w2s_v), (w2c, CP, w2n_v)):
        padded[first:first + CP] = jnp.zeros((CP, padded.shape[1]), BF)
        padded[first:first + C] = given[...]
    count(swap(snear_v[...]), swap(sid_v[...]), 64, 1, seedtally.at[1], seedtally.at[0])
    back = jnp.concatenate(
        [dot_dims(seedtally[0], lgp[...], 1, 1), dot_dims(seedtally[1], lgp[...], 1, 1) / K2], axis=1
    ).astype(BF)
    bw_src[...] = dot(back, w2c[...]).astype(BF).reshape(Q, 32, HS)
    ew_src[...] = back.reshape(Q, 32, 2 * CP)

    def to_w(src, dst, s_sem, r_sem):
        def copy_of(d):
            ww, where = w_peer(d)
            return remote(src.at[ww], dst.at[w], s_sem.at[d - 1], r_sem.at[d - 1], where)

        send_each(copy_of)
        dst[w] = src[w]

    def to_z(src, dst, s_sem, r_sem):
        def copy_of(d):
            zz, where = z_peer(d)
            return remote(src.at[zz], dst.at[z], s_sem.at[d - 1], r_sem.at[d - 1], where)

        send_each(copy_of)
        dst[z] = src[z]

    def from_w(dst, r_sem):
        each(lambda d: landed(dst.at[w ^ d], r_sem.at[d - 1]))

    def from_z(dst, r_sem):
        each(lambda d: landed(dst.at[z ^ d], r_sem.at[d - 1]))

    to_w(bw_src, bw_rcv, bw_s, bw_r)
    loads[8].wait()
    loads[9].wait()
    for place, dh in enumerate((2, 1, 3, 0)):
        send(w1_v.at[:, cols_of(dh, 1 - c)], w1_p.at[place], wx_s.at[place], wx_r.at[place], partner)
    to_w(ew_src, ew_rcv, ew_s, ew_r)

    loads[5].wait()
    loads[6].wait()
    count(near_v[...], tid_v[...], 128, 2, tally, sel)

    loads[7].wait()
    landed(feat_v.at[1 - c], fx_r.at[0])
    both = feat_v[...].reshape(2 * FSL, ND)
    x_self = dot(both, sel[...]).astype(BF)
    agg = (dot(both, tally[...]) / K1).astype(BF)
    for cc in range(2):
        part = slice(cc * FSL, cc * FSL + FSL)
        mine = jnp.concatenate([x_self[part], agg[part]], axis=0)
        xt[cc] = mine
        x_v[cc] = mine.astype(F32).T.astype(BF)

    for place in range(4):
        landed(w1_p.at[place], wx_r.at[place])
    own_rows = jnp.concatenate([w1_v[:, cols_of(dh, c)] for dh in (2, 1, 3, 0)], axis=1)
    partner_rows = jnp.concatenate([w1_p[place] for place in range(4)], axis=1)
    partials = dot(x_v[c], own_rows) + dot(x_v[1 - c], partner_rows)
    for place in range(4):
        p_own[place] = partials[:, place * HS:(place + 1) * HS]

    for place, where in enumerate((across, up, down)):
        rs_src[place] = p_own[place].astype(BF)
        send(rs_src.at[place], rs_rcv.at[place], rs_s.at[place], rs_r.at[place], where)

    a = lax.broadcasted_iota(jnp.int32, (TGT, TGT), 0)
    b = lax.broadcasted_iota(jnp.int32, (TGT, TGT), 1)
    perm[...] = jnp.where(swap(a) == b, 1.0, 0.0).astype(BF)
    from_w(bw_rcv, bw_r)
    bz_src[...] = dot(perm[...], bw_rcv[...].reshape(TGT, HS)).astype(BF).reshape(Q, 32, HS)
    to_z(bz_src, bz_rcv, bz_s, bz_r)
    from_w(ew_rcv, ew_r)
    turned = dot(perm[...], ew_rcv[...].reshape(TGT, 2 * CP)).astype(BF)
    ez_src[...] = turned.reshape(Q, 32, 2 * CP)
    to_z(ez_src, ez_rcv, ez_s, ez_r)

    from_z(bz_rcv, bz_r)

    pre = p_own[3]
    for place in range(3):
        landed(rs_rcv.at[place], rs_r.at[place])
        pre = pre + rs_rcv[place].astype(F32)
    sigma = 1.0 / (1.0 + jnp.exp(-pre))
    d_hidden = bz_rcv[...].reshape(TGT, HS).astype(F32)
    ag[0] = (d_hidden * (sigma * (1.0 + pre * (1.0 - sigma)))).astype(BF)
    send(ag.at[0], ag.at[3], ag_s.at[0], ag_r.at[0], up)
    send(ag.at[0], ag.at[1], ag_s.at[1], ag_r.at[1], down)
    send(ag.at[0], ag.at[2], ag_s.at[2], ag_r.at[2], across)
    fz_src[...] = (pre * sigma).astype(BF).reshape(Q, 32, HS)
    to_z(fz_src, fz_rcv, fz_s, fz_r)

    slots = {0: 0, 1: 1, 3: 2, 2: 3}

    def lower(dh):
        grad = dot(xt[...].reshape(4 * FSL, TGT), ag[dh])
        gst[:, slots[dh]] = grad.astype(BF).reshape(Q, PIECE, HS)

    def scatter(n):
        span = pl.ds(*SETS[n])

        def copy_of(d):
            ww, where = w_peer(d)
            return remote(
                gst.at[ww, span], rw_rcv.at[d - 1, span], rw_s.at[n, d - 1], rw_r.at[n, d - 1], where
            )

        send_each(copy_of)

    def scatter_upper():
        for kk in range(Q):
            ww, cc = 4 * c + kk // 2, kk % 2
            here = jnp.logical_and(w == ww, c == cc)
            there = jnp.logical_not(here)
            far = remote(
                gup.at[kk], rg_rcv.at[w], rg_s.at[kk], rg_r.at[w], (node - w + ww, 2 * h + cc)
            )
            near = pltpu.make_async_copy(gup.at[kk], rg_rcv.at[w], rg_r.at[w])
            pl.when(there)(far.start)
            pl.when(here)(near.start)
            pending.append(lambda there=there, far=far: pl.when(there)(far.wait_send))

    def reduce_w(n):
        first, many = SETS[n]
        each(lambda d: landed(rw_rcv.at[d - 1, pl.ds(first, many)], rw_r.at[n, d - 1]))
        for slot in range(first, first + many):
            total = gst[w, slot].astype(F32)
            for d in range(1, Q):
                total = total + rw_rcv[d - 1, slot].astype(F32)
            piece = 8 * n + 3 * (slot - first)
            zsrc[piece:piece + 3] = total.astype(BF).reshape(3, 16, HS)
        if n == 0:
            for ww in range(Q):
                landed(rg_rcv.at[ww], rg_r.at[ww])
            total = rg_rcv[0].astype(F32)
            for ww in range(1, Q):
                total = total + rg_rcv[ww].astype(F32)
            zsrc[3:6] = total.astype(BF).reshape(3, 16, HS)

    def scatter_z(n):
        reduce_w(n)
        zsrc[8 * n + 6:8 * n + 8] = jnp.zeros((2, 16, HS), BF)

        def copy_of(d):
            zz, where = z_peer(d)
            return remote(zsrc.at[8 * n + zz], z_rcv.at[n, d - 1], z_s.at[n, d - 1], z_r.at[n, d - 1], where)

        send_each(copy_of)

    def gather_z(n):
        k = 8 * n + z
        each(lambda d: landed(z_rcv.at[n, d - 1], z_r.at[n, d - 1]))
        total = zsrc[k].astype(F32)
        for d in range(1, Q):
            total = total + z_rcv[n, d - 1].astype(F32)
        zfull[k] = total.astype(BF)

        def copy_of(d):
            return remote(zfull.at[k], zfull.at[k], az_s.at[n, d - 1], az_r.at[n, d - 1], z_peer(d)[1])

        send_each(copy_of)

    def gather_w(n):
        pieces = pl.ds(8 * n, WIDTHS[n])
        if n < 2:
            each(lambda d: landed(zfull.at[8 * n + (z ^ d)], az_r.at[n, d - 1]))
        cc, place = w // 4, c * 4 + w % 4

        def copy_of(d):
            return remote(
                zfull.at[pieces], gath.at[place, pieces], aw_s.at[n, d], aw_r.at[n, place],
                (node ^ d, 2 * h + cc),
            )

        send_each(copy_of)
        far = copy_of(0)
        near = pltpu.make_async_copy(zfull.at[pieces], gath.at[place, pieces], aw_r.at[n, place])
        pl.when(c != cc)(far.start)
        pl.when(c == cc)(near.start)
        pending.append(lambda: pl.when(c != cc)(far.wait_send))

    last = pl.ds(16, 3)

    def exchange_z():
        reduce_w(2)

        def copy_of(d):
            return remote(zsrc.at[last], zc_rcv.at[z], z_s.at[2, d - 1], z_r.at[2, d - 1], z_peer(d)[1])

        send_each(copy_of)
        zc_rcv[z] = zsrc[16:19]

    def sum_z():
        from_z(zc_rcv, z_r.at[2])
        total = zc_rcv[0].astype(F32)
        for zz in range(1, Q):
            total = total + zc_rcv[zz].astype(F32)
        zfull[16:19] = total.astype(BF)

    lower(0)
    scatter(0)

    from_z(ez_rcv, ez_r)
    collected = ez_rcv[...].reshape(TGT, 2 * CP).astype(F32).T.astype(BF)
    gup[...] = dot(collected, fz_src[...].reshape(TGT, HS)).astype(BF).reshape(Q, PIECE, HS)
    scatter_upper()

    landed(ag.at[3], ag_r.at[0])
    landed(ag.at[1], ag_r.at[1])
    grads = dot(xt[...].reshape(4 * FSL, TGT), jnp.concatenate([ag[3], ag[1]], axis=1)).astype(BF)
    gst[:, slots[3]] = grads[:, 0:HS].reshape(Q, PIECE, HS)
    gst[:, slots[1]] = grads[:, HS:2 * HS].reshape(Q, PIECE, HS)
    scatter(1)

    from_z(fz_rcv, fz_r)
    fw_src[...] = dot(perm[...], fz_rcv[...].reshape(TGT, HS)).astype(BF).reshape(Q, 32, HS)
    to_w(fw_src, fw_rcv, fw_s, fw_r)

    scatter_z(0)
    landed(ag.at[2], ag_r.at[2])
    lower(2)
    scatter(2)
    scatter_z(1)

    from_w(fw_rcv, fw_r)
    received = fw_rcv[...].reshape(TGT, HS).astype(F32).T.astype(BF)
    h_self = dot(received, seedtally[0]).astype(BF)
    agg_two = (dot(received, seedtally[1]) / K2).astype(BF)
    part = dot(w2c[0:CP], h_self) + dot(w2c[CP:2 * CP], agg_two)
    lst[...] = part[0:LP * 32].astype(BF).reshape(LP, 32, TGT)

    def logit_part(d):
        ff, where = f_peer(d)
        return remote(lst.at[lax.rem(ff, LP)], l_rcv.at[d - 1], l_s.at[d - 1], l_r.at[d - 1], where)

    send_each(logit_part, lambda d: f_peer(d)[0] < LP)

    gather_z(0)
    exchange_z()
    gather_z(1)

    fl = lax.rem(f, LP)

    @pl.when(f < LP)
    def _():
        each(lambda d: landed(l_rcv.at[d - 1], l_r.at[d - 1]))
        total = lst[fl].astype(F32)
        for d in range(1, Q):
            total = total + l_rcv[d - 1].astype(F32)
        ltot[...] = total.astype(BF)
        pltpu.make_async_copy(ltot, lout.at[fl], out_sem.at[3]).start()

    def logit_sum(d):
        return remote(ltot, lout.at[fl], la_s.at[d - 1], la_r.at[d - 1], f_peer(d)[1])

    send_each(logit_sum, lambda d: f < LP)

    gather_w(0)
    gather_w(1)
    sum_z()
    gather_w(2)
    sent()

    def logits_in(d):
        ff = f ^ d
        pl.when(ff < LP)(lambda: landed(lout.at[lax.rem(ff, LP)], la_r.at[d - 1]))

    each(logits_in)

    @pl.when(f < LP)
    def _():
        landed(lout.at[fl], out_sem.at[3])

    for n in range(3):
        for place in range(Q):
            landed(gath.at[place, pl.ds(8 * n, WIDTHS[n])], aw_r.at[n, place])


def finish_kernel(gath, lout, logits, g1s, g1n, g2s, g2n):
    h = lax.axis_index("feat") // 2
    logits[...] = lout[...].reshape(LP * 32, TGT)[0:C].astype(F32)
    for place in range(Q):
        cc, k = place // 4, place % 4
        mine = gath[place].reshape(19 * 16, HS).astype(F32)
        out = g1s if k < 2 else g1n
        for first, dh in ((0, 0), (128, 1), (176, 3), (256, 2)):
            col = pl.ds(pl.multiple_of((2 * lax.rem(h + dh, 4) + cc) * HS, HS), HS)
            out[(k % 2) * PIECE:(k % 2 + 1) * PIECE, col] = mine[first:first + PIECE]
        kk = 2 * k + cc
        out = g2s if kk < 4 else g2n
        first = (kk % 4) * PIECE
        count = min(PIECE, C - first)
        out[first:first + count] = mine[PIECE:PIECE + count]


def local(
    features, target_ids, near_ids, seed_ids, seed_near, w1_self, w1_neigh, w2_self, w2_neigh, logit_grad
):
    vm = pltpu.VMEM
    dma = pltpu.SemaphoreType.DMA
    vspec = pl.BlockSpec(memory_space=pltpu.VMEM)
    hspec = pl.BlockSpec(memory_space=pltpu.HBM)
    blocks = vm((Q, 32, HS), BF)
    wide = vm((Q, 32, 2 * CP), BF)
    scratch = [
        vm((2, FSL, ND), BF), vm((K1, TGT), jnp.int32), vm((1, TGT), jnp.int32), vm((1, TGT), jnp.int32),
        vm((K2, TGT), jnp.int32), vm((2 * FSL, HID), BF), vm((C, HS), BF), vm((C, HS), BF), vm((C, TGT), BF),
        vm((3, K1 + 1, 8, TGT), jnp.int32), vm((ND, TGT), BF), vm((ND, TGT), BF), vm((2, TGT, 2 * FSL), BF),
        vm((2, 2 * FSL, TGT), BF), vm((2, TGT, TGT), BF), vm((CP, TGT), BF), vm((2 * CP, HS), BF),
        vm((TGT, TGT), BF),
        vm((4, 2 * FSL, HS), BF), vm((4, TGT, HS), F32), vm((3, TGT, HS), BF),
        vm((3, TGT, HS), BF),
        blocks, blocks, blocks, blocks, wide, wide, wide, wide,
        blocks, blocks, blocks, blocks,
        vm((4, TGT, HS), BF), vm((Q, 4, PIECE, HS), BF), vm((Q, PIECE, HS), BF),
        vm((Q - 1, 4, PIECE, HS), BF), vm((Q, PIECE, HS), BF),
        vm((19, 16, HS), BF), vm((2, Q - 1, 16, HS), BF), vm((Q, 3, 16, HS), BF), vm((19, 16, HS), BF),
        vm((LP, 32, TGT), BF), vm((Q - 1, 32, TGT), BF), vm((32, TGT), BF),
        dma((10,)), dma((4,)), dma((1,)), dma((1,)), dma((4,)), dma((4,)), dma((6,)), dma((6,)),
        dma((7,)), dma((7,)), dma((7,)), dma((7,)), dma((7,)), dma((7,)), dma((7,)), dma((7,)),
        dma((7,)), dma((7,)), dma((7,)), dma((7,)), dma((6,)), dma((6,)),
        dma((3, 7)), dma((3, 7)), dma((8,)), dma((8,)), dma((3, 7)), dma((3, 7)), dma((3, 7)), dma((3, 7)),
        dma((3, 8)), dma((3, 8)), dma((7,)), dma((7,)), dma((7,)), dma((7,)),
    ]
    gath, lout = pl.pallas_call(
        main_kernel,
        out_shape=(
            jax.ShapeDtypeStruct((Q, 19, 16, HS), BF),
            jax.ShapeDtypeStruct((LP, 32, TGT), BF),
        ),
        in_specs=[hspec] * 10,
        out_specs=(hspec, hspec),
        scratch_shapes=scratch,
        compiler_params=pltpu.CompilerParams(
            collective_id=0, has_side_effects=True, vmem_limit_bytes=62 * 1024 * 1024
        ),
        name="sage_step",
    )(
        features.T, near_ids.T, target_ids.reshape(1, TGT), seed_ids.reshape(1, TGT), seed_near.T,
        w1_self, w1_neigh, w2_self.T, w2_neigh.T, logit_grad.T,
    )
    logits, g1s, g1n, g2s, g2n = pl.pallas_call(
        finish_kernel,
        out_shape=(
            jax.ShapeDtypeStruct((C, TGT), F32),
            jax.ShapeDtypeStruct((FSL, HID), F32),
            jax.ShapeDtypeStruct((FSL, HID), F32),
            jax.ShapeDtypeStruct((C, HS), F32),
            jax.ShapeDtypeStruct((C, HS), F32),
        ),
        in_specs=[vspec, vspec],
        out_specs=(vspec,) * 5,
        compiler_params=pltpu.CompilerParams(vmem_limit_bytes=62 * 1024 * 1024),
        name="finish",
    )(gath, lout)
    return logits.T, g1s, g1n, g2s.T, g2n.T


def solution(mesh):
    return jax.shard_map(
        local,
        mesh=mesh,
        in_specs=(
            P("nodes", "feat"),
            P("nodes"),
            P("nodes", None),
            P("nodes"),
            P("nodes", None),
            P("feat", None),
            P("feat", None),
            P("feat", None),
            P("feat", None),
            P("nodes", None),
        ),
        out_specs=(
            P("nodes", None),
            P("feat", None),
            P("feat", None),
            P("feat", None),
            P("feat", None),
        ),
        check_vma=False,
    )
```

```python
import jax
import jax.numpy as jnp
from jax import lax
from jax.experimental import pallas as pl
from jax.experimental.pallas import tpu as pltpu
from jax.sharding import PartitionSpec as P

BF = jnp.bfloat16
F32 = jnp.float32
MESH = pl.DeviceIdType.MESH

TGT = 256
ND = 1024
FSL = 96
HID = 1024
HS = 128
C = 153
K1 = 25
K2 = 15
CP = 192
LP = 5
Q = 8
PIECE = 48
SETS = ((0, 1), (1, 2), (3, 1))
WIDTHS = (6, 6, 3)


def dot(a, b):
    return jnp.dot(a, b, preferred_element_type=F32)


def dot_dims(a, b, ca, cb):
    return lax.dot_general(a, b, (((ca,), (cb,)), ((), ())), preferred_element_type=F32)


def main_kernel(
    features_hbm, near_hbm, tid_hbm, sid_hbm, snear_hbm,
    w1s_hbm, w1n_hbm, w2s_hbm, w2n_hbm, lg_hbm,
    gath, lout,
    feat_v, near_v, tid_v, sid_v, snear_v, w1_v, w2s_v, w2n_v, lg_v,
    keys, tally, sel, x_v, xt, seedtally, lgp, w2c, perm,
    w1_p, p_own, rs_src, relay_rcv, rs_rcv,
    bw_src, bw_rcv, bz_src, bz_rcv, ew_src, ew_rcv, ez_src, ez_rcv,
    fw_src, fw_rcv, fz_src, fz_rcv,
    ag, gst, gup, rw_rcv, rg_rcv, zsrc, z_rcv, zc_rcv, zfull, lst, l_rcv, ltot,
    in_sem, out_sem, fx_s, fx_r, wx_s, wx_r, rs_s, rs_r, bw_s, bw_r, bz_s, bz_r,
    ew_s, ew_r, ez_s, ez_r, fw_s, fw_r, fz_s, fz_r, ag_s, ag_r,
    rw_s, rw_r, rg_s, rg_r, z_s, z_r, az_s, az_r, aw_s, aw_r, l_s, l_r, la_s, la_r,
):
    node = lax.axis_index("nodes")
    f = lax.axis_index("feat")
    z = node // Q
    w = node % Q
    h = f // 2
    c = f % 2

    def z_peer(d):
        return z ^ d, (node ^ (d * Q), f)

    def w_peer(d):
        return w ^ d, (node ^ d, f)

    def v_peer(d):
        return w ^ d, (node ^ d, f ^ 1)

    def f_peer(d):
        return f ^ d, (node, f ^ d)

    partner = (node, h * 2 + (1 - c))

    up = (node, lax.rem(h + 1, 4) * 2 + c)
    down = (node, lax.rem(h + 3, 4) * 2 + c)

    def each(body):
        for d in range(1, Q):
            body(d)

    loads = [
        pltpu.make_async_copy(src, dst, in_sem.at[n])
        for n, (src, dst) in enumerate(
            (
                (snear_hbm, snear_v),
                (sid_hbm, sid_v),
                (lg_hbm, lg_v),
                (w2s_hbm, w2s_v),
                (w2n_hbm, w2n_v),
                (near_hbm, near_v),
                (tid_hbm, tid_v),
                (features_hbm, feat_v.at[c]),
                (w1s_hbm, w1_v.at[pl.ds(0, FSL)]),
                (w1n_hbm, w1_v.at[pl.ds(FSL, FSL)]),
            )
        )
    ]
    for load in loads:
        load.start()

    barrier = pltpu.get_barrier_semaphore()

    def greet(d):
        for where in (z_peer(d)[1], w_peer(d)[1], f_peer(d)[1], v_peer(d)[1]):
            pl.semaphore_signal(barrier, inc=1, device_id=where, device_id_type=MESH)

    each(greet)

    pending = []

    def remote(src, dst, s_sem, r_sem, where):
        return pltpu.make_async_remote_copy(
            src_ref=src, dst_ref=dst, send_sem=s_sem, recv_sem=r_sem,
            device_id=where, device_id_type=MESH,
        )

    def send(*args):
        copy = remote(*args)
        copy.start()
        pending.append(copy.wait_send)

    def send_each(copy_of, test_of=None):
        def start(d):
            if test_of is None:
                copy_of(d).start()
            else:
                pl.when(test_of(d))(lambda: copy_of(d).start())

        def finish(d):
            if test_of is None:
                copy_of(d).wait_send()
            else:
                pl.when(test_of(d))(lambda: copy_of(d).wait_send())

        each(start)
        pending.append(lambda: each(finish))

    def sent():
        for finish in pending:
            finish()
        pending.clear()

    def landed(ref, r_sem):
        pltpu.make_async_copy(ref, ref, r_sem).wait()

    row = lax.broadcasted_iota(jnp.int32, (8, 128), 0)

    def count(ids, own, low, words, totals_of, ones_of):
        fan = ids.shape[0]
        high = lax.shift_right_logical(ids, low.bit_length() - 1)
        digit = lax.shift_left(jnp.ones_like(ids), (high & 3) * 8)
        tables = [ids & (low - 1)]
        tables += [jnp.where((high >> 2) == g, digit, 0) for g in range(words)]
        for n, table in enumerate(tables):
            for k in range(fan):
                keys[n, k] = jnp.broadcast_to(table[k:k + 1], (8, TGT))
        keys[0, K1] = jnp.broadcast_to(own, (8, TGT))

        def body(step, carry):
            mine = [step * 32 + j * 8 + row for j in range(4)]
            for half in range(2):
                cols = slice(half * 128, half * 128 + 128)
                totals = [[jnp.zeros((8, 128), jnp.int32)] * 4 for _ in range(words)]
                for k in range(fan):
                    theirs = keys[0, k, :, cols]
                    hits = [theirs == m for m in mine]
                    for g in range(words):
                        word = keys[1 + g, k, :, cols]
                        totals[g] = [t + jnp.where(hit, word, 0) for t, hit in zip(totals[g], hits)]
                theirs = keys[0, K1, :, cols]
                for part in range(4 * words):
                    for j in (0, 2):
                        first = part * low + step * 32 + j * 8
                        rows = pl.ds(pl.multiple_of(first, 16), 16)
                        both = [
                            lax.shift_right_logical(totals[part // 4][n], 8 * (part % 4)) & 255
                            for n in (j, j + 1)
                        ]
                        totals_of[rows, cols] = jnp.concatenate(both, axis=0).astype(F32).astype(BF)
                        both = [
                            jnp.where(theirs == mine[n] + part * low, 1.0, 0.0) for n in (j, j + 1)
                        ]
                        ones_of[rows, cols] = jnp.concatenate(both, axis=0).astype(BF)
            return carry

        lax.fori_loop(0, low // 32, body, 0)

    pl.semaphore_wait(barrier, 4 * (Q - 1))
    send(features_hbm, feat_v.at[c], fx_s.at[0], fx_r.at[0], partner)

    def cols_of(dh, cc):
        return pl.ds(pl.multiple_of((lax.rem(h + dh, 4) * 2 + cc) * HS, HS), HS)

    def swap(n):
        return ((n >> 2) & 7) * 32 + (n >> 5) * 4 + (n & 3)

    for n in range(5):
        loads[n].wait()
    for padded, first, given in ((lgp, 0, lg_v), (w2c, 0, w2s_v), (w2c, CP, w2n_v)):
        padded[first:first + CP] = jnp.zeros((CP, padded.shape[1]), BF)
        padded[first:first + C] = given[...]
    count(swap(snear_v[...]), swap(sid_v[...]), 64, 1, seedtally.at[1], seedtally.at[0])
    back = jnp.concatenate(
        [dot_dims(seedtally[0], lgp[...], 1, 1), dot_dims(seedtally[1], lgp[...], 1, 1) / K2], axis=1
    ).astype(BF)
    bw_src[...] = dot(back, w2c[...]).astype(BF).reshape(Q, 32, HS)
    ew_src[...] = back.reshape(Q, 32, 2 * CP)

    def to_w(src, dst, s_sem, r_sem):
        def copy_of(d):
            ww, where = w_peer(d)
            return remote(src.at[ww], dst.at[w], s_sem.at[d - 1], r_sem.at[d - 1], where)

        send_each(copy_of)
        dst[w] = src[w]

    def to_z(src, dst, s_sem, r_sem):
        def copy_of(d):
            zz, where = z_peer(d)
            return remote(src.at[zz], dst.at[z], s_sem.at[d - 1], r_sem.at[d - 1], where)

        send_each(copy_of)
        dst[z] = src[z]

    def from_w(dst, r_sem):
        each(lambda d: landed(dst.at[w ^ d], r_sem.at[d - 1]))

    def from_z(dst, r_sem):
        each(lambda d: landed(dst.at[z ^ d], r_sem.at[d - 1]))

    to_w(bw_src, bw_rcv, bw_s, bw_r)
    loads[8].wait()
    loads[9].wait()
    for place, dh in enumerate((2, 1, 3, 0)):
        send(w1_v.at[:, cols_of(dh, 1 - c)], w1_p.at[place], wx_s.at[place], wx_r.at[place], partner)
    to_w(ew_src, ew_rcv, ew_s, ew_r)

    loads[5].wait()
    loads[6].wait()
    count(near_v[...], tid_v[...], 128, 2, tally, sel)

    loads[7].wait()
    landed(feat_v.at[1 - c], fx_r.at[0])
    both = feat_v[...].reshape(2 * FSL, ND)
    x_self = dot(both, sel[...]).astype(BF)
    agg = (dot(both, tally[...]) / K1).astype(BF)
    for cc in range(2):
        part = slice(cc * FSL, cc * FSL + FSL)
        mine = jnp.concatenate([x_self[part], agg[part]], axis=0)
        xt[cc] = mine
        x_v[cc] = mine.astype(F32).T.astype(BF)

    for place, dh in enumerate((2, 1, 3, 0)):
        landed(w1_p.at[place], wx_r.at[place])
        p_own[place] = dot(x_v[c], w1_v[:, cols_of(dh, c)]) + dot(x_v[1 - c], w1_p[place])

    lo, hi = pl.ds(0, 128), pl.ds(128, 128)
    rs_src[0] = p_own[0].astype(BF)
    send(rs_src.at[0, lo], relay_rcv.at[0], rs_s.at[0], rs_r.at[0], up)
    send(rs_src.at[0, hi], relay_rcv.at[1], rs_s.at[1], rs_r.at[1], down)
    rs_src[1, 128:256] = p_own[1, 128:256].astype(BF)
    send(rs_src.at[1, hi], rs_rcv.at[0, hi], rs_s.at[2], rs_r.at[2], up)
    rs_src[2, 0:128] = p_own[2, 0:128].astype(BF)
    send(rs_src.at[2, lo], rs_rcv.at[1, lo], rs_s.at[3], rs_r.at[3], down)

    a = lax.broadcasted_iota(jnp.int32, (TGT, TGT), 0)
    b = lax.broadcasted_iota(jnp.int32, (TGT, TGT), 1)
    perm[...] = jnp.where(swap(a) == b, 1.0, 0.0).astype(BF)
    from_w(bw_rcv, bw_r)
    bz_src[...] = dot(perm[...], bw_rcv[...].reshape(TGT, HS)).astype(BF).reshape(Q, 32, HS)
    to_z(bz_src, bz_rcv, bz_s, bz_r)
    from_w(ew_rcv, ew_r)
    turned = dot(perm[...], ew_rcv[...].reshape(TGT, 2 * CP)).astype(BF)
    ez_src[...] = turned.reshape(Q, 32, 2 * CP)
    to_z(ez_src, ez_rcv, ez_s, ez_r)

    landed(relay_rcv.at[0], rs_r.at[0])
    rs_src[1, 0:128] = (p_own[1, 0:128] + relay_rcv[0].astype(F32)).astype(BF)
    send(rs_src.at[1, lo], rs_rcv.at[0, lo], rs_s.at[4], rs_r.at[4], up)
    landed(relay_rcv.at[1], rs_r.at[1])
    rs_src[2, 128:256] = (p_own[2, 128:256] + relay_rcv[1].astype(F32)).astype(BF)
    send(rs_src.at[2, hi], rs_rcv.at[1, hi], rs_s.at[5], rs_r.at[5], down)
    from_z(bz_rcv, bz_r)

    pre = p_own[3]
    landed(rs_rcv.at[0, hi], rs_r.at[2])
    landed(rs_rcv.at[1, lo], rs_r.at[3])
    landed(rs_rcv.at[0, lo], rs_r.at[4])
    landed(rs_rcv.at[1, hi], rs_r.at[5])
    pre = pre + rs_rcv[0].astype(F32) + rs_rcv[1].astype(F32)
    sigma = 1.0 / (1.0 + jnp.exp(-pre))
    d_hidden = bz_rcv[...].reshape(TGT, HS).astype(F32)
    ag[0] = (d_hidden * (sigma * (1.0 + pre * (1.0 - sigma)))).astype(BF)
    send(ag.at[0, lo], ag.at[3, lo], ag_s.at[0], ag_r.at[0], up)
    send(ag.at[0, hi], ag.at[1, hi], ag_s.at[1], ag_r.at[1], down)
    send(ag.at[0, hi], ag.at[3, hi], ag_s.at[2], ag_r.at[2], up)
    send(ag.at[0, lo], ag.at[1, lo], ag_s.at[3], ag_r.at[3], down)
    fz_src[...] = (pre * sigma).astype(BF).reshape(Q, 32, HS)
    to_z(fz_src, fz_rcv, fz_s, fz_r)

    slots = {0: 0, 1: 1, 3: 2, 2: 3}

    def lower(dh):
        grad = dot(xt[...].reshape(4 * FSL, TGT), ag[dh])
        gst[:, slots[dh]] = grad.astype(BF).reshape(Q, PIECE, HS)

    def scatter(n):
        span = pl.ds(*SETS[n])

        def copy_of(d):
            ww, where = w_peer(d)
            return remote(
                gst.at[ww, span], rw_rcv.at[d - 1, span], rw_s.at[n, d - 1], rw_r.at[n, d - 1], where
            )

        send_each(copy_of)

    def scatter_upper():
        for kk in range(Q):
            ww, cc = 4 * c + kk // 2, kk % 2
            here = jnp.logical_and(w == ww, c == cc)
            there = jnp.logical_not(here)
            far = remote(
                gup.at[kk], rg_rcv.at[w], rg_s.at[kk], rg_r.at[w], (node - w + ww, 2 * h + cc)
            )
            near = pltpu.make_async_copy(gup.at[kk], rg_rcv.at[w], rg_r.at[w])
            pl.when(there)(far.start)
            pl.when(here)(near.start)
            pending.append(lambda there=there, far=far: pl.when(there)(far.wait_send))

    def reduce_w(n):
        first, many = SETS[n]
        each(lambda d: landed(rw_rcv.at[d - 1, pl.ds(first, many)], rw_r.at[n, d - 1]))
        for slot in range(first, first + many):
            total = gst[w, slot].astype(F32)
            for d in range(1, Q):
                total = total + rw_rcv[d - 1, slot].astype(F32)
            piece = 8 * n + 3 * (slot - first)
            zsrc[piece:piece + 3] = total.astype(BF).reshape(3, 16, HS)
        if n == 0:
            for ww in range(Q):
                landed(rg_rcv.at[ww], rg_r.at[ww])
            total = rg_rcv[0].astype(F32)
            for ww in range(1, Q):
                total = total + rg_rcv[ww].astype(F32)
            zsrc[3:6] = total.astype(BF).reshape(3, 16, HS)

    def scatter_z(n):
        reduce_w(n)
        zsrc[8 * n + 6:8 * n + 8] = jnp.zeros((2, 16, HS), BF)

        def copy_of(d):
            zz, where = z_peer(d)
            return remote(zsrc.at[8 * n + zz], z_rcv.at[n, d - 1], z_s.at[n, d - 1], z_r.at[n, d - 1], where)

        send_each(copy_of)

    def gather_z(n):
        k = 8 * n + z
        each(lambda d: landed(z_rcv.at[n, d - 1], z_r.at[n, d - 1]))
        total = zsrc[k].astype(F32)
        for d in range(1, Q):
            total = total + z_rcv[n, d - 1].astype(F32)
        zfull[k] = total.astype(BF)

        def copy_of(d):
            return remote(zfull.at[k], zfull.at[k], az_s.at[n, d - 1], az_r.at[n, d - 1], z_peer(d)[1])

        send_each(copy_of)

    def gather_w(n):
        pieces = pl.ds(8 * n, WIDTHS[n])
        if n < 2:
            each(lambda d: landed(zfull.at[8 * n + (z ^ d)], az_r.at[n, d - 1]))
        cc, place = w // 4, c * 4 + w % 4

        def copy_of(d):
            return remote(
                zfull.at[pieces], gath.at[place, pieces], aw_s.at[n, d], aw_r.at[n, place],
                (node ^ d, 2 * h + cc),
            )

        send_each(copy_of)
        far = copy_of(0)
        near = pltpu.make_async_copy(zfull.at[pieces], gath.at[place, pieces], aw_r.at[n, place])
        pl.when(c != cc)(far.start)
        pl.when(c == cc)(near.start)
        pending.append(lambda: pl.when(c != cc)(far.wait_send))

    last = pl.ds(16, 3)

    def exchange_z():
        reduce_w(2)

        def copy_of(d):
            return remote(zsrc.at[last], zc_rcv.at[z], z_s.at[2, d - 1], z_r.at[2, d - 1], z_peer(d)[1])

        send_each(copy_of)
        zc_rcv[z] = zsrc[16:19]

    def sum_z():
        from_z(zc_rcv, z_r.at[2])
        total = zc_rcv[0].astype(F32)
        for zz in range(1, Q):
            total = total + zc_rcv[zz].astype(F32)
        zfull[16:19] = total.astype(BF)

    lower(0)
    scatter(0)

    landed(ag.at[3, lo], ag_r.at[0])
    send(ag.at[3, lo], ag.at[2, lo], ag_s.at[4], ag_r.at[4], up)
    landed(ag.at[1, hi], ag_r.at[1])
    send(ag.at[1, hi], ag.at[2, hi], ag_s.at[5], ag_r.at[5], down)

    from_z(ez_rcv, ez_r)
    collected = ez_rcv[...].reshape(TGT, 2 * CP).astype(F32).T.astype(BF)
    gup[...] = dot(collected, fz_src[...].reshape(TGT, HS)).astype(BF).reshape(Q, PIECE, HS)
    scatter_upper()

    landed(ag.at[3, hi], ag_r.at[2])
    lower(3)
    landed(ag.at[1, lo], ag_r.at[3])
    lower(1)
    scatter(1)

    from_z(fz_rcv, fz_r)
    fw_src[...] = dot(perm[...], fz_rcv[...].reshape(TGT, HS)).astype(BF).reshape(Q, 32, HS)
    to_w(fw_src, fw_rcv, fw_s, fw_r)

    scatter_z(0)
    landed(ag.at[2, lo], ag_r.at[4])
    landed(ag.at[2, hi], ag_r.at[5])
    lower(2)
    scatter(2)
    scatter_z(1)

    from_w(fw_rcv, fw_r)
    received = fw_rcv[...].reshape(TGT, HS).astype(F32).T.astype(BF)
    h_self = dot(received, seedtally[0]).astype(BF)
    agg_two = (dot(received, seedtally[1]) / K2).astype(BF)
    part = dot(w2c[0:CP], h_self) + dot(w2c[CP:2 * CP], agg_two)
    lst[...] = part[0:LP * 32].astype(BF).reshape(LP, 32, TGT)

    def logit_part(d):
        ff, where = f_peer(d)
        return remote(lst.at[lax.rem(ff, LP)], l_rcv.at[d - 1], l_s.at[d - 1], l_r.at[d - 1], where)

    send_each(logit_part, lambda d: f_peer(d)[0] < LP)

    gather_z(0)
    exchange_z()
    gather_z(1)

    fl = lax.rem(f, LP)

    @pl.when(f < LP)
    def _():
        each(lambda d: landed(l_rcv.at[d - 1], l_r.at[d - 1]))
        total = lst[fl].astype(F32)
        for d in range(1, Q):
            total = total + l_rcv[d - 1].astype(F32)
        ltot[...] = total.astype(BF)
        pltpu.make_async_copy(ltot, lout.at[fl], out_sem.at[3]).start()

    def logit_sum(d):
        return remote(ltot, lout.at[fl], la_s.at[d - 1], la_r.at[d - 1], f_peer(d)[1])

    send_each(logit_sum, lambda d: f < LP)

    gather_w(0)
    gather_w(1)
    sum_z()
    gather_w(2)
    sent()

    def logits_in(d):
        ff = f ^ d
        pl.when(ff < LP)(lambda: landed(lout.at[lax.rem(ff, LP)], la_r.at[d - 1]))

    each(logits_in)

    @pl.when(f < LP)
    def _():
        landed(lout.at[fl], out_sem.at[3])

    for n in range(3):
        for place in range(Q):
            landed(gath.at[place, pl.ds(8 * n, WIDTHS[n])], aw_r.at[n, place])


def finish_kernel(gath, lout, logits, g1s, g1n, g2s, g2n):
    h = lax.axis_index("feat") // 2
    logits[...] = lout[...].reshape(LP * 32, TGT)[0:C].astype(F32)
    for place in range(Q):
        cc, k = place // 4, place % 4
        mine = gath[place].reshape(19 * 16, HS).astype(F32)
        out = g1s if k < 2 else g1n
        for first, dh in ((0, 0), (128, 1), (176, 3), (256, 2)):
            col = pl.ds(pl.multiple_of((2 * lax.rem(h + dh, 4) + cc) * HS, HS), HS)
            out[(k % 2) * PIECE:(k % 2 + 1) * PIECE, col] = mine[first:first + PIECE]
        kk = 2 * k + cc
        out = g2s if kk < 4 else g2n
        first = (kk % 4) * PIECE
        count = min(PIECE, C - first)
        out[first:first + count] = mine[PIECE:PIECE + count]


def local(
    features, target_ids, near_ids, seed_ids, seed_near, w1_self, w1_neigh, w2_self, w2_neigh, logit_grad
):
    vm = pltpu.VMEM
    dma = pltpu.SemaphoreType.DMA
    vspec = pl.BlockSpec(memory_space=pltpu.VMEM)
    hspec = pl.BlockSpec(memory_space=pltpu.HBM)
    blocks = vm((Q, 32, HS), BF)
    wide = vm((Q, 32, 2 * CP), BF)
    scratch = [
        vm((2, FSL, ND), BF), vm((K1, TGT), jnp.int32), vm((1, TGT), jnp.int32), vm((1, TGT), jnp.int32),
        vm((K2, TGT), jnp.int32), vm((2 * FSL, HID), BF), vm((C, HS), BF), vm((C, HS), BF), vm((C, TGT), BF),
        vm((3, K1 + 1, 8, TGT), jnp.int32), vm((ND, TGT), BF), vm((ND, TGT), BF), vm((2, TGT, 2 * FSL), BF),
        vm((2, 2 * FSL, TGT), BF), vm((2, TGT, TGT), BF), vm((CP, TGT), BF), vm((2 * CP, HS), BF),
        vm((TGT, TGT), BF),
        vm((4, 2 * FSL, HS), BF), vm((4, TGT, HS), F32), vm((3, TGT, HS), BF),
        vm((2, 128, HS), BF), vm((2, TGT, HS), BF),
        blocks, blocks, blocks, blocks, wide, wide, wide, wide,
        blocks, blocks, blocks, blocks,
        vm((4, TGT, HS), BF), vm((Q, 4, PIECE, HS), BF), vm((Q, PIECE, HS), BF),
        vm((Q - 1, 4, PIECE, HS), BF), vm((Q, PIECE, HS), BF),
        vm((19, 16, HS), BF), vm((2, Q - 1, 16, HS), BF), vm((Q, 3, 16, HS), BF), vm((19, 16, HS), BF),
        vm((LP, 32, TGT), BF), vm((Q - 1, 32, TGT), BF), vm((32, TGT), BF),
        dma((10,)), dma((4,)), dma((1,)), dma((1,)), dma((4,)), dma((4,)), dma((6,)), dma((6,)),
        dma((7,)), dma((7,)), dma((7,)), dma((7,)), dma((7,)), dma((7,)), dma((7,)), dma((7,)),
        dma((7,)), dma((7,)), dma((7,)), dma((7,)), dma((6,)), dma((6,)),
        dma((3, 7)), dma((3, 7)), dma((8,)), dma((8,)), dma((3, 7)), dma((3, 7)), dma((3, 7)), dma((3, 7)),
        dma((3, 8)), dma((3, 8)), dma((7,)), dma((7,)), dma((7,)), dma((7,)),
    ]
    gath, lout = pl.pallas_call(
        main_kernel,
        out_shape=(
            jax.ShapeDtypeStruct((Q, 19, 16, HS), BF),
            jax.ShapeDtypeStruct((LP, 32, TGT), BF),
        ),
        in_specs=[hspec] * 10,
        out_specs=(hspec, hspec),
        scratch_shapes=scratch,
        compiler_params=pltpu.CompilerParams(
            collective_id=0, has_side_effects=True, vmem_limit_bytes=62 * 1024 * 1024
        ),
        name="sage_step",
    )(
        features.T, near_ids.T, target_ids.reshape(1, TGT), seed_ids.reshape(1, TGT), seed_near.T,
        w1_self, w1_neigh, w2_self.T, w2_neigh.T, logit_grad.T,
    )
    logits, g1s, g1n, g2s, g2n = pl.pallas_call(
        finish_kernel,
        out_shape=(
            jax.ShapeDtypeStruct((C, TGT), F32),
            jax.ShapeDtypeStruct((FSL, HID), F32),
            jax.ShapeDtypeStruct((FSL, HID), F32),
            jax.ShapeDtypeStruct((C, HS), F32),
            jax.ShapeDtypeStruct((C, HS), F32),
        ),
        in_specs=[vspec, vspec],
        out_specs=(vspec,) * 5,
        compiler_params=pltpu.CompilerParams(vmem_limit_bytes=62 * 1024 * 1024),
        name="finish",
    )(gath, lout)
    return logits.T, g1s, g1n, g2s.T, g2n.T


def solution(mesh):
    return jax.shard_map(
        local,
        mesh=mesh,
        in_specs=(
            P("nodes", "feat"),
            P("nodes"),
            P("nodes", None),
            P("nodes"),
            P("nodes", None),
            P("feat", None),
            P("feat", None),
            P("feat", None),
            P("feat", None),
            P("nodes", None),
        ),
        out_specs=(
            P("nodes", None),
            P("feat", None),
            P("feat", None),
            P("feat", None),
            P("feat", None),
        ),
        check_vma=False,
    )
```
